256 devices in a mesh: grp: 16 (over z_lo, x, core), dev: 16 (over z_hi, y).
Axes of the slice: x: 4, y: 4, z: 8 (z_hi: 4, z_lo: 2; z = z_hi * 2 + z_lo), core: 2. Of those that a mesh axis runs over, the one named last changes fastest.
Arguments:
- patches: bfloat16 [512, 256, 384], P('dev', 'grp'), may hold values from -6 to 6
- tissue: int32 [512, 256], replicated, may hold values from 0 to 1, as said below
- region_slide: int32 [512], replicated, may hold values from 0 to 3, never falling along the last dimension, each value on 1 to 256 neighbouring positions
- w_up: bfloat16 [384, 1536], replicated, may hold values from -0.3125 to 0.3125
- w_down: bfloat16 [1536, 384], replicated, may hold values from -0.15625 to 0.15625
- w_embed: bfloat16 [384, 192], replicated, may hold values from -0.3125 to 0.3125
- w_query: bfloat16 [192, 192], replicated, may hold values from -0.4375 to 0.4375
- w_key: bfloat16 [192, 192], replicated, may hold values from -0.4375 to 0.4375
- w_value: bfloat16 [192, 192], replicated, may hold values from -0.4375 to 0.4375
- w_out: bfloat16 [192, 192], replicated, may hold values from -0.4375 to 0.4375
- att_v: float32 [192, 192], replicated, may hold values from -0.4375 to 0.4375
- att_u: float32 [192, 192], replicated, may hold values from -0.4375 to 0.4375
- att_w: float32 [192], replicated, may hold values from -0.4 to 0.4
- w_class: float32 [192, 3], replicated, may hold values from -0.4375 to 0.4375
- g_logits: float32 [4, 3], replicated, may hold values from -6 to 6
Outputs:
- logits: float32 [4, 3], replicated
- g_up: float32 [384, 1536], replicated
- g_down: float32 [1536, 384], replicated
- g_embed: float32 [384, 192], replicated
- g_query: float32 [192, 192], replicated
- g_key: float32 [192, 192], replicated
- g_value: float32 [192, 192], replicated
- g_out: float32 [192, 192], replicated
- g_att_v: float32 [192, 192], replicated
- g_att_u: float32 [192, 192], replicated
- g_att_w: float32 [192], replicated
- g_class: float32 [192, 3], replicated
The draws below stay inside these ranges and needn't reach their ends.
Inputs may be any that keep to these rules, and one draw needn't show every extreme that they name: Each region has its own share of tissue patches, from none of its 256 patches to all of them. `region_slide`: slide numbers never fall along the regions, and every slide has a region.
All inputs are finite; a program needn't handle non-finite values.
Results may differ from the reference program's by a relative error of at most 0.019.
Values may be sent and summed in bfloat16 or wider, within the bound.
No kernel may reach another device: no remote copies, remote signals or barrier semaphores. Data moves between devices by JAX's collectives and lax.ppermute only.
A program may use at most 64 MiB of HBM per device.

```python
import math
import jax
import jax.numpy as jnp
import numpy as np
from jax import lax

D1 = 384
F1 = 1536
HEADS = 6
HEAD_DIM = 32
D2 = 192
PATCH = 256
REGIONS = 512
SLIDES = 4
CLASSES = 3


def draw_tissue(key, part):
    key = jax.random.fold_in(key, 11)
    level_key, cell_key = jax.random.split(key)
    tissue_level = jax.random.randint(level_key, (REGIONS, 1), 0, 9)
    patch_draws = jax.random.randint(cell_key, (REGIONS, PATCH), 0, 8)
    return (patch_draws < tissue_level).astype(jnp.int32)


def levels(rng, extent, pieces, smallest, top_value):
    def one(position, blocks):
        heights = jax.random.uniform(jax.random.fold_in(jax.random.fold_in(rng, 6), position), (blocks,), jnp.float32, smallest / len(pieces), top_value / len(pieces))
        return jnp.repeat(jnp.exp(heights), extent[position] // blocks).reshape((-1,) + (1,) * (len(extent) - position - 1))

    gain = one(*pieces[0])
    for cut in pieces[1:]:
        gain = gain * one(*cut)
    return gain


def split_up(number_of, total, bound, slope):
    portions = [(1 << 20) // math.isqrt(rank ** slope) + 1 for rank in range(2, number_of + 1)]
    rest, holding = total - bound - (number_of - 1), [1] * (number_of - 1)
    while rest > 0:
        candidates = [i for i in range(number_of - 1) if holding[i] < bound]
        mass, remaining = sum([portions[i] for i in candidates]), rest
        for i in candidates:
            more = min(bound - holding[i], max(1, remaining * portions[i] // mass), rest)
            holding[i] = holding[i] + more
            rest = rest - more
    return np.array([bound] + holding)


def ragged(key, amount, total, most, skew):
    if amount == 2:
        one = jax.random.randint(key, (), max(1, total - most), min(most, total - 1) + 1)
        return jnp.stack([one, total - one])
    tallies = jnp.asarray(split_up(amount, total, most, skew), jnp.int32)
    couples = (amount - 1) // 2
    source_of, sink = tallies[1:1 + 2 * couples:2], tallies[2:2 + 2 * couples:2]
    slack = jnp.minimum(source_of - 1, most - sink)
    moved = jax.random.randint(jax.random.fold_in(key, 1), (couples,), 0, 1 << 20) % (slack + 1)
    tallies = tallies.at[1:1 + 2 * couples:2].set(source_of - moved).at[2:2 + 2 * couples:2].set(sink + moved)
    return tallies[jax.random.permutation(jax.random.fold_in(key, 2), amount)]


def noise(key, extent, deviation, bound, cuts=(), kind=jnp.bfloat16):
    drawn = jax.random.normal(key, extent, jnp.float32) * deviation
    if len(cuts) > 0:
        drawn = levels(key, extent, cuts, -0.22, 0.18) * drawn
    return jnp.clip(drawn, min=-bound, max=bound).astype(kind)


def setup_inputs(seed: int = 0) -> dict:
    keys = jax.random.split(jax.random.key(seed), 16)
    return {
        "patches": noise(keys[0], (REGIONS, PATCH, D1), 1.0, 6.0, ((0, 16), (1, 16))),
        "tissue": draw_tissue(jax.random.fold_in(keys[15], 71), 0),
        "region_slide": jnp.searchsorted(jnp.cumsum(ragged(keys[2], SLIDES, REGIONS, REGIONS // 2, 2)), jnp.arange(REGIONS), side="right").astype(jnp.int32),
        "w_up": noise(keys[3], (D1, F1), D1 ** -0.5, 0.3125),
        "w_down": noise(keys[4], (F1, D1), F1 ** -0.5, 0.15625),
        "w_embed": noise(keys[5], (D1, D2), D1 ** -0.5, 0.3125),
        "w_query": noise(keys[6], (D2, D2), D2 ** -0.5, 0.4375),
        "w_key": noise(keys[7], (D2, D2), D2 ** -0.5, 0.4375),
        "w_value": noise(keys[8], (D2, D2), D2 ** -0.5, 0.4375),
        "w_out": noise(keys[9], (D2, D2), D2 ** -0.5, 0.4375),
        "att_v": noise(keys[10], (D2, D2), D2 ** -0.5, 0.4375, (), jnp.float32),
        "att_u": noise(keys[11], (D2, D2), D2 ** -0.5, 0.4375, (), jnp.float32),
        "att_w": jnp.clip(jax.random.uniform(keys[12], (D2,), jnp.float32, -0.4, 0.4), -0.4, 0.4),
        "w_class": noise(keys[13], (D2, CLASSES), D2 ** -0.5, 0.4375, (), jnp.float32),
        "g_logits": noise(keys[14], (SLIDES, CLASSES), 1.0, 6.0, (), jnp.float32),
    }


HIGHEST = lax.Precision.HIGHEST

def product(left_op, right_op):
    return jnp.dot(left_op, right_op, preferred_element_type=jnp.float32)

def gram_product(left_op, right_op):
    return lax.dot_general(left_op, right_op, (((0,), (0,)), ((), ())), preferred_element_type=jnp.float32)

def back_product(left_op, right_op):
    return lax.dot_general(left_op, right_op, (((1,), (1,)), ((), ())), preferred_element_type=jnp.float32)

def precise(left_op, right_op):
    return jnp.dot(left_op, right_op, precision=HIGHEST, preferred_element_type=jnp.float32)

def mix_heads(form, left_op, right_op):
    return jnp.einsum(form, left_op.astype(jnp.float32), right_op.astype(jnp.float32))

def patch_forward(token_rows, tissue_rows, w_up, w_down, w_embed):
    pre_act = product(token_rows, w_up)
    hidden = jax.nn.gelu(pre_act).astype(jnp.bfloat16)
    middle = (token_rows.astype(jnp.float32) + product(hidden, w_down)).astype(jnp.bfloat16)
    features = (tissue_rows[:, None] * product(middle, w_embed)).astype(jnp.bfloat16)
    return (features, (pre_act, hidden, middle))

def patch_backward(token_rows, kept_patch, d_features, w_down, w_embed):
    pre_act, hidden, middle = kept_patch
    g_embed = gram_product(middle, d_features)
    d_middle = back_product(d_features, w_embed).astype(jnp.bfloat16)
    g_down = gram_product(hidden, d_middle)
    d_hidden = back_product(d_middle, w_down)
    pullback = jax.vjp(jax.nn.gelu, pre_act)[1]
    d_pre = pullback(d_hidden)[0].astype(jnp.bfloat16)
    g_up = gram_product(token_rows, d_pre)
    return (g_up, g_down, g_embed)

def region_forward(features, tissue_f, w_query, w_key, w_value, w_out):
    flat = features.reshape(-1, features.shape[2])
    split = (features.shape[0], PATCH, HEADS, HEAD_DIM)
    queries = product(flat, w_query).astype(jnp.bfloat16).reshape(split)
    key_heads = product(flat, w_key).astype(jnp.bfloat16).reshape(split)
    value_heads = product(flat, w_value).astype(jnp.bfloat16).reshape(split)
    scores = mix_heads('nqhd,nkhd->nhqk', queries, key_heads) * (1.0 / math.sqrt(HEAD_DIM))
    attn_probs = jax.nn.softmax(scores, axis=-1)
    attn_b = attn_probs.astype(jnp.bfloat16)
    attended = mix_heads('nhqk,nkhd->nqhd', attn_b, value_heads).astype(jnp.bfloat16).reshape(flat.shape)
    mixed = flat.astype(jnp.float32) + product(attended, w_out)
    tissue_count = jnp.maximum(lax.optimization_barrier(jnp.sum(tissue_f, axis=1)), 1.0)
    region = lax.optimization_barrier(jnp.sum(tissue_f[:, :, None] * mixed.reshape(features.shape), axis=1)) / tissue_count[:, None]
    return (region, (queries, key_heads, value_heads, attn_probs, attn_b, attended))

def region_backward(features, tissue_f, d_region, kept_region, w_query, w_key, w_value, w_out):
    queries, key_heads, value_heads, attn_probs, attn_b, attended = kept_region
    flat = features.reshape(-1, features.shape[2])
    tissue_count = jnp.maximum(lax.optimization_barrier(jnp.sum(tissue_f, axis=1)), 1.0)
    d_mixed = (tissue_f[:, :, None] * d_region[:, None, :] / tissue_count[:, None, None]).astype(jnp.bfloat16).reshape(flat.shape)
    g_out = gram_product(attended, d_mixed)
    d_attended = back_product(d_mixed, w_out).astype(jnp.bfloat16).reshape(queries.shape)
    d_probs = mix_heads('nqhd,nkhd->nhqk', d_attended, value_heads)
    centered = d_probs - lax.optimization_barrier(jnp.sum(attn_probs * d_probs, axis=-1, keepdims=True))
    d_scores = (attn_probs * centered * (1.0 / math.sqrt(HEAD_DIM))).astype(jnp.bfloat16)
    d_query = mix_heads('nhqk,nkhd->nqhd', d_scores, key_heads).astype(jnp.bfloat16).reshape(flat.shape)
    d_key = mix_heads('nhqk,nqhd->nkhd', d_scores, queries).astype(jnp.bfloat16).reshape(flat.shape)
    d_value = mix_heads('nhqk,nqhd->nkhd', attn_b, d_attended).astype(jnp.bfloat16).reshape(flat.shape)
    g_query = gram_product(flat, d_query)
    g_key = gram_product(flat, d_key)
    g_value = gram_product(flat, d_value)
    d_flat = d_mixed.astype(jnp.float32) + back_product(d_query, w_query) + back_product(d_key, w_key) + back_product(d_value, w_value)
    d_features = (tissue_f.reshape(-1, 1) * d_flat).astype(jnp.bfloat16)
    return (d_features, (g_query, g_key, g_value, g_out))

def slide_scores(region, att_v, att_u, att_w):
    tanh_part = jnp.tanh(precise(region, att_v))
    gate_part = jax.nn.sigmoid(precise(region, att_u))
    gated_act = tanh_part * gate_part
    return ((tanh_part, gate_part, gated_act), precise(gated_act, att_w))

def slide_backward(region, member, share, d_summary, summary, parts, att_v, att_u, att_w):
    tanh_part, gate_part, gated_act = parts
    d_own = precise(member, d_summary)
    own_summary = precise(member, summary)
    d_score = share * lax.optimization_barrier(jnp.sum(d_own * (region - own_summary), axis=1))
    d_gated = d_score[:, None] * att_w[None, :]
    d_pre_v = d_gated * gate_part * (1.0 - tanh_part * tanh_part)
    d_pre_u = d_gated * tanh_part * gate_part * (1.0 - gate_part)
    d_region = share[:, None] * d_own + precise(d_pre_v, att_v.T) + precise(d_pre_u, att_u.T)
    g_att_v = precise(region.T, d_pre_v)
    g_att_u = precise(region.T, d_pre_u)
    g_att_w = precise(d_score, gated_act)
    return (d_region, (g_att_v, g_att_u, g_att_w))

def reference(patches, tissue, region_slide, w_up, w_down, w_embed, w_query, w_key, w_value, w_out, att_v, att_u, att_w, w_class, g_logits):
    tissue_f = tissue.astype(jnp.float32)
    block = 16
    width = w_embed.shape[1]
    patch_blocks = patches.reshape(REGIONS // block, block, PATCH, D1)
    tissue_blocks = tissue_f.reshape(REGIONS // block, block, PATCH)

    def encode(pair):
        token_block, tissue_block = pair
        token_rows = token_block.reshape(-1, D1)
        features, kept_patch = patch_forward(token_rows, tissue_block.reshape(-1), w_up, w_down, w_embed)
        features = features.reshape(block, PATCH, width)
        region, kept_region = region_forward(features, tissue_block, w_query, w_key, w_value, w_out)
        return (region, features, kept_patch, kept_region)
    regions = lax.map(lambda pair: encode(pair)[0], (patch_blocks, tissue_blocks)).reshape(REGIONS, width)
    member = (region_slide[:, None] == jnp.arange(SLIDES, dtype=jnp.int32)[None, :]).astype(jnp.float32)
    parts, region_score = slide_scores(regions, att_v, att_u, att_w)
    weight = jnp.exp(region_score)
    slide_total = precise(weight, member)
    slide_sum = precise(member.T, weight[:, None] * regions)
    summary = slide_sum / slide_total[:, None]
    logits = precise(summary, w_class)
    g_class = precise(summary.T, g_logits)
    d_summary = precise(g_logits, w_class.T)
    share = weight / slide_total[region_slide]
    d_regions, slide_grads = slide_backward(regions, member, share, d_summary, summary, parts, att_v, att_u, att_w)
    d_blocks = d_regions.reshape(REGIONS // block, block, width)

    def accumulate(carry, triple):
        token_block, tissue_block, d_block = triple
        region, features, kept_patch, kept_region = encode((token_block, tissue_block))
        d_features, region_grads = region_backward(features, tissue_block, d_block, kept_region, w_query, w_key, w_value, w_out)
        patch_grads = patch_backward(token_block.reshape(-1, D1), kept_patch, d_features, w_down, w_embed)
        return (jax.tree.map(jnp.add, carry, patch_grads + region_grads), region)
    zeros = (jnp.zeros((D1, F1), jnp.float32), jnp.zeros((F1, D1), jnp.float32), jnp.zeros((D1, width), jnp.float32), jnp.zeros((width, width), jnp.float32), jnp.zeros((width, width), jnp.float32), jnp.zeros((width, width), jnp.float32), jnp.zeros((width, width), jnp.float32))
    totals, ignored = lax.scan(accumulate, zeros, (patch_blocks, tissue_blocks, d_blocks))
    g_up, g_down, g_embed, g_query, g_key, g_value, g_out = totals
    g_att_v, g_att_u, g_att_w = slide_grads
    return (logits, g_up, g_down, g_embed, g_query, g_key, g_value, g_out, g_att_v, g_att_u, g_att_w, g_class)
```

```python
import math

import jax
import jax.numpy as jnp
from jax import lax
from jax.experimental import pallas as pl
from jax.experimental.pallas import tpu as pltpu
from jax.sharding import Mesh, PartitionSpec as P

D1 = 384
F1 = 1536
HEADS = 6
HEAD_DIM = 32
D2 = 192
PATCH = 256
SLIDES = 4
GRP = 16
OWN = 2
SCALE = 1.0 / math.sqrt(HEAD_DIM)
GELU_C = math.sqrt(2.0 / math.pi)
GELU_A = 0.044715

BF = jnp.bfloat16
F32 = jnp.float32
HIGHEST = lax.Precision.HIGHEST
VMEM_LIMIT = 48 * 1024 * 1024

CHUNKS = 32
HALF = CHUNKS // 2
CH_ROWS = 384


def nn(a, b, precision=None):
    return jnp.dot(a, b, precision=precision, preferred_element_type=F32)


def nt(a, b, precision=None):
    return lax.dot_general(
        a, b, (((1,), (1,)), ((), ())), precision=precision, preferred_element_type=F32
    )


def tn(a, b, precision=None):
    return lax.dot_general(
        a, b, (((0,), (0,)), ((), ())), precision=precision, preferred_element_type=F32
    )


def params():
    return pltpu.CompilerParams(vmem_limit_bytes=VMEM_LIMIT)


def patch_forward_kernel(x_ref, wu_ref, wd_ref, we_ref, feat_ref, hid_ref, gp_ref, mid_ref, acc):
    step = pl.program_id(0)
    x = x_ref[...]
    pre = nn(x, wu_ref[...])
    sq = pre * pre
    t = jnp.tanh(GELU_C * (pre + GELU_A * (pre * sq)))
    half_up = 0.5 + 0.5 * t
    hid = (pre * half_up).astype(BF)
    hid_ref[...] = hid
    slope = (0.5 * GELU_C) * (1.0 - t * t) * (1.0 + (3.0 * GELU_A) * sq)
    gp_ref[...] = (half_up + pre * slope).astype(BF)
    part = nn(hid, wd_ref[...])

    @pl.when(step == 0)
    def _():
        acc[...] = x.astype(F32) + part

    @pl.when(step > 0)
    def _():
        acc[...] += part

    @pl.when(step == pl.num_programs(0) - 1)
    def _():
        mid = acc[...].astype(BF)
        mid_ref[...] = mid
        feat_ref[...] = nn(mid, we_ref[...]).astype(BF)


def patch_forward(tokens, w_up, w_down, w_embed):
    rows = tokens.shape[0]
    steps = 3
    fb = F1 // steps
    whole = lambda i: (0, 0)
    return pl.pallas_call(
        patch_forward_kernel,
        grid=(steps,),
        in_specs=[
            pl.BlockSpec((rows, D1), whole),
            pl.BlockSpec((D1, fb), lambda i: (0, i)),
            pl.BlockSpec((fb, D1), lambda i: (i, 0)),
            pl.BlockSpec((D1, D2), whole),
        ],
        out_specs=[
            pl.BlockSpec((rows, D2), whole),
            pl.BlockSpec((rows, fb), lambda i: (0, i)),
            pl.BlockSpec((rows, fb), lambda i: (0, i)),
            pl.BlockSpec((rows, D1), whole),
        ],
        out_shape=[
            jax.ShapeDtypeStruct((rows, D2), BF),
            jax.ShapeDtypeStruct((rows, F1), BF),
            jax.ShapeDtypeStruct((rows, F1), BF),
            jax.ShapeDtypeStruct((rows, D1), BF),
        ],
        scratch_shapes=[pltpu.VMEM((rows, D1), F32)],
        compiler_params=params(),
        name="patch_forward",
    )(tokens, w_up, w_down, w_embed)


def tissue_row(idx_ref, tis_ref, r):
    return tis_ref[pl.ds(idx_ref[1] + r, 1), :].astype(F32)


def column_of(row, width):
    return jnp.broadcast_to(row, (PATCH, row.shape[1])).T[:, :width]


def head_mask(h, shape, dim):
    return (lax.broadcasted_iota(jnp.int32, shape, dim) // HEAD_DIM == h).astype(F32)


def region_forward_kernel(
    idx_ref, slide_ref, f_ref, tis_ref, wq_ref, wk_ref, wv_ref, wo_ref, av_ref, au_ref, aw_ref,
    p_ref, x_ref, q_ref, k_ref, v_ref, se_ref, asum_ref, reg_ref, tanh_ref, gate_ref, w_ref,
    part_ref,
):
    r = pl.program_id(0)
    trow = tissue_row(idx_ref, tis_ref, r)
    tcol = column_of(trow, D2)
    x = (f_ref[...].reshape(PATCH, D2).astype(F32) * tcol).astype(BF)
    x_ref[0] = x
    q = nn(x, wq_ref[...]).astype(BF)
    k = nn(x, wk_ref[...])
    v = nn(x, wv_ref[...]).astype(BF)
    q_ref[0] = q
    k_ref[0] = k.astype(BF)
    v_ref[0] = v
    spread = jnp.zeros((PATCH, D2), F32)
    for h in range(HEADS):
        mask = head_mask(h, (1, D2), 1)
        st = nt((k * mask).astype(BF), q) * SCALE
        top = jnp.max(st, axis=0, keepdims=True)
        ex = jnp.exp(st - top)
        total = jnp.sum(ex, axis=0, keepdims=True)
        pb = (ex * (1.0 / total)).astype(BF)
        p_ref[0, pl.ds(h * PATCH, PATCH), :] = pb
        spread = spread + nn(pb, (tcol * mask).astype(BF))
    se_ref[0] = spread
    asum = jnp.sum(spread * v.astype(F32), axis=0, keepdims=True)
    xsum = jnp.sum(x.astype(F32), axis=0, keepdims=True)
    count = jnp.maximum(jnp.sum(trow, axis=1, keepdims=True), 1.0)
    mixed = xsum + nn(jnp.broadcast_to(asum, (8, D2)), wo_ref[...].astype(F32), HIGHEST)[0:1]

    @pl.when(r == 0)
    def _():
        lane = lax.broadcasted_iota(jnp.int32, (8, PATCH), 1)
        reg_ref[...] = jnp.where(lane < D2, 0.0, 1.0)
        asum_ref[...] = jnp.zeros_like(asum_ref)

    asum_ref[pl.ds(r, 1), :] = asum
    reg_ref[pl.ds(r, 1), pl.ds(0, D2)] = mixed / count

    @pl.when(r == OWN - 1)
    def _():
        region = reg_ref[:, pl.ds(0, D2)]
        tanh_part = jnp.tanh(nn(region, av_ref[...], HIGHEST))
        gate_part = jax.nn.sigmoid(nn(region, au_ref[...], HIGHEST))
        tanh_ref[...] = tanh_part
        gate_ref[...] = gate_part
        score = jnp.sum(tanh_part * gate_part * aw_ref[...], axis=1, keepdims=True)
        weight = jnp.exp(score)
        w_ref[...] = jnp.broadcast_to(weight, w_ref.shape)
        wide = reg_ref[...] * weight
        slot = lax.broadcasted_iota(jnp.int32, (SLIDES, 1), 0)
        sums = jnp.zeros((SLIDES, PATCH), F32)
        for i in range(OWN):
            own = (slot == slide_ref[idx_ref[0] + i]).astype(F32)
            sums = sums + own * wide[i : i + 1]
        both = jnp.concatenate([sums[:, :128], sums[:, 128:]], axis=0)
        part_ref[...] = jnp.broadcast_to(both[None], part_ref.shape)


def region_forward(idx, slide, got, tissue, w_query, w_key, w_value, w_out, att_v, att_u, att_w):
    sq = pl.BlockSpec((D2, D2), lambda r, *_: (0, 0))
    row8 = lambda width: pl.BlockSpec((8, width), lambda r, *_: (0, 0))
    per_region = lambda rows, width: pl.BlockSpec((1, rows, width), lambda r, *_: (r, 0, 0))
    tok = lambda dt: jax.ShapeDtypeStruct((OWN, PATCH, D2), dt)
    return pl.pallas_call(
        region_forward_kernel,
        grid_spec=pltpu.PrefetchScalarGridSpec(
            num_scalar_prefetch=2,
            grid=(OWN,),
            in_specs=[
                pl.BlockSpec((GRP, 1, PATCH // GRP, D2), lambda r, *_: (0, r, 0, 0)),
                pl.BlockSpec((8, PATCH), lambda r, idx, _: (idx[2], 0)),
                sq, sq, sq, sq, sq, sq,
                pl.BlockSpec((1, D2), lambda r, *_: (0, 0)),
            ],
            out_specs=[
                per_region(HEADS * PATCH, PATCH),
                per_region(PATCH, D2),
                per_region(PATCH, D2),
                per_region(PATCH, D2),
                per_region(PATCH, D2),
                per_region(PATCH, D2),
                row8(D2),
                row8(PATCH),
                row8(D2),
                row8(D2),
                row8(128),
                pl.BlockSpec((CHUNKS, 8, 128), lambda r, *_: (0, 0, 0)),
            ],
        ),
        out_shape=[
            jax.ShapeDtypeStruct((OWN, HEADS * PATCH, PATCH), BF),
            tok(BF), tok(BF), tok(BF), tok(BF), tok(F32),
            jax.ShapeDtypeStruct((8, D2), F32),
            jax.ShapeDtypeStruct((8, PATCH), F32),
            jax.ShapeDtypeStruct((8, D2), F32),
            jax.ShapeDtypeStruct((8, D2), F32),
            jax.ShapeDtypeStruct((8, 128), F32),
            jax.ShapeDtypeStruct((CHUNKS, 8, 128), F32),
        ],
        compiler_params=params(),
        name="region_forward",
    )(idx, slide, got, tissue, w_query, w_key, w_value, w_out, att_v, att_u, att_w)


def region_backward_kernel(
    idx_ref, slide_ref, z_ref, tis_ref, wq_ref, wk_ref, wv_ref, wo_ref, av_ref, au_ref, aw_ref,
    wc_ref, gl_ref,
    p_ref, x_ref, q_ref, k_ref, v_ref, se_ref, asum_ref, reg_ref, tanh_ref, gate_ref, w_ref,
    df_ref, rest_ref, logits_ref, gc_ref,
    dm_s, da_s, kt_s, dqt_s, gq_s, gk_s, gv_s,
):
    r = pl.program_id(0)
    trow = tissue_row(idx_ref, tis_ref, r)
    tcol = column_of(trow, D2)

    def put(slot, grad, fill=None):
        low = 2 * D2 * slot
        rest_ref[pl.ds(low, D2), :] = grad[:, :128].astype(BF)
        if fill is None:
            fill = jnp.zeros((D2, 64), F32)
        high = jnp.concatenate([grad[:, 128:], fill], axis=1)
        rest_ref[pl.ds(low + D2, D2), :] = high.astype(BF)

    @pl.when(r == 0)
    def _():
        z = jnp.sum(z_ref[...], axis=0)
        low, high = z[0:SLIDES], z[SLIDES:]
        total = high[:, 64:65]
        summary = jnp.concatenate([low, high[:, :64]], axis=1) / total
        wc = wc_ref[...]
        gl = gl_ref[...]
        logits_ref[...] = nn(summary, wc, HIGHEST)
        gc_ref[...] = tn(summary, gl, HIGHEST)
        d_summary = nt(gl, wc, HIGHEST)
        slot = lax.broadcasted_iota(jnp.int32, (SLIDES, 1), 0)
        row = lax.broadcasted_iota(jnp.int32, (8, 1), 0)
        d_own = jnp.zeros((8, D2), F32)
        own_summary = jnp.zeros((8, D2), F32)
        own_total = jnp.ones((8, 1), F32)
        count = jnp.ones((8, 1), F32)
        for i in range(OWN):
            mine = slot == slide_ref[idx_ref[0] + i]
            pick = lambda a: jnp.sum(jnp.where(mine, a, 0.0), axis=0, keepdims=True)
            d_own = jnp.where(row == i, pick(d_summary), d_own)
            own_summary = jnp.where(row == i, pick(summary), own_summary)
            own_total = jnp.where(row == i, pick(total), own_total)
            t_i = tissue_row(idx_ref, tis_ref, i)
            count = jnp.where(
                row == i, jnp.maximum(jnp.sum(t_i, axis=1, keepdims=True), 1.0), count
            )
        region = reg_ref[:, pl.ds(0, D2)]
        tanh_part = tanh_ref[...]
        gate_part = gate_ref[...]
        share = jnp.where(row < OWN, w_ref[:, 0:1] / own_total, 0.0)
        d_score = share * jnp.sum(d_own * (region - own_summary), axis=1, keepdims=True)
        d_gated = d_score * aw_ref[...]
        d_pre_v = d_gated * gate_part * (1.0 - tanh_part * tanh_part)
        d_pre_u = d_gated * tanh_part * gate_part * (1.0 - gate_part)
        d_region = (
            share * d_own + nt(d_pre_v, av_ref[...], HIGHEST) + nt(d_pre_u, au_ref[...], HIGHEST)
        )
        dm = (d_region / count).astype(BF)
        dm_s[...] = dm.astype(F32)
        da_s[...] = nt(dm, wo_ref[...])
        put(3, tn(asum_ref[...], dm.astype(F32), HIGHEST))
        put(4, tn(region, d_pre_v, HIGHEST))
        put(
            5,
            tn(region, d_pre_u, HIGHEST),
            tn(tanh_part * gate_part, jnp.broadcast_to(d_score, (8, 64)), HIGHEST),
        )
        gq_s[...] = jnp.zeros_like(gq_s)
        gk_s[...] = jnp.zeros_like(gk_s)
        gv_s[...] = jnp.zeros_like(gv_s)

    x = x_ref[0]
    q = q_ref[0].astype(F32)
    v = v_ref[0]
    kt_s[...] = k_ref[0].astype(F32).T.astype(BF)
    dm = dm_s[pl.ds(r, 1), :]
    da = da_s[pl.ds(r, 1), :].astype(BF).astype(F32)
    da_col = jnp.broadcast_to(da, (128, D2)).T
    dk = jnp.zeros((PATCH, D2), F32)
    for h in range(HEADS):
        one_head = (da_col * head_mask(h, (D2, 1), 0)).astype(BF)
        e = nn(v, one_head)
        e = jnp.concatenate([e, e], axis=1)
        pt = p_ref[0, pl.ds(h * PATCH, PATCH), :].astype(F32)
        pe = pt * e
        ds = (pe - pt * jnp.sum(pe, axis=0, keepdims=True)).astype(BF)
        dk = dk + nn(ds, (q * head_mask(h, (1, D2), 1)).astype(BF))
        dqt_s[pl.ds(h * HEAD_DIM, HEAD_DIM), :] = nn(kt_s[pl.ds(h * HEAD_DIM, HEAD_DIM), :], ds)
    dq = (dqt_s[...] * (trow * SCALE)).T.astype(BF)
    dk = (dk * SCALE).astype(BF)
    dv = (se_ref[0] * da).astype(BF)
    xt = x.astype(F32).T.astype(BF)
    gq_s[...] += nn(xt, dq)
    gk_s[...] += nn(xt, dk)
    gv_s[...] += nn(xt, dv)
    d_flat = dm + nt(dq, wq_ref[...]) + nt(dk, wk_ref[...]) + nt(dv, wv_ref[...])
    df_ref[...] = (tcol * d_flat).astype(BF).reshape(df_ref.shape)

    @pl.when(r == OWN - 1)
    def _():
        put(0, gq_s[...])
        put(1, gk_s[...])
        put(2, gv_s[...])


def region_backward(idx, slide, z, tissue, weights, kept):
    sq = pl.BlockSpec((D2, D2), lambda r, *_: (0, 0))
    row8 = lambda width: pl.BlockSpec((8, width), lambda r, *_: (0, 0))
    per_region = lambda rows, width: pl.BlockSpec((1, rows, width), lambda r, *_: (r, 0, 0))
    return pl.pallas_call(
        region_backward_kernel,
        grid_spec=pltpu.PrefetchScalarGridSpec(
            num_scalar_prefetch=2,
            grid=(OWN,),
            in_specs=[
                pl.BlockSpec((8, 8, 128), lambda r, *_: (0, 0, 0)),
                pl.BlockSpec((8, PATCH), lambda r, idx, _: (idx[2], 0)),
                sq, sq, sq, sq, sq, sq,
                pl.BlockSpec((1, D2), lambda r, *_: (0, 0)),
                pl.BlockSpec((D2, 3), lambda r, *_: (0, 0)),
                pl.BlockSpec((SLIDES, 3), lambda r, *_: (0, 0)),
                per_region(HEADS * PATCH, PATCH),
                per_region(PATCH, D2),
                per_region(PATCH, D2),
                per_region(PATCH, D2),
                per_region(PATCH, D2),
                per_region(PATCH, D2),
                row8(D2),
                row8(PATCH),
                row8(D2),
                row8(D2),
                row8(128),
            ],
            out_specs=[
                pl.BlockSpec((GRP, 1, PATCH // GRP, D2), lambda r, *_: (0, r, 0, 0)),
                pl.BlockSpec((12 * D2, 128), lambda r, *_: (0, 0)),
                pl.BlockSpec((SLIDES, 3), lambda r, *_: (0, 0)),
                pl.BlockSpec((D2, 3), lambda r, *_: (0, 0)),
            ],
            scratch_shapes=[
                pltpu.VMEM((8, D2), F32),
                pltpu.VMEM((8, D2), F32),
                pltpu.VMEM((D2, PATCH), BF),
                pltpu.VMEM((D2, PATCH), F32),
                pltpu.VMEM((D2, D2), F32),
                pltpu.VMEM((D2, D2), F32),
                pltpu.VMEM((D2, D2), F32),
            ],
        ),
        out_shape=[
            jax.ShapeDtypeStruct((GRP, OWN, PATCH // GRP, D2), BF),
            jax.ShapeDtypeStruct((12 * D2, 128), BF),
            jax.ShapeDtypeStruct((SLIDES, 3), F32),
            jax.ShapeDtypeStruct((D2, 3), F32),
        ],
        compiler_params=params(),
        name="region_backward",
    )(idx, slide, z, tissue, *weights, *kept)


STEPS4 = 4
FB4 = F1 // STEPS4


def patch_backward_kernel(
    idx_ref, df_ref, x_ref, mid_ref, hid_ref, gp_ref, we_ref, wd_ref, rest_ref,
    mine_ref, other_ref,
    pack, dmid_s, sems,
):
    step = pl.program_id(0)

    @pl.when(step == 0)
    def _():
        df = df_ref[...]
        dmid_s[...] = nt(df, we_ref[...]).astype(BF)
        g_embed = tn(mid_ref[...], df)
        for j in range(24):
            pack[j, pl.ds(288, 96), :] = rest_ref[pl.ds(96 * j, 96), :]
        high = jnp.concatenate([g_embed[:, 128:], jnp.zeros((D1, 64), F32)], axis=1)
        for j in range(4):
            pack[24 + j, pl.ds(288, 96), :] = g_embed[96 * j : 96 * j + 96, :128].astype(BF)
            pack[28 + j, pl.ds(288, 96), :] = high[96 * j : 96 * j + 96].astype(BF)

    dmid = dmid_s[...]
    d_pre = (nt(dmid, wd_ref[...]) * gp_ref[...].astype(F32)).astype(BF)
    g_down = tn(hid_ref[...], dmid).astype(BF)
    g_up = tn(x_ref[...], d_pre).astype(BF)
    for j in range(8):
        for l in range(3):
            block = g_up[48 * j : 48 * j + 48, 128 * l : 128 * l + 128]
            pack[4 * j + step, pl.ds(48 * l, 48), :] = block
            block = g_down[48 * j : 48 * j + 48, 128 * l : 128 * l + 128]
            pack[8 * step + j, pl.ds(144 + 48 * l, 48), :] = block

    @pl.when(step == pl.num_programs(0) - 1)
    def _():
        core = idx_ref[3]
        keep = pltpu.make_async_copy(pack.at[pl.ds(core * HALF, HALF)], mine_ref, sems.at[0])
        send = pltpu.make_async_copy(
            pack.at[pl.ds((1 - core) * HALF, HALF)], other_ref, sems.at[1]
        )
        send.start()
        keep.start()
        send.wait()
        keep.wait()


def patch_backward(idx, df, tokens, mid, hid, gp, w_embed, w_down, rest):
    rows = tokens.shape[0]
    whole = lambda i, *_: (0, 0)
    return pl.pallas_call(
        patch_backward_kernel,
        grid_spec=pltpu.PrefetchScalarGridSpec(
            num_scalar_prefetch=1,
            grid=(STEPS4,),
            in_specs=[
                pl.BlockSpec((rows, D2), whole),
                pl.BlockSpec((rows, D1), whole),
                pl.BlockSpec((rows, D1), whole),
                pl.BlockSpec((rows, FB4), lambda i, *_: (0, i)),
                pl.BlockSpec((rows, FB4), lambda i, *_: (0, i)),
                pl.BlockSpec((D1, D2), whole),
                pl.BlockSpec((FB4, D1), lambda i, *_: (i, 0)),
                pl.BlockSpec((12 * D2, 128), whole),
            ],
            out_specs=[
                pl.BlockSpec(memory_space=pl.ANY),
                pl.BlockSpec(memory_space=pl.ANY),
            ],
            scratch_shapes=[
                pltpu.VMEM((CHUNKS, CH_ROWS, 128), BF),
                pltpu.VMEM((rows, D1), BF),
                pltpu.SemaphoreType.DMA((2,)),
            ],
        ),
        out_shape=[
            jax.ShapeDtypeStruct((HALF, CH_ROWS, 128), BF),
            jax.ShapeDtypeStruct((HALF, CH_ROWS, 128), BF),
        ],
        compiler_params=params(),
        name="patch_backward",
    )(idx, df, tokens, mid, hid, gp, w_embed, w_down, rest)


def unpack_kernel(
    idx_ref, mine_ref, other_ref,
    up_ref, down_ref, embed_ref, q_ref, k_ref, v_ref, o_ref, av_ref, au_ref, aw_ref,
    pack, sems,
):
    core = idx_ref[3]
    keep = pltpu.make_async_copy(mine_ref, pack.at[pl.ds(core * HALF, HALF)], sems.at[0])
    got = pltpu.make_async_copy(other_ref, pack.at[pl.ds((1 - core) * HALF, HALF)], sems.at[1])
    keep.start()
    got.start()
    keep.wait()
    got.wait()
    for j in range(CHUNKS):
        for l in range(3):
            lanes = pl.ds(384 * (j % 4) + 128 * l, 128)
            up_ref[pl.ds(48 * (j // 4), 48), lanes] = pack[j, pl.ds(48 * l, 48), :].astype(F32)
            lanes = pl.ds(128 * l, 128)
            down_ref[pl.ds(48 * j, 48), lanes] = pack[j, pl.ds(144 + 48 * l, 48), :].astype(F32)
    for slot, ref in enumerate((q_ref, k_ref, v_ref, o_ref, av_ref, au_ref)):
        for i in range(2):
            rows = pl.ds(96 * i, 96)
            ref[rows, pl.ds(0, 128)] = pack[4 * slot + i, pl.ds(288, 96), :].astype(F32)
            ref[rows, pl.ds(128, 64)] = pack[4 * slot + 2 + i, pl.ds(288, 96), :][:, :64].astype(F32)
    tail = jnp.concatenate(
        [pack[22, pl.ds(288, 96), :].astype(F32), pack[23, pl.ds(288, 96), :].astype(F32)], axis=0
    )
    aw_ref[...] = tail.T[64:65, :]
    for i in range(4):
        rows = pl.ds(96 * i, 96)
        embed_ref[rows, pl.ds(0, 128)] = pack[24 + i, pl.ds(288, 96), :].astype(F32)
        embed_ref[rows, pl.ds(128, 64)] = pack[28 + i, pl.ds(288, 96), :][:, :64].astype(F32)


def unpack(idx, mine, other):
    square = jax.ShapeDtypeStruct((D2, D2), F32)
    vm = pl.BlockSpec(memory_space=pltpu.VMEM)
    return pl.pallas_call(
        unpack_kernel,
        in_specs=[
            pl.BlockSpec(memory_space=pltpu.SMEM),
            pl.BlockSpec(memory_space=pl.ANY),
            pl.BlockSpec(memory_space=pl.ANY),
        ],
        out_specs=[vm] * 10,
        out_shape=[
            jax.ShapeDtypeStruct((D1, F1), F32),
            jax.ShapeDtypeStruct((F1, D1), F32),
            jax.ShapeDtypeStruct((D1, D2), F32),
            square, square, square, square, square, square,
            jax.ShapeDtypeStruct((1, D2), F32),
        ],
        scratch_shapes=[
            pltpu.VMEM((CHUNKS, CH_ROWS, 128), BF),
            pltpu.SemaphoreType.DMA((2,)),
        ],
        compiler_params=params(),
        name="unpack",
    )(idx, mine, other)


GRP_AXES = ("zl", "x", "c")
DEV_AXES = ("zh", "y")
XY = ("y", "x")
XYC = ("y", "x", "c")
Z = ("zh", "zl")


def exchange(x, axes):
    return lax.all_to_all(x, axes, split_axis=0, concat_axis=0, tiled=True)


def swap_cores(x):
    return lax.ppermute(x, "c", [(0, 1), (1, 0)])


def spread(x, n):
    return jnp.broadcast_to(x[None], (n,) + x.shape)


def add_up(x):
    return jnp.sum(x.astype(F32), axis=0).astype(x.dtype)


def body(
    patches, tissue, region_slide, w_up, w_down, w_embed, w_query, w_key, w_value, w_out,
    att_v, att_u, att_w, w_class, g_logits,
):
    grp = lax.axis_index(GRP_AXES)
    dev = lax.axis_index(DEV_AXES)
    core = lax.axis_index("c")
    first = (dev * GRP + grp) * OWN
    idx = jnp.stack([first, first % 8, first // 8, core]).astype(jnp.int32)
    tokens = patches.reshape(-1, D1)
    att_row = att_w.reshape(1, D2)
    feat, hid, gp, mid = patch_forward(tokens, w_up, w_down, w_embed)
    got = exchange(feat.reshape(GRP, -1, D2), GRP_AXES)
    got = got.reshape(GRP, OWN, PATCH // GRP, D2)
    *kept, part = region_forward(
        idx, region_slide, got, tissue, w_query, w_key, w_value, w_out, att_v, att_u, att_row
    )
    z = add_up(exchange(part, XYC))
    z = exchange(spread(z, 8), Z)
    df, rest, logits, g_class = region_backward(
        idx, region_slide, z, tissue,
        (w_query, w_key, w_value, w_out, att_v, att_u, att_row, w_class, g_logits), kept,
    )
    back = exchange(df.reshape(GRP, -1, D2), GRP_AXES).reshape(-1, D2)
    mine, other = patch_backward(idx, back, tokens, mid, hid, gp, w_embed, w_down, rest)
    half = (mine.astype(F32) + swap_cores(other).astype(F32)).astype(BF)
    chunk = add_up(exchange(half, XY))
    piece = add_up(exchange(chunk.reshape(8, CH_ROWS // 8, 128), Z))
    chunk = exchange(spread(piece, 8), Z).reshape(CH_ROWS, 128)
    half = exchange(spread(chunk, HALF), XY)
    up, down, embed, query, key, value, out, gv, gu, gw = unpack(idx, half, swap_cores(half))
    return (
        logits, up, down, embed, query, key, value, out, gv, gu, gw.reshape(D2), g_class,
    )


def solution(mesh):
    fine = Mesh(mesh.devices.reshape(2, 4, 2, 4, 4), GRP_AXES + DEV_AXES)
    placed = (P(DEV_AXES, GRP_AXES, None),) + (P(),) * 14
    return jax.shard_map(
        body,
        mesh=fine,
        in_specs=placed,
        out_specs=(P(),) * 12,
        check_vma=False,
    )
```

```python
import math

import jax
import jax.numpy as jnp
from jax import lax
from jax.experimental import pallas as pl
from jax.experimental.pallas import tpu as pltpu
from jax.sharding import Mesh, PartitionSpec as P

D1 = 384
F1 = 1536
HEADS = 6
HEAD_DIM = 32
D2 = 192
PATCH = 256
SLIDES = 4
GRP = 16
OWN = 2
SCALE = 1.0 / math.sqrt(HEAD_DIM)
GELU_C = math.sqrt(2.0 / math.pi)
GELU_A = 0.044715

BF = jnp.bfloat16
F32 = jnp.float32
HIGHEST = lax.Precision.HIGHEST
MIB = 1024 * 1024

HALF_ROWS = 6144
DOWN_AT = 2304
REST_AT = 4608
REST_ROWS = 1152
EMBED_AT = REST_AT + REST_ROWS
PAD_AT = EMBED_AT + 288
PEERS = 32


def nn(a, b, precision=None):
    return jnp.dot(a, b, precision=precision, preferred_element_type=F32)


def nt(a, b, precision=None):
    return lax.dot_general(
        a, b, (((1,), (1,)), ((), ())), precision=precision, preferred_element_type=F32
    )


def tn(a, b, precision=None):
    return lax.dot_general(
        a, b, (((0,), (0,)), ((), ())), precision=precision, preferred_element_type=F32
    )


def params(mib=32):
    return pltpu.CompilerParams(vmem_limit_bytes=mib * MIB)


def fetch_all(srcs, dsts, sems):
    copies = [
        pltpu.make_async_copy(src, dst, sems.at[i]) for i, (src, dst) in enumerate(zip(srcs, dsts))
    ]
    for copy in copies:
        copy.start()
    for copy in copies:
        copy.wait()


def weight_scratch():
    return [pltpu.VMEM((D2, D2), BF)] * 4 + [pltpu.VMEM((D2, D2), F32)] * 2 + [
        pltpu.SemaphoreType.DMA((6,))
    ]


def patch_forward_kernel(x_ref, wu_ref, wd_ref, we_ref, feat_ref, hid_ref, gp_ref, mid_ref, acc):
    step = pl.program_id(0)
    x = x_ref[...]
    pre = nn(x, wu_ref[...])
    sq = pre * pre
    t = jnp.tanh(GELU_C * (pre + GELU_A * (pre * sq)))
    half_up = 0.5 + 0.5 * t
    hid = (pre * half_up).astype(BF)
    hid_ref[...] = hid
    slope = (0.5 * GELU_C) * (1.0 - t * t) * (1.0 + (3.0 * GELU_A) * sq)
    gp_ref[...] = (half_up + pre * slope).astype(BF)
    part = nn(hid, wd_ref[...])

    @pl.when(step == 0)
    def _():
        acc[...] = x.astype(F32) + part

    @pl.when(step > 0)
    def _():
        acc[...] += part

    @pl.when(step == pl.num_programs(0) - 1)
    def _():
        mid = acc[...].astype(BF)
        mid_ref[...] = mid
        feat_ref[...] = nt(mid, we_ref[...]).astype(BF)


def patch_forward(tokens, w_up, w_down, w_embed):
    rows = tokens.shape[0]
    steps = 3
    fb = F1 // steps
    whole = lambda i: (0, 0)
    return pl.pallas_call(
        patch_forward_kernel,
        grid=(steps,),
        in_specs=[
            pl.BlockSpec((rows, D1), whole),
            pl.BlockSpec((D1, fb), lambda i: (0, i)),
            pl.BlockSpec((fb, D1), lambda i: (i, 0)),
            pl.BlockSpec((D2, D1), whole),
        ],
        out_specs=[
            pl.BlockSpec((rows, D2), whole),
            pl.BlockSpec((rows, fb), lambda i: (0, i)),
            pl.BlockSpec((rows, fb), lambda i: (0, i)),
            pl.BlockSpec((rows, D1), whole),
        ],
        out_shape=[
            jax.ShapeDtypeStruct((rows, D2), BF),
            jax.ShapeDtypeStruct((rows, F1), BF),
            jax.ShapeDtypeStruct((rows, F1), BF),
            jax.ShapeDtypeStruct((rows, D1), BF),
        ],
        scratch_shapes=[pltpu.VMEM((rows, D1), F32)],
        compiler_params=params(60),
        name="patch_forward",
    )(tokens, w_up, w_down, w_embed)


def tissue_row(idx_ref, tis_ref, r):
    return tis_ref[pl.ds(idx_ref[1] + r, 1), :].astype(F32)


def column_of(row, width):
    return jnp.broadcast_to(row, (PATCH, row.shape[1])).T[:, :width]


def head_mask(h, shape, dim):
    return (lax.broadcasted_iota(jnp.int32, shape, dim) // HEAD_DIM == h).astype(F32)


def region_forward_kernel(
    idx_ref, slide_ref, f_ref, tis_ref, wq_in, wk_in, wv_in, wo_in, av_in, au_in, aw_ref,
    p_ref, x_ref, q_ref, k_ref, v_ref, se_ref, asum_ref, reg_ref, tanh_ref, gate_ref, w_ref,
    part_ref,
    wq_ref, wk_ref, wv_ref, wo_ref, av_ref, au_ref, wsems,
):
    r = pl.program_id(0)

    @pl.when(r == 0)
    def _():
        fetch_all(
            (wq_in, wk_in, wv_in, wo_in, av_in, au_in),
            (wq_ref, wk_ref, wv_ref, wo_ref, av_ref, au_ref),
            wsems,
        )

    trow = tissue_row(idx_ref, tis_ref, r)
    tcol = column_of(trow, D2)
    x = (f_ref[...].reshape(PATCH, D2).astype(F32) * tcol).astype(BF)
    x_ref[0] = x
    q = nn(x, wq_ref[...]).astype(BF)
    k = nn(x, wk_ref[...])
    v = nn(x, wv_ref[...]).astype(BF)
    q_ref[0] = q
    k_ref[0] = k.astype(BF)
    v_ref[0] = v
    spread = jnp.zeros((PATCH, D2), F32)
    for h in range(HEADS):
        mask = head_mask(h, (1, D2), 1)
        st = nt((k * mask).astype(BF), q) * SCALE
        top = jnp.max(st, axis=0, keepdims=True)
        ex = jnp.exp(st - top)
        total = jnp.sum(ex, axis=0, keepdims=True)
        pb = (ex * (1.0 / total)).astype(BF)
        p_ref[0, pl.ds(h * PATCH, PATCH), :] = pb
        spread = spread + nn(pb, (tcol * mask).astype(BF))
    se_ref[0] = spread
    asum = jnp.sum(spread * v.astype(F32), axis=0, keepdims=True)
    xsum = jnp.sum(x.astype(F32), axis=0, keepdims=True)
    count = jnp.maximum(jnp.sum(trow, axis=1, keepdims=True), 1.0)
    mixed = xsum + nn(jnp.broadcast_to(asum, (8, D2)), wo_ref[...].astype(F32), HIGHEST)[0:1]

    @pl.when(r == 0)
    def _():
        lane = lax.broadcasted_iota(jnp.int32, (8, PATCH), 1)
        reg_ref[...] = jnp.where(lane < D2, 0.0, 1.0)
        asum_ref[...] = jnp.zeros_like(asum_ref)

    asum_ref[pl.ds(r, 1), :] = asum
    reg_ref[pl.ds(r, 1), pl.ds(0, D2)] = mixed / count

    @pl.when(r == OWN - 1)
    def _():
        region = reg_ref[:, pl.ds(0, D2)]
        tanh_part = jnp.tanh(nn(region, av_ref[...], HIGHEST))
        gate_part = jax.nn.sigmoid(nn(region, au_ref[...], HIGHEST))
        tanh_ref[...] = tanh_part
        gate_ref[...] = gate_part
        score = jnp.sum(tanh_part * gate_part * aw_ref[...], axis=1, keepdims=True)
        weight = jnp.exp(score)
        w_ref[...] = jnp.broadcast_to(weight, w_ref.shape)
        wide = reg_ref[...] * weight
        slot = lax.broadcasted_iota(jnp.int32, (SLIDES, 1), 0)
        sums = jnp.zeros((SLIDES, PATCH), F32)
        for i in range(OWN):
            own = (slot == slide_ref[idx_ref[0] + i]).astype(F32)
            sums = sums + own * wide[i : i + 1]
        both = jnp.concatenate([sums[:, :128], sums[:, 128:]], axis=0)
        part_ref[...] = jnp.broadcast_to(both[None], part_ref.shape)


def region_forward(idx, slide, got, tissue, w_query, w_key, w_value, w_out, att_v, att_u, att_w):
    sq = pl.BlockSpec(memory_space=pltpu.HBM)
    row8 = lambda width: pl.BlockSpec((8, width), lambda r, *_: (0, 0))
    per_region = lambda rows, width: pl.BlockSpec((1, rows, width), lambda r, *_: (r, 0, 0))
    tok = lambda dt: jax.ShapeDtypeStruct((OWN, PATCH, D2), dt)
    return pl.pallas_call(
        region_forward_kernel,
        grid_spec=pltpu.PrefetchScalarGridSpec(
            num_scalar_prefetch=2,
            grid=(OWN,),
            in_specs=[
                pl.BlockSpec((GRP, 1, PATCH // GRP, D2), lambda r, *_: (0, r, 0, 0)),
                pl.BlockSpec((8, PATCH), lambda r, idx, _: (idx[2], 0)),
                sq, sq, sq, sq, sq, sq,
                pl.BlockSpec((1, D2), lambda r, *_: (0, 0)),
            ],
            out_specs=[
                per_region(HEADS * PATCH, PATCH),
                per_region(PATCH, D2),
                per_region(PATCH, D2),
                per_region(PATCH, D2),
                per_region(PATCH, D2),
                per_region(PATCH, D2),
                row8(D2),
                row8(PATCH),
                row8(D2),
                row8(D2),
                row8(128),
                pl.BlockSpec((PEERS, 8, 128), lambda r, *_: (0, 0, 0)),
            ],
            scratch_shapes=weight_scratch(),
        ),
        out_shape=[
            jax.ShapeDtypeStruct((OWN, HEADS * PATCH, PATCH), BF),
            tok(BF), tok(BF), tok(BF), tok(BF), tok(F32),
            jax.ShapeDtypeStruct((8, D2), F32),
            jax.ShapeDtypeStruct((8, PATCH), F32),
            jax.ShapeDtypeStruct((8, D2), F32),
            jax.ShapeDtypeStruct((8, D2), F32),
            jax.ShapeDtypeStruct((8, 128), F32),
            jax.ShapeDtypeStruct((PEERS, 8, 128), F32),
        ],
        compiler_params=params(60),
        name="region_forward",
    )(idx, slide, got, tissue, w_query, w_key, w_value, w_out, att_v, att_u, att_w)


def region_backward_kernel(
    idx_ref, slide_ref, z_ref, tis_ref, wq_in, wk_in, wv_in, wo_in, av_in, au_in, aw_ref,
    wc_ref, gl_ref,
    p_ref, x_ref, q_ref, k_ref, v_ref, se_ref, asum_ref, reg_ref, tanh_ref, gate_ref, w_ref,
    df_ref, rest_ref, logits_ref, gc_ref,
    dm_s, da_s, kt_s, dqt_s, gq_s, gk_s, gv_s,
    wq_ref, wk_ref, wv_ref, wo_ref, av_ref, au_ref, wsems,
):
    r = pl.program_id(0)
    trow = tissue_row(idx_ref, tis_ref, r)
    tcol = column_of(trow, D2)

    def put(slot, grad, fill=None):
        for half in range(2):
            rows = grad[96 * half : 96 * half + 96]
            rest_ref[half, pl.ds(192 * slot, 96), :] = rows[:, :128].astype(BF)
            tail = jnp.zeros((96, 64), F32) if fill is None else fill
            high = jnp.concatenate([rows[:, 128:], tail], axis=1)
            rest_ref[half, pl.ds(192 * slot + 96, 96), :] = high.astype(BF)

    @pl.when(r == 0)
    def _():
        fetch_all(
            (wq_in, wk_in, wv_in, wo_in, av_in, au_in),
            (wq_ref, wk_ref, wv_ref, wo_ref, av_ref, au_ref),
            wsems,
        )
        z = jnp.sum(z_ref[...], axis=0)
        low, high = z[0:SLIDES], z[SLIDES:]
        total = high[:, 64:65]
        summary = jnp.concatenate([low, high[:, :64]], axis=1) / total
        wc = wc_ref[...]
        gl = gl_ref[...]
        logits_ref[...] = nt(summary, wc, HIGHEST)
        gc_ref[...] = tn(gl, summary, HIGHEST)
        d_summary = nn(gl, wc, HIGHEST)
        slot = lax.broadcasted_iota(jnp.int32, (SLIDES, 1), 0)
        row = lax.broadcasted_iota(jnp.int32, (8, 1), 0)
        d_own = jnp.zeros((8, D2), F32)
        own_summary = jnp.zeros((8, D2), F32)
        own_total = jnp.ones((8, 1), F32)
        count = jnp.ones((8, 1), F32)
        for i in range(OWN):
            mine = slot == slide_ref[idx_ref[0] + i]
            pick = lambda a: jnp.sum(jnp.where(mine, a, 0.0), axis=0, keepdims=True)
            d_own = jnp.where(row == i, pick(d_summary), d_own)
            own_summary = jnp.where(row == i, pick(summary), own_summary)
            own_total = jnp.where(row == i, pick(total), own_total)
            t_i = tissue_row(idx_ref, tis_ref, i)
            count = jnp.where(
                row == i, jnp.maximum(jnp.sum(t_i, axis=1, keepdims=True), 1.0), count
            )
        region = reg_ref[:, pl.ds(0, D2)]
        tanh_part = tanh_ref[...]
        gate_part = gate_ref[...]
        share = jnp.where(row < OWN, w_ref[:, 0:1] / own_total, 0.0)
        d_score = share * jnp.sum(d_own * (region - own_summary), axis=1, keepdims=True)
        d_gated = d_score * aw_ref[...]
        d_pre_v = d_gated * gate_part * (1.0 - tanh_part * tanh_part)
        d_pre_u = d_gated * tanh_part * gate_part * (1.0 - gate_part)
        d_region = (
            share * d_own + nt(d_pre_v, av_ref[...], HIGHEST) + nt(d_pre_u, au_ref[...], HIGHEST)
        )
        dm = (d_region / count).astype(BF)
        dm_s[...] = dm.astype(F32)
        da_s[...] = nt(dm, wo_ref[...])
        put(3, tn(asum_ref[...], dm.astype(F32), HIGHEST))
        put(4, tn(region, d_pre_v, HIGHEST))
        g_aw = tn(tanh_part * gate_part, jnp.broadcast_to(d_score, (8, 64)), HIGHEST)
        lane = lax.broadcasted_iota(jnp.int32, (96, 64), 1)
        put(5, tn(region, d_pre_u, HIGHEST), jnp.where(lane == 0, g_aw[:96], g_aw[96:]))
        gq_s[...] = jnp.zeros_like(gq_s)
        gk_s[...] = jnp.zeros_like(gk_s)
        gv_s[...] = jnp.zeros_like(gv_s)

    x = x_ref[0]
    q = q_ref[0].astype(F32)
    v = v_ref[0]
    kt_s[...] = k_ref[0].astype(F32).T.astype(BF)
    dm = dm_s[pl.ds(r, 1), :]
    da = da_s[pl.ds(r, 1), :].astype(BF).astype(F32)
    da_col = jnp.broadcast_to(da, (128, D2)).T
    dk = jnp.zeros((PATCH, D2), F32)
    for h in range(HEADS):
        one_head = (da_col * head_mask(h, (D2, 1), 0)).astype(BF)
        e = nn(v, one_head)
        e = jnp.concatenate([e, e], axis=1)
        pt = p_ref[0, pl.ds(h * PATCH, PATCH), :].astype(F32)
        pe = pt * e
        ds = (pe - pt * jnp.sum(pe, axis=0, keepdims=True)).astype(BF)
        dk = dk + nn(ds, (q * head_mask(h, (1, D2), 1)).astype(BF))
        dqt_s[pl.ds(h * HEAD_DIM, HEAD_DIM), :] = nn(kt_s[pl.ds(h * HEAD_DIM, HEAD_DIM), :], ds)
    dq = (dqt_s[...] * (trow * SCALE)).T.astype(BF)
    dk = (dk * SCALE).astype(BF)
    dv = (se_ref[0] * da).astype(BF)
    xt = x.astype(F32).T.astype(BF)
    gq_s[...] += nn(xt, dq)
    gk_s[...] += nn(xt, dk)
    gv_s[...] += nn(xt, dv)
    d_flat = dm + nt(dq, wq_ref[...]) + nt(dk, wk_ref[...]) + nt(dv, wv_ref[...])
    df_ref[...] = (tcol * d_flat).astype(BF).reshape(df_ref.shape)

    @pl.when(r == OWN - 1)
    def _():
        put(0, gq_s[...])
        put(1, gk_s[...])
        put(2, gv_s[...])


def region_backward(idx, slide, z, tissue, weights, kept):
    sq = pl.BlockSpec(memory_space=pltpu.HBM)
    row8 = lambda width: pl.BlockSpec((8, width), lambda r, *_: (0, 0))
    per_region = lambda rows, width: pl.BlockSpec((1, rows, width), lambda r, *_: (r, 0, 0))
    return pl.pallas_call(
        region_backward_kernel,
        grid_spec=pltpu.PrefetchScalarGridSpec(
            num_scalar_prefetch=2,
            grid=(OWN,),
            in_specs=[
                pl.BlockSpec((8, 8, 128), lambda r, *_: (0, 0, 0)),
                pl.BlockSpec((8, PATCH), lambda r, idx, _: (idx[2], 0)),
                sq, sq, sq, sq, sq, sq,
                pl.BlockSpec((1, D2), lambda r, *_: (0, 0)),
                pl.BlockSpec((3, D2), lambda r, *_: (0, 0)),
                pl.BlockSpec((SLIDES, 3), lambda r, *_: (0, 0)),
                per_region(HEADS * PATCH, PATCH),
                per_region(PATCH, D2),
                per_region(PATCH, D2),
                per_region(PATCH, D2),
                per_region(PATCH, D2),
                per_region(PATCH, D2),
                row8(D2),
                row8(PATCH),
                row8(D2),
                row8(D2),
                row8(128),
            ],
            out_specs=[
                pl.BlockSpec((GRP, 1, PATCH // GRP, D2), lambda r, *_: (0, r, 0, 0)),
                pl.BlockSpec((2, REST_ROWS, 128), lambda r, *_: (0, 0, 0)),
                pl.BlockSpec((SLIDES, 3), lambda r, *_: (0, 0)),
                pl.BlockSpec((3, D2), lambda r, *_: (0, 0)),
            ],
            scratch_shapes=[
                pltpu.VMEM((8, D2), F32),
                pltpu.VMEM((8, D2), F32),
                pltpu.VMEM((D2, PATCH), BF),
                pltpu.VMEM((D2, PATCH), F32),
                pltpu.VMEM((D2, D2), F32),
                pltpu.VMEM((D2, D2), F32),
                pltpu.VMEM((D2, D2), F32),
            ] + weight_scratch(),
        ),
        out_shape=[
            jax.ShapeDtypeStruct((GRP, OWN, PATCH // GRP, D2), BF),
            jax.ShapeDtypeStruct((2, REST_ROWS, 128), BF),
            jax.ShapeDtypeStruct((SLIDES, 3), F32),
            jax.ShapeDtypeStruct((3, D2), F32),
        ],
        compiler_params=params(60),
        name="region_backward",
    )(idx, slide, z, tissue, *weights, *kept)


STEPS4 = 4
FB4 = F1 // STEPS4


def patch_backward_kernel(
    idx_ref, df_ref, x_ref, mid_ref, hid_ref, gp_ref, we_ref, wd_ref, rest_ref,
    mine_ref, other_ref,
    pack, dmid_s, sems,
):
    step = pl.program_id(0)
    core = idx_ref[3]

    def up_copies(i):
        rows = pl.ds(pl.multiple_of(576 * i, 64), 576)
        return (
            pltpu.make_async_copy(pack.at[core, rows], mine_ref.at[rows], sems.at[2 * i]),
            pltpu.make_async_copy(pack.at[1 - core, rows], other_ref.at[rows], sems.at[2 * i + 1]),
        )

    def down_copy(i, dst):
        rows = pl.ds(pl.multiple_of(DOWN_AT + 1152 * lax.rem(i, 2), 128), 1152)
        return pltpu.make_async_copy(pack.at[i // 2, rows], dst.at[rows], sems.at[8 + i])

    def rest_copies():
        rows = pl.ds(REST_AT, HALF_ROWS - REST_AT)
        return (
            pltpu.make_async_copy(pack.at[core, rows], mine_ref.at[rows], sems.at[12]),
            pltpu.make_async_copy(pack.at[1 - core, rows], other_ref.at[rows], sems.at[13]),
        )

    @pl.when(step == 0)
    def _():
        df = df_ref[...]
        dmid_s[...] = nn(df, we_ref[...]).astype(BF)
        g_embed = tn(df, mid_ref[...]).astype(BF)
        for half in range(2):
            pack[half, pl.ds(REST_AT, REST_ROWS), :] = rest_ref[half]
            for l in range(3):
                block = g_embed[96 * half : 96 * half + 96, 128 * l : 128 * l + 128]
                pack[half, pl.ds(EMBED_AT + 96 * l, 96), :] = block
            pack[half, pl.ds(PAD_AT, 96), :] = jnp.zeros((96, 128), BF)
        for copy in rest_copies():
            copy.start()

    dmid = dmid_s[...]
    d_pre = (nt(dmid, wd_ref[...]) * gp_ref[...].astype(F32)).astype(BF)
    g_up = tn(x_ref[...], d_pre).astype(BF)
    for half in range(2):
        for l in range(3):
            block = g_up[192 * half : 192 * half + 192, 128 * l : 128 * l + 128]
            pack[half, pl.ds(pl.multiple_of(576 * step + 192 * l, 64), 192), :] = block
    for copy in up_copies(step):
        copy.start()
    g_down = tn(hid_ref[...], dmid).astype(BF)
    at = DOWN_AT + 1152 * lax.rem(step, 2)
    for l in range(3):
        rows = pl.ds(pl.multiple_of(at + 384 * l, 128), 384)
        pack[step // 2, rows, :] = g_down[:, 128 * l : 128 * l + 128]

    @pl.when(step // 2 == core)
    def _():
        down_copy(step, mine_ref).start()

    @pl.when(step // 2 != core)
    def _():
        down_copy(step, other_ref).start()

    @pl.when(step == pl.num_programs(0) - 1)
    def _():
        for copy in rest_copies():
            copy.wait()
        for i in range(STEPS4):
            for copy in up_copies(i):
                copy.wait()
            down_copy(i, mine_ref).wait()


def patch_backward(idx, df, tokens, mid, hid, gp, w_embed, w_down, rest):
    rows = tokens.shape[0]
    whole = lambda i, *_: (0, 0)
    return pl.pallas_call(
        patch_backward_kernel,
        grid_spec=pltpu.PrefetchScalarGridSpec(
            num_scalar_prefetch=1,
            grid=(STEPS4,),
            in_specs=[
                pl.BlockSpec((rows, D2), whole),
                pl.BlockSpec((rows, D1), whole),
                pl.BlockSpec((rows, D1), whole),
                pl.BlockSpec((rows, FB4), lambda i, *_: (0, i)),
                pl.BlockSpec((rows, FB4), lambda i, *_: (0, i)),
                pl.BlockSpec((D2, D1), whole),
                pl.BlockSpec((FB4, D1), lambda i, *_: (i, 0)),
                pl.BlockSpec((2, REST_ROWS, 128), lambda i, *_: (0, 0, 0)),
            ],
            out_specs=[
                pl.BlockSpec(memory_space=pl.ANY),
                pl.BlockSpec(memory_space=pl.ANY),
            ],
            scratch_shapes=[
                pltpu.VMEM((2, HALF_ROWS, 128), BF),
                pltpu.VMEM((rows, D1), BF),
                pltpu.SemaphoreType.DMA((14,)),
            ],
        ),
        out_shape=[
            jax.ShapeDtypeStruct((HALF_ROWS, 128), BF),
            jax.ShapeDtypeStruct((HALF_ROWS, 128), BF),
        ],
        compiler_params=params(58),
        name="patch_backward",
    )(idx, df, tokens, mid, hid, gp, w_embed, w_down, rest)


def unpack_kernel(idx_ref, src_ref, *refs):
    up_ref, down_ref, embed_ref, q_ref, k_ref, v_ref, o_ref, av_ref, au_ref, aw_ref = refs[-10:]
    for l in range(12):
        up_ref[:, pl.ds(128 * l, 128)] = src_ref[pl.ds(192 * l, 192), :].astype(F32)
    for i in range(2):
        for l in range(3):
            rows = src_ref[pl.ds(DOWN_AT + 1152 * i + 384 * l, 384), :]
            down_ref[pl.ds(384 * i, 384), pl.ds(128 * l, 128)] = rows.astype(F32)
    for slot, ref in enumerate((q_ref, k_ref, v_ref, o_ref, av_ref, au_ref)):
        at = REST_AT + 192 * slot
        ref[:, pl.ds(0, 128)] = src_ref[pl.ds(at, 96), :].astype(F32)
        ref[:, pl.ds(128, 64)] = src_ref[pl.ds(at + 96, 96), :][:, :64].astype(F32)
    for l in range(3):
        embed_ref[:, pl.ds(128 * l, 128)] = src_ref[pl.ds(EMBED_AT + 96 * l, 96), :].astype(F32)
    tail = src_ref[pl.ds(EMBED_AT - 96, 96), :].astype(F32).T
    aw_ref[:, pl.ds(0, 96)] = tail[64:65, :]
    aw_ref[:, pl.ds(96, 96)] = tail[65:66, :]


def unpack(idx, src, which, earlier=()):
    square = jax.ShapeDtypeStruct((D2, D2), F32)
    half = lambda rows, width: pl.BlockSpec((rows, width), lambda i, idx: (idx[which], 0))
    hbm = pl.BlockSpec(memory_space=pltpu.HBM)
    return pl.pallas_call(
        unpack_kernel,
        grid_spec=pltpu.PrefetchScalarGridSpec(
            num_scalar_prefetch=1,
            grid=(1,),
            in_specs=[pl.BlockSpec((HALF_ROWS, 128), lambda i, idx: (0, 0))] + [hbm] * len(earlier),
            out_specs=[
                half(D1 // 2, F1),
                half(F1 // 2, D1),
                half(D2 // 2, D1),
            ]
            + [half(D2 // 2, D2)] * 6
            + [pl.BlockSpec((1, D2), lambda i, idx: (0, 0))],
        ),
        out_shape=[
            jax.ShapeDtypeStruct((D1, F1), F32),
            jax.ShapeDtypeStruct((F1, D1), F32),
            jax.ShapeDtypeStruct((D2, D1), F32),
            square, square, square, square, square, square,
            jax.ShapeDtypeStruct((1, D2), F32),
        ],
        input_output_aliases={2 + i: i for i in range(len(earlier))},
        compiler_params=params(),
        name="unpack",
    )(idx, src, *earlier)


GRP_AXES = ("zl", "x", "c")
DEV_AXES = ("zh", "y")
ZLXY = ("y", "zl", "x")
XYC = ("y", "x", "c")
Z = ("zh", "zl")


def exchange(x, axes):
    return lax.all_to_all(x, axes, split_axis=0, concat_axis=0, tiled=True)


def swap_cores(x):
    return lax.ppermute(x, "c", [(0, 1), (1, 0)])


def spread(x, n):
    return jnp.broadcast_to(x[None], (n,) + x.shape)


def add_pair(x, y):
    return (x.astype(F32) + y.astype(F32)).astype(x.dtype)


def add_over_zh(x):
    for flip in (1, 3):
        x = add_pair(x, lax.ppermute(x, "zh", [(i, i ^ flip) for i in range(4)]))
    return x


def add_up(x):
    return jnp.sum(x.astype(F32), axis=0).astype(x.dtype)


def body(
    patches, tissue, region_slide, w_up, w_down, w_embed, w_query, w_key, w_value, w_out,
    att_v, att_u, att_w, w_class, g_logits,
):
    grp = lax.axis_index(GRP_AXES)
    dev = lax.axis_index(DEV_AXES)
    core = lax.axis_index("c")
    first = (dev * GRP + grp) * OWN
    idx = jnp.stack([first, first % 8, first // 8, core, 1 - core]).astype(jnp.int32)
    tokens = patches.reshape(-1, D1)
    att_row = att_w.reshape(1, D2)
    feat, hid, gp, mid = patch_forward(tokens, w_up, w_down, w_embed.T)
    got = exchange(feat.reshape(GRP, -1, D2), GRP_AXES)
    got = got.reshape(GRP, OWN, PATCH // GRP, D2)
    *kept, part = region_forward(
        idx, region_slide, got, tissue, w_query, w_key, w_value, w_out, att_v, att_u, att_row
    )
    z = add_up(exchange(part, XYC))
    z = exchange(spread(z, 8), Z)
    df, rest, logits, g_class = region_backward(
        idx, region_slide, z, tissue,
        (w_query, w_key, w_value, w_out, att_v, att_u, att_row, w_class.T, g_logits), kept,
    )
    back = exchange(df.reshape(GRP, -1, D2), GRP_AXES).reshape(-1, D2)
    mine, other = patch_backward(idx, back, tokens, mid, hid, gp, w_embed.T, w_down, rest)
    half = add_pair(mine, swap_cores(other))
    chunk = add_up(exchange(half.reshape(PEERS, -1, 128), ZLXY))
    chunk = add_over_zh(chunk)
    half = exchange(spread(chunk, PEERS), ZLXY).reshape(HALF_ROWS, 128)
    other = swap_cores(half)
    grads = unpack(idx, other, 4, unpack(idx, half, 3))
    up, down, embed, query, key, value, out, gv, gu, gw = grads
    return (
        logits, up, down, embed.T, query, key, value, out, gv, gu, gw.reshape(D2), g_class.T,
    )


def solution(mesh):
    fine = Mesh(mesh.devices.reshape(2, 4, 2, 4, 4), GRP_AXES + DEV_AXES)
    placed = (P(DEV_AXES, GRP_AXES, None),) + (P(),) * 14
    return jax.shard_map(
        body,
        mesh=fine,
        in_specs=placed,
        out_specs=(P(),) * 12,
        check_vma=False,
    )
```

```python
import math

import jax
import jax.numpy as jnp
from jax import lax
from jax.experimental import pallas as pl
from jax.experimental.pallas import tpu as pltpu
from jax.sharding import Mesh, PartitionSpec as P

D1 = 384
F1 = 1536
HEADS = 6
HEAD_DIM = 32
D2 = 192
PATCH = 256
SLIDES = 4
GRP = 16
OWN = 2
SCALE = 1.0 / math.sqrt(HEAD_DIM)
GELU_C = math.sqrt(2.0 / math.pi)
GELU_A = 0.044715

BF = jnp.bfloat16
F32 = jnp.float32
HIGHEST = lax.Precision.HIGHEST
MIB = 1024 * 1024

HALF_ROWS = 6144
DOWN_AT = 2304
REST_AT = 4608
REST_ROWS = 1152
EMBED_AT = REST_AT + REST_ROWS
PAD_AT = EMBED_AT + 288
PEERS = 32


def nn(a, b, precision=None):
    return jnp.dot(a, b, precision=precision, preferred_element_type=F32)


def nt(a, b, precision=None):
    return lax.dot_general(
        a, b, (((1,), (1,)), ((), ())), precision=precision, preferred_element_type=F32
    )


def tn(a, b, precision=None):
    return lax.dot_general(
        a, b, (((0,), (0,)), ((), ())), precision=precision, preferred_element_type=F32
    )


def params(mib=32):
    return pltpu.CompilerParams(vmem_limit_bytes=mib * MIB)


def fetch_all(srcs, dsts, sems):
    copies = [
        pltpu.make_async_copy(src, dst, sems.at[i]) for i, (src, dst) in enumerate(zip(srcs, dsts))
    ]
    for copy in copies:
        copy.start()
    for copy in copies:
        copy.wait()


def weight_scratch():
    return [pltpu.VMEM((D2, D2), BF)] * 4 + [pltpu.VMEM((D2, D2), F32)] * 2 + [
        pltpu.SemaphoreType.DMA((6,))
    ]


def patch_forward_kernel(x_ref, wu_ref, wd_ref, we_ref, feat_ref, hid_ref, gp_ref, mid_ref, acc):
    step = pl.program_id(0)
    x = x_ref[...]
    pre = nn(x, wu_ref[...])
    sq = pre * pre
    t = jnp.tanh(GELU_C * (pre + GELU_A * (pre * sq)))
    half_up = 0.5 + 0.5 * t
    hid = (pre * half_up).astype(BF)
    hid_ref[...] = hid
    slope = (0.5 * GELU_C) * (1.0 - t * t) * (1.0 + (3.0 * GELU_A) * sq)
    gp_ref[...] = (half_up + pre * slope).astype(BF)
    part = nn(hid, wd_ref[...])

    @pl.when(step == 0)
    def _():
        acc[...] = x.astype(F32) + part

    @pl.when(step > 0)
    def _():
        acc[...] += part

    @pl.when(step == pl.num_programs(0) - 1)
    def _():
        mid = acc[...].astype(BF)
        mid_ref[...] = mid
        feat_ref[...] = nt(mid, we_ref[...]).astype(BF)


def patch_forward(tokens, w_up, w_down, w_embed):
    rows = tokens.shape[0]
    steps = 3
    fb = F1 // steps
    whole = lambda i: (0, 0)
    return pl.pallas_call(
        patch_forward_kernel,
        grid=(steps,),
        in_specs=[
            pl.BlockSpec((rows, D1), whole),
            pl.BlockSpec((D1, fb), lambda i: (0, i)),
            pl.BlockSpec((fb, D1), lambda i: (i, 0)),
            pl.BlockSpec((D2, D1), whole),
        ],
        out_specs=[
            pl.BlockSpec((rows, D2), whole),
            pl.BlockSpec((rows, fb), lambda i: (0, i)),
            pl.BlockSpec((rows, fb), lambda i: (0, i)),
            pl.BlockSpec((rows, D1), whole),
        ],
        out_shape=[
            jax.ShapeDtypeStruct((rows, D2), BF),
            jax.ShapeDtypeStruct((rows, F1), BF),
            jax.ShapeDtypeStruct((rows, F1), BF),
            jax.ShapeDtypeStruct((rows, D1), BF),
        ],
        scratch_shapes=[pltpu.VMEM((rows, D1), F32)],
        compiler_params=params(60),
        name="patch_forward",
    )(tokens, w_up, w_down, w_embed)


def tissue_row(idx_ref, tis_ref, r):
    return tis_ref[pl.ds(idx_ref[1] + r, 1), :].astype(F32)


def column_of(row, width):
    return jnp.broadcast_to(row, (PATCH, row.shape[1])).T[:, :width]


def head_mask(h, shape, dim):
    return (lax.broadcasted_iota(jnp.int32, shape, dim) // HEAD_DIM == h).astype(F32)


def region_forward_kernel(
    idx_ref, slide_ref, f_ref, tis_ref, wq_in, wk_in, wv_in, wo_in, av_in, au_in, aw_ref,
    p_ref, x_ref, q_ref, k_ref, v_ref, se_ref, asum_ref, reg_ref, tanh_ref, gate_ref, w_ref,
    part_ref,
    wq_ref, wk_ref, wv_ref, wo_ref, av_ref, au_ref, wsems,
):
    r = pl.program_id(0)

    @pl.when(r == 0)
    def _():
        fetch_all(
            (wq_in, wk_in, wv_in, wo_in, av_in, au_in),
            (wq_ref, wk_ref, wv_ref, wo_ref, av_ref, au_ref),
            wsems,
        )

    trow = tissue_row(idx_ref, tis_ref, r)
    tcol = column_of(trow, D2)
    x = (f_ref[...].reshape(PATCH, D2).astype(F32) * tcol).astype(BF)
    x_ref[0] = x
    q = nn(x, wq_ref[...]).astype(BF)
    k = nn(x, wk_ref[...])
    v = nn(x, wv_ref[...]).astype(BF)
    q_ref[0] = q
    k_ref[0] = k.astype(BF)
    v_ref[0] = v
    spread = jnp.zeros((PATCH, D2), F32)
    for h in range(HEADS):
        mask = head_mask(h, (1, D2), 1)
        st = nt((k * mask).astype(BF), q) * SCALE
        top = jnp.max(st, axis=0, keepdims=True)
        ex = jnp.exp(st - top)
        total = jnp.sum(ex, axis=0, keepdims=True)
        pb = (ex * (1.0 / total)).astype(BF)
        p_ref[0, pl.ds(h * PATCH, PATCH), :] = pb
        spread = spread + nn(pb, (tcol * mask).astype(BF))
    se_ref[0] = spread
    asum = jnp.sum(spread * v.astype(F32), axis=0, keepdims=True)
    xsum = jnp.sum(x.astype(F32), axis=0, keepdims=True)
    count = jnp.maximum(jnp.sum(trow, axis=1, keepdims=True), 1.0)
    mixed = xsum + nn(jnp.broadcast_to(asum, (8, D2)), wo_ref[...].astype(F32), HIGHEST)[0:1]

    @pl.when(r == 0)
    def _():
        lane = lax.broadcasted_iota(jnp.int32, (8, PATCH), 1)
        reg_ref[...] = jnp.where(lane < D2, 0.0, 1.0)
        asum_ref[...] = jnp.zeros_like(asum_ref)

    asum_ref[pl.ds(r, 1), :] = asum
    reg_ref[pl.ds(r, 1), pl.ds(0, D2)] = mixed / count

    @pl.when(r == OWN - 1)
    def _():
        region = reg_ref[:, pl.ds(0, D2)]
        tanh_part = jnp.tanh(nn(region, av_ref[...], HIGHEST))
        gate_part = jax.nn.sigmoid(nn(region, au_ref[...], HIGHEST))
        tanh_ref[...] = tanh_part
        gate_ref[...] = gate_part
        score = jnp.sum(tanh_part * gate_part * aw_ref[...], axis=1, keepdims=True)
        weight = jnp.exp(score)
        w_ref[...] = jnp.broadcast_to(weight, w_ref.shape)
        wide = reg_ref[...] * weight
        slot = lax.broadcasted_iota(jnp.int32, (SLIDES, 1), 0)
        sums = jnp.zeros((SLIDES, PATCH), F32)
        for i in range(OWN):
            own = (slot == slide_ref[idx_ref[0] + i]).astype(F32)
            sums = sums + own * wide[i : i + 1]
        both = jnp.concatenate([sums[:, :128], sums[:, 128:]], axis=0)
        part_ref[...] = jnp.broadcast_to(both[None], part_ref.shape)


def region_forward(idx, slide, got, tissue, w_query, w_key, w_value, w_out, att_v, att_u, att_w):
    sq = pl.BlockSpec(memory_space=pltpu.HBM)
    row8 = lambda width: pl.BlockSpec((8, width), lambda r, *_: (0, 0))
    per_region = lambda rows, width: pl.BlockSpec((1, rows, width), lambda r, *_: (r, 0, 0))
    tok = lambda dt: jax.ShapeDtypeStruct((OWN, PATCH, D2), dt)
    return pl.pallas_call(
        region_forward_kernel,
        grid_spec=pltpu.PrefetchScalarGridSpec(
            num_scalar_prefetch=2,
            grid=(OWN,),
            in_specs=[
                pl.BlockSpec((GRP, 1, PATCH // GRP, D2), lambda r, *_: (0, r, 0, 0)),
                pl.BlockSpec((8, PATCH), lambda r, idx, _: (idx[2], 0)),
                sq, sq, sq, sq, sq, sq,
                pl.BlockSpec((1, D2), lambda r, *_: (0, 0)),
            ],
            out_specs=[
                per_region(HEADS * PATCH, PATCH),
                per_region(PATCH, D2),
                per_region(PATCH, D2),
                per_region(PATCH, D2),
                per_region(PATCH, D2),
                per_region(PATCH, D2),
                row8(D2),
                row8(PATCH),
                row8(D2),
                row8(D2),
                row8(128),
                pl.BlockSpec((GRP, 8, 128), lambda r, *_: (0, 0, 0)),
            ],
            scratch_shapes=weight_scratch(),
        ),
        out_shape=[
            jax.ShapeDtypeStruct((OWN, HEADS * PATCH, PATCH), BF),
            tok(BF), tok(BF), tok(BF), tok(BF), tok(F32),
            jax.ShapeDtypeStruct((8, D2), F32),
            jax.ShapeDtypeStruct((8, PATCH), F32),
            jax.ShapeDtypeStruct((8, D2), F32),
            jax.ShapeDtypeStruct((8, D2), F32),
            jax.ShapeDtypeStruct((8, 128), F32),
            jax.ShapeDtypeStruct((GRP, 8, 128), F32),
        ],
        compiler_params=params(60),
        name="region_forward",
    )(idx, slide, got, tissue, w_query, w_key, w_value, w_out, att_v, att_u, att_w)


def region_backward_kernel(
    idx_ref, slide_ref, tis_ref, wq_in, wk_in, wv_in, wo_in, av_in, au_in, aw_ref,
    wc_ref, gl_ref,
    p_ref, x_ref, q_ref, k_ref, v_ref, se_ref, asum_ref, reg_ref, tanh_ref, gate_ref, w_ref,
    df_ref, grad_ref, rows_ref,
    da_s, kt_s, dqt_s,
    wq_ref, wk_ref, wv_ref, wo_ref, av_ref, au_ref, wsems,
):
    r = pl.program_id(0)
    trow = tissue_row(idx_ref, tis_ref, r)
    tcol = column_of(trow, D2)

    @pl.when(r == 0)
    def _():
        fetch_all(
            (wq_in, wk_in, wv_in, wo_in, av_in, au_in),
            (wq_ref, wk_ref, wv_ref, wo_ref, av_ref, au_ref),
            wsems,
        )
        d_summary = nn(gl_ref[...], wc_ref[...], HIGHEST)
        slot = lax.broadcasted_iota(jnp.int32, (SLIDES, 1), 0)
        row = lax.broadcasted_iota(jnp.int32, (8, 1), 0)
        d_own = jnp.zeros((8, D2), F32)
        count = jnp.ones((8, 1), F32)
        for i in range(OWN):
            mine = slot == slide_ref[idx_ref[0] + i]
            d_own = jnp.where(
                row == i, jnp.sum(jnp.where(mine, d_summary, 0.0), axis=0, keepdims=True), d_own
            )
            t_i = tissue_row(idx_ref, tis_ref, i)
            count = jnp.where(
                row == i, jnp.maximum(jnp.sum(t_i, axis=1, keepdims=True), 1.0), count
            )
        region = reg_ref[:, pl.ds(0, D2)]
        tanh_part = tanh_ref[...]
        gate_part = gate_ref[...]
        pre_v = aw_ref[...] * gate_part * (1.0 - tanh_part * tanh_part)
        pre_u = aw_ref[...] * tanh_part * gate_part * (1.0 - gate_part)
        second = nt(pre_v, av_ref[...], HIGHEST) + nt(pre_u, au_ref[...], HIGHEST)
        own = jnp.sum(d_own * region, axis=1, keepdims=True)
        dm = (d_own / count, second / count)
        kept = (
            region, asum_ref[...], tanh_part * gate_part, pre_v, pre_u, dm[0], dm[1],
            jnp.broadcast_to(w_ref[:, 0:1], (8, D2)), jnp.broadcast_to(own, (8, D2)),
        )
        for i, value in enumerate(kept):
            rows_ref[pl.ds(8 * i, 8), :] = value
        for j in range(2):
            da_s[pl.ds(8 * j, 8), :] = nt(dm[j].astype(BF), wo_ref[...])

    x = x_ref[0]
    q = q_ref[0].astype(F32)
    v = v_ref[0]
    kt_s[...] = k_ref[0].astype(F32).T.astype(BF)
    dm = [rows_ref[pl.ds(8 * (5 + j) + r, 1), :] for j in range(2)]
    da = [da_s[pl.ds(8 * j + r, 1), :].astype(BF).astype(F32) for j in range(2)]
    da_col = jnp.concatenate([jnp.broadcast_to(d, (128, D2)) for d in da], axis=0).T
    dk = [jnp.zeros((PATCH, D2), F32) for _ in range(2)]
    for h in range(HEADS):
        e = nn(v, (da_col * head_mask(h, (D2, 1), 0)).astype(BF))
        pt = p_ref[0, pl.ds(h * PATCH, PATCH), :].astype(F32)
        q_head = (q * head_mask(h, (1, D2), 1)).astype(BF)
        k_head = kt_s[pl.ds(h * HEAD_DIM, HEAD_DIM), :]
        for j in range(2):
            e_j = e[:, 128 * j : 128 * j + 128]
            pe = pt * jnp.concatenate([e_j, e_j], axis=1)
            ds = (pe - pt * jnp.sum(pe, axis=0, keepdims=True)).astype(BF)
            dk[j] = dk[j] + nn(ds, q_head)
            dqt_s[j, pl.ds(h * HEAD_DIM, HEAD_DIM), :] = nn(k_head, ds)
    xt = x.astype(F32).T.astype(BF)
    for j in range(2):
        dq = (dqt_s[j] * (trow * SCALE)).T.astype(BF)
        dk_j = (dk[j] * SCALE).astype(BF)
        dv = (se_ref[0] * da[j]).astype(BF)
        grad_ref[0, 0, j] = nn(xt, dq)
        grad_ref[0, 1, j] = nn(xt, dk_j)
        grad_ref[0, 2, j] = nn(xt, dv)
        d_flat = dm[j] + nt(dq, wq_ref[...]) + nt(dk_j, wk_ref[...]) + nt(dv, wv_ref[...])
        d_flat = (tcol * d_flat).astype(BF).reshape(GRP, PATCH // GRP, D2)
        df_ref[:, j, :, pl.ds(0, D2)] = d_flat
        df_ref[:, j, :, pl.ds(D2, 64)] = jnp.zeros((GRP, PATCH // GRP, 64), BF)


BLOCKS = 2 * OWN + 1


def region_backward(idx, slide, tissue, weights, kept):
    sq = pl.BlockSpec(memory_space=pltpu.HBM)
    whole = lambda rows, width: pl.BlockSpec((rows, width), lambda r, *_: (0, 0))
    per_region = lambda rows, width: pl.BlockSpec((1, rows, width), lambda r, *_: (r, 0, 0))
    return pl.pallas_call(
        region_backward_kernel,
        grid_spec=pltpu.PrefetchScalarGridSpec(
            num_scalar_prefetch=2,
            grid=(OWN,),
            in_specs=[
                pl.BlockSpec((8, PATCH), lambda r, idx, _: (idx[2], 0)),
                sq, sq, sq, sq, sq, sq,
                whole(1, D2),
                whole(3, D2),
                whole(SLIDES, 3),
                per_region(HEADS * PATCH, PATCH),
                per_region(PATCH, D2),
                per_region(PATCH, D2),
                per_region(PATCH, D2),
                per_region(PATCH, D2),
                per_region(PATCH, D2),
                whole(8, D2),
                whole(8, PATCH),
                whole(8, D2),
                whole(8, D2),
                whole(8, 128),
            ],
            out_specs=[
                pl.BlockSpec((GRP, 2, PATCH // GRP, PATCH), lambda r, *_: (0, r, 0, 0)),
                pl.BlockSpec((1, 3, 2, D2, D2), lambda r, *_: (r, 0, 0, 0, 0)),
                whole(72, D2),
            ],
            scratch_shapes=[
                pltpu.VMEM((16, D2), F32),
                pltpu.VMEM((D2, PATCH), BF),
                pltpu.VMEM((2, D2, PATCH), F32),
            ] + weight_scratch(),
        ),
        out_shape=[
            jax.ShapeDtypeStruct((GRP, BLOCKS, PATCH // GRP, PATCH), BF),
            jax.ShapeDtypeStruct((OWN, 3, 2, D2, D2), F32),
            jax.ShapeDtypeStruct((72, D2), F32),
        ],
        compiler_params=params(60),
        cost_estimate=pl.CostEstimate(
            flops=4_000_000_000, bytes_accessed=20_000_000, transcendentals=0
        ),
        name="region_backward",
    )(idx, slide, tissue, *weights, *kept)


def split_three(x):
    parts = []
    for _ in range(3):
        top = x.astype(BF).astype(F32)
        parts.append(top)
        x = x - top
    return parts


def join_sums_kernel(z_ref, rows_ref, df_ref, out_ref, ext, wide, sem):
    z = jnp.sum(z_ref[...], axis=0)
    z = jnp.concatenate([z[0:SLIDES], z[SLIDES:]], axis=1)
    lane = lax.broadcasted_iota(jnp.int32, (1, PATCH), 1) // 64
    scalars = jnp.zeros((1, PATCH), F32)
    for i in range(OWN):
        scalars = jnp.where(lane == 2 * i, rows_ref[56 + i : 57 + i, 0:1], scalars)
        scalars = jnp.where(lane == 2 * i + 1, rows_ref[64 + i : 65 + i, 0:1], scalars)
    ext[...] = jnp.zeros_like(ext)
    for i, (part, tops) in enumerate(zip(split_three(z), split_three(scalars))):
        ext[pl.ds(4 * i, 4), :] = part
        ext[pl.ds(12 + i, 1), :] = tops
    wide[...] = jnp.broadcast_to(ext[...].astype(BF)[None], wide.shape)
    copy = pltpu.make_async_copy(wide, out_ref.at[:, BLOCKS - 1], sem)
    copy.start()
    copy.wait()


def join_sums(z, rows, df):
    return pl.pallas_call(
        join_sums_kernel,
        in_specs=[
            pl.BlockSpec(memory_space=pltpu.VMEM),
            pl.BlockSpec(memory_space=pltpu.VMEM),
            pl.BlockSpec(memory_space=pl.ANY),
        ],
        out_specs=pl.BlockSpec(memory_space=pl.ANY),
        out_shape=jax.ShapeDtypeStruct(df.shape, df.dtype),
        scratch_shapes=[
            pltpu.VMEM((16, PATCH), F32),
            pltpu.VMEM((GRP, 16, PATCH), BF),
            pltpu.SemaphoreType.DMA,
        ],
        input_output_aliases={2: 0},
        compiler_params=params(16),
        name="join_sums",
    )(z, rows, df)


STEPS4 = 4
FB4 = F1 // STEPS4


def put_rest(pack, slot, grad, fill=None):
    at = REST_AT + 192 * slot
    if not isinstance(slot, int):
        at = pl.multiple_of(at, 64)
    for half in range(2):
        rows = grad[96 * half : 96 * half + 96]
        pack[half, pl.ds(at, 96), :] = rows[:, :128].astype(BF)
        tail = jnp.zeros((96, 64), F32) if fill is None else fill
        high = jnp.concatenate([rows[:, 128:], tail], axis=1)
        pack[half, pl.ds(at + 96, 96), :] = high.astype(BF)


def finish_slides(
    idx_ref, slide_ref, back_ref, rows_ref, wc_ref, gl_ref, logits_ref, gc_ref, df_s, pq_s, pack
):
    ext = back_ref[:, BLOCKS - 1].astype(F32)
    sums = jnp.sum(ext, axis=0)
    sums = sums[0:4] + sums[4:8] + sums[8:12]
    total = sums[:, D2 : D2 + 1]
    summary = sums[:, :D2] / total
    wc = wc_ref[...]
    gl = gl_ref[...]
    logits_ref[...] = nt(summary, wc, HIGHEST)
    gc_ref[...] = tn(gl, summary, HIGHEST)
    along = jnp.sum(nn(gl, wc, HIGHEST) * summary, axis=1, keepdims=True)

    def of_slide(column, s):
        out = column[SLIDES - 1 : SLIDES]
        for i in range(SLIDES - 1):
            out = jnp.where(s == i, column[i : i + 1], out)
        return out

    def factors(w, a, s):
        share = w / of_slide(total, s)
        return share, share * (a - of_slide(along, s))

    for src in range(GRP):
        scalars = ext[src, 12:13] + ext[src, 13:14] + ext[src, 14:15]
        for i in range(OWN):
            w = scalars[:, 128 * i : 128 * i + 1]
            a = scalars[:, 128 * i + 64 : 128 * i + 65]
            p, q = factors(w, a, slide_ref[idx_ref[5] + OWN * src + i])
            f = [back_ref[src, 2 * i + j].astype(F32)[:, :D2] for j in range(2)]
            df_s[pl.ds(32 * src + 16 * i, 16), :] = (p * f[0] + q * f[1]).astype(BF)

    kept = [rows_ref[pl.ds(8 * i, 8), :] for i in range(9)]
    region, asum, gated, pre_v, pre_u, dm0, dm1, w_own, a_own = kept
    row = lax.broadcasted_iota(jnp.int32, (8, 1), 0)
    p_own = jnp.zeros((8, 1), F32)
    q_own = jnp.zeros((8, 1), F32)
    for i in range(OWN):
        p, q = factors(w_own[i : i + 1, 0:1], a_own[i : i + 1, 0:1], slide_ref[idx_ref[0] + i])
        p_own = jnp.where(row == i, p, p_own)
        q_own = jnp.where(row == i, q, q_own)
    pq_s[0] = jnp.broadcast_to(p_own, (8, 128))
    pq_s[1] = jnp.broadcast_to(q_own, (8, 128))
    put_rest(pack, 3, tn(asum, p_own * dm0 + q_own * dm1, HIGHEST))
    put_rest(pack, 4, tn(region, q_own * pre_v, HIGHEST))
    g_aw = tn(gated, jnp.broadcast_to(q_own, (8, 64)), HIGHEST)
    lane = lax.broadcasted_iota(jnp.int32, (96, 64), 1)
    put_rest(
        pack, 5, tn(region, q_own * pre_u, HIGHEST), jnp.where(lane == 0, g_aw[:96], g_aw[96:])
    )


def patch_backward_kernel(
    idx_ref, slide_ref, back_ref, x_ref, mid_ref, hid_ref, gp_ref, we_ref, wd_ref, grad_ref,
    rows_ref, wc_ref, gl_ref,
    mine_ref, other_ref, logits_ref, gc_ref,
    pack, dmid_s, df_s, pq_s, sems,
):
    step = pl.program_id(0)
    core = idx_ref[3]

    def up_copies(i):
        rows = pl.ds(pl.multiple_of(576 * i, 64), 576)
        return (
            pltpu.make_async_copy(pack.at[core, rows], mine_ref.at[rows], sems.at[2 * i]),
            pltpu.make_async_copy(pack.at[1 - core, rows], other_ref.at[rows], sems.at[2 * i + 1]),
        )

    def down_copy(i, dst):
        rows = pl.ds(pl.multiple_of(DOWN_AT + 1152 * lax.rem(i, 2), 128), 1152)
        return pltpu.make_async_copy(pack.at[i // 2, rows], dst.at[rows], sems.at[8 + i])

    def rest_copies():
        rows = pl.ds(REST_AT, HALF_ROWS - REST_AT)
        return (
            pltpu.make_async_copy(pack.at[core, rows], mine_ref.at[rows], sems.at[12]),
            pltpu.make_async_copy(pack.at[1 - core, rows], other_ref.at[rows], sems.at[13]),
        )

    @pl.when(step == 0)
    def _():
        finish_slides(
            idx_ref, slide_ref, back_ref, rows_ref, wc_ref, gl_ref, logits_ref, gc_ref,
            df_s, pq_s, pack,
        )
        df = df_s[...]
        dmid_s[...] = nn(df, we_ref[...]).astype(BF)
        g_embed = tn(df, mid_ref[...]).astype(BF)
        for half in range(2):
            for l in range(3):
                block = g_embed[96 * half : 96 * half + 96, 128 * l : 128 * l + 128]
                pack[half, pl.ds(EMBED_AT + 96 * l, 96), :] = block
            pack[half, pl.ds(PAD_AT, 96), :] = jnp.zeros((96, 128), BF)

    @pl.when(step > 0)
    def _():
        grad = jnp.zeros((D2, D2), F32)
        for i in range(OWN):
            for j in range(2):
                grad = grad + pq_s[j, i : i + 1, 0:1] * grad_ref[i, 0, j]
        put_rest(pack, step - 1, grad)

    dmid = dmid_s[...]
    d_pre = (nt(dmid, wd_ref[...]) * gp_ref[...].astype(F32)).astype(BF)
    g_up = tn(x_ref[...], d_pre).astype(BF)
    for half in range(2):
        for l in range(3):
            block = g_up[192 * half : 192 * half + 192, 128 * l : 128 * l + 128]
            pack[half, pl.ds(pl.multiple_of(576 * step + 192 * l, 64), 192), :] = block
    g_down = tn(hid_ref[...], dmid).astype(BF)
    at = DOWN_AT + 1152 * lax.rem(step, 2)
    for l in range(3):
        rows = pl.ds(pl.multiple_of(at + 384 * l, 128), 384)
        pack[step // 2, rows, :] = g_down[:, 128 * l : 128 * l + 128]

    for copy in up_copies(step):
        copy.start()

    @pl.when(step // 2 == core)
    def _():
        down_copy(step, mine_ref).start()

    @pl.when(step // 2 != core)
    def _():
        down_copy(step, other_ref).start()

    @pl.when(step == pl.num_programs(0) - 1)
    def _():
        for copy in rest_copies():
            copy.start()
        for copy in rest_copies():
            copy.wait()
        for i in range(STEPS4):
            for copy in up_copies(i):
                copy.wait()
            down_copy(i, mine_ref).wait()


def patch_backward(
    idx, slide, back, tokens, mid, hid, gp, w_embed, w_down, grad, kept_rows, w_class, g_logits
):
    rows = tokens.shape[0]
    whole = lambda i, *_: (0, 0)
    return pl.pallas_call(
        patch_backward_kernel,
        grid_spec=pltpu.PrefetchScalarGridSpec(
            num_scalar_prefetch=2,
            grid=(STEPS4,),
            in_specs=[
                pl.BlockSpec(back.shape, lambda i, *_: (0, 0, 0, 0)),
                pl.BlockSpec((rows, D1), whole),
                pl.BlockSpec((rows, D1), whole),
                pl.BlockSpec((rows, FB4), lambda i, *_: (0, i)),
                pl.BlockSpec((rows, FB4), lambda i, *_: (0, i)),
                pl.BlockSpec((D2, D1), whole),
                pl.BlockSpec((FB4, D1), lambda i, *_: (i, 0)),
                pl.BlockSpec(
                    (OWN, 1, 2, D2, D2), lambda i, *_: (0, jnp.maximum(i - 1, 0), 0, 0, 0)
                ),
                pl.BlockSpec((72, D2), whole),
                pl.BlockSpec((3, D2), whole),
                pl.BlockSpec((SLIDES, 3), whole),
            ],
            out_specs=[
                pl.BlockSpec(memory_space=pl.ANY),
                pl.BlockSpec(memory_space=pl.ANY),
                pl.BlockSpec((SLIDES, 3), whole),
                pl.BlockSpec((3, D2), whole),
            ],
            scratch_shapes=[
                pltpu.VMEM((2, HALF_ROWS, 128), BF),
                pltpu.VMEM((rows, D1), BF),
                pltpu.VMEM((rows, D2), BF),
                pltpu.VMEM((2, 8, 128), F32),
                pltpu.SemaphoreType.DMA((14,)),
            ],
        ),
        out_shape=[
            jax.ShapeDtypeStruct((HALF_ROWS, 128), BF),
            jax.ShapeDtypeStruct((HALF_ROWS, 128), BF),
            jax.ShapeDtypeStruct((SLIDES, 3), F32),
            jax.ShapeDtypeStruct((3, D2), F32),
        ],
        compiler_params=params(44),
        name="patch_backward",
    )(
        idx, slide, back, tokens, mid, hid, gp, w_embed, w_down, grad, kept_rows, w_class,
        g_logits,
    )


def unpack_kernel(idx_ref, src_ref, *refs):
    up_ref, down_ref, embed_ref, q_ref, k_ref, v_ref, o_ref, av_ref, au_ref, aw_ref = refs[-10:]
    for l in range(12):
        up_ref[:, pl.ds(128 * l, 128)] = src_ref[pl.ds(192 * l, 192), :].astype(F32)
    for i in range(2):
        for l in range(3):
            rows = src_ref[pl.ds(DOWN_AT + 1152 * i + 384 * l, 384), :]
            down_ref[pl.ds(384 * i, 384), pl.ds(128 * l, 128)] = rows.astype(F32)
    for slot, ref in enumerate((q_ref, k_ref, v_ref, o_ref, av_ref, au_ref)):
        at = REST_AT + 192 * slot
        ref[:, pl.ds(0, 128)] = src_ref[pl.ds(at, 96), :].astype(F32)
        ref[:, pl.ds(128, 64)] = src_ref[pl.ds(at + 96, 96), :][:, :64].astype(F32)
    for l in range(3):
        embed_ref[:, pl.ds(128 * l, 128)] = src_ref[pl.ds(EMBED_AT + 96 * l, 96), :].astype(F32)
    tail = src_ref[pl.ds(EMBED_AT - 96, 96), :].astype(F32).T
    aw_ref[:, pl.ds(0, 96)] = tail[64:65, :]
    aw_ref[:, pl.ds(96, 96)] = tail[65:66, :]


def unpack(idx, src, which, earlier=()):
    square = jax.ShapeDtypeStruct((D2, D2), F32)
    half = lambda rows, width: pl.BlockSpec((rows, width), lambda i, idx: (idx[which], 0))
    hbm = pl.BlockSpec(memory_space=pltpu.HBM)
    return pl.pallas_call(
        unpack_kernel,
        grid_spec=pltpu.PrefetchScalarGridSpec(
            num_scalar_prefetch=1,
            grid=(1,),
            in_specs=[pl.BlockSpec((HALF_ROWS, 128), lambda i, idx: (0, 0))] + [hbm] * len(earlier),
            out_specs=[
                half(D1 // 2, F1),
                half(F1 // 2, D1),
                half(D2 // 2, D1),
            ]
            + [half(D2 // 2, D2)] * 6
            + [pl.BlockSpec((1, D2), lambda i, idx: (0, 0))],
        ),
        out_shape=[
            jax.ShapeDtypeStruct((D1, F1), F32),
            jax.ShapeDtypeStruct((F1, D1), F32),
            jax.ShapeDtypeStruct((D2, D1), F32),
            square, square, square, square, square, square,
            jax.ShapeDtypeStruct((1, D2), F32),
        ],
        input_output_aliases={2 + i: i for i in range(len(earlier))},
        compiler_params=params(),
        name="unpack",
    )(idx, src, *earlier)


GRP_AXES = ("zl", "x", "c")
DEV_AXES = ("zh", "y")
ZLXY = ("y", "zl", "x")


def exchange(x, axes):
    return lax.all_to_all(x, axes, split_axis=0, concat_axis=0, tiled=True)


def swap_cores(x):
    return lax.ppermute(x, "c", [(0, 1), (1, 0)])


def spread(x, n):
    return jnp.broadcast_to(x[None], (n,) + x.shape)


def add_pair(x, y):
    return (x.astype(F32) + y.astype(F32)).astype(x.dtype)


def add_over_zh(x):
    for flip in (1, 3):
        x = add_pair(x, lax.ppermute(x, "zh", [(i, i ^ flip) for i in range(4)]))
    return x


def add_up(x):
    return jnp.sum(x.astype(F32), axis=0).astype(x.dtype)


def body(
    patches, tissue, region_slide, w_up, w_down, w_embed, w_query, w_key, w_value, w_out,
    att_v, att_u, att_w, w_class, g_logits,
):
    grp = lax.axis_index(GRP_AXES)
    dev = lax.axis_index(DEV_AXES)
    core = lax.axis_index("c")
    first = (dev * GRP + grp) * OWN
    idx = jnp.stack([first, first % 8, first // 8, core, 1 - core, dev * GRP * OWN]).astype(jnp.int32)
    tokens = patches.reshape(-1, D1)
    att_row = att_w.reshape(1, D2)
    feat, hid, gp, mid = patch_forward(tokens, w_up, w_down, w_embed.T)
    got = exchange(feat.reshape(GRP, -1, D2), GRP_AXES)
    got = got.reshape(GRP, OWN, PATCH // GRP, D2)
    *kept, part = region_forward(
        idx, region_slide, got, tissue, w_query, w_key, w_value, w_out, att_v, att_u, att_row
    )
    z = exchange(part, DEV_AXES)
    class_rows = w_class.T
    df, grad, rows = region_backward(
        idx, region_slide, tissue,
        (w_query, w_key, w_value, w_out, att_v, att_u, att_row, class_rows, g_logits), kept,
    )
    df = join_sums(z, rows, df)
    back = exchange(df.reshape(GRP, -1, PATCH), GRP_AXES).reshape(df.shape)
    mine, other, logits, g_class = patch_backward(
        idx, region_slide, back, tokens, mid, hid, gp, w_embed.T, w_down, grad, rows, class_rows,
        g_logits,
    )
    half = add_pair(mine, swap_cores(other))
    chunk = add_up(exchange(half.reshape(PEERS, -1, 128), ZLXY))
    chunk = add_over_zh(chunk)
    half = exchange(spread(chunk, PEERS), ZLXY).reshape(HALF_ROWS, 128)
    other = swap_cores(half)
    grads = unpack(idx, other, 4, unpack(idx, half, 3))
    up, down, embed, query, key, value, out, gv, gu, gw = grads
    return (
        logits, up, down, embed.T, query, key, value, out, gv, gu, gw.reshape(D2), g_class.T,
    )


def solution(mesh):
    fine = Mesh(mesh.devices.reshape(2, 4, 2, 4, 4), GRP_AXES + DEV_AXES)
    placed = (P(DEV_AXES, GRP_AXES, None),) + (P(),) * 14
    return jax.shard_map(
        body,
        mesh=fine,
        in_specs=placed,
        out_specs=(P(),) * 12,
        check_vma=False,
    )
```

```python
import math

import jax
import jax.numpy as jnp
from jax import lax
from jax.experimental import pallas as pl
from jax.experimental.pallas import tpu as pltpu
from jax.sharding import Mesh, PartitionSpec as P

D1 = 384
F1 = 1536
HEADS = 6
HEAD_DIM = 32
D2 = 192
PATCH = 256
SLIDES = 4
GRP = 16
OWN = 2
SCALE = 1.0 / math.sqrt(HEAD_DIM)
GELU_C = math.sqrt(2.0 / math.pi)
GELU_A = 0.044715

BF = jnp.bfloat16
F32 = jnp.float32
HIGHEST = lax.Precision.HIGHEST
MIB = 1024 * 1024

HALF_ROWS = 6144
DOWN_AT = 2304
REST_AT = 4608
REST_ROWS = 1152
EMBED_AT = REST_AT + REST_ROWS
PAD_AT = EMBED_AT + 288
PEERS = 32


def nn(a, b, precision=None):
    return jnp.dot(a, b, precision=precision, preferred_element_type=F32)


def nt(a, b, precision=None):
    return lax.dot_general(
        a, b, (((1,), (1,)), ((), ())), precision=precision, preferred_element_type=F32
    )


def tn(a, b, precision=None):
    return lax.dot_general(
        a, b, (((0,), (0,)), ((), ())), precision=precision, preferred_element_type=F32
    )


def params(mib=32):
    return pltpu.CompilerParams(vmem_limit_bytes=mib * MIB)


def patch_forward_kernel(x_ref, wu_ref, wd_ref, we_ref, feat_ref, mid_ref, acc):
    step = pl.program_id(0)
    x = x_ref[...]
    pre = nn(x, wu_ref[...])
    sq = pre * pre
    t = jnp.tanh(GELU_C * (pre + GELU_A * (pre * sq)))
    part = nn((pre * (0.5 + 0.5 * t)).astype(BF), wd_ref[...])

    @pl.when(step == 0)
    def _():
        acc[...] = x.astype(F32) + part

    @pl.when(step > 0)
    def _():
        acc[...] += part

    @pl.when(step == pl.num_programs(0) - 1)
    def _():
        mid = acc[...].astype(BF)
        mid_ref[...] = mid
        feat_ref[...] = nt(mid, we_ref[...]).astype(BF)


STEPS1 = 4
FB1 = F1 // STEPS1


def patch_forward(tokens, w_up, w_down, w_embed):
    rows = tokens.shape[0]
    whole = lambda i: (0, 0)
    return pl.pallas_call(
        patch_forward_kernel,
        grid=(STEPS1,),
        in_specs=[
            pl.BlockSpec((rows, D1), whole),
            pl.BlockSpec((D1, FB1), lambda i: (0, i)),
            pl.BlockSpec((FB1, D1), lambda i: (i, 0)),
            pl.BlockSpec((D2, D1), whole),
        ],
        out_specs=[
            pl.BlockSpec((rows, D2), whole),
            pl.BlockSpec((rows, D1), whole),
        ],
        out_shape=[
            jax.ShapeDtypeStruct((rows, D2), BF),
            jax.ShapeDtypeStruct((rows, D1), BF),
        ],
        scratch_shapes=[pltpu.VMEM((rows, D1), F32)],
        compiler_params=params(61),
        name="patch_forward",
    )(tokens, w_up, w_down, w_embed)


def patch_slopes_kernel(after_ref, x_ref, wu_ref, hid_ref, gp_ref, xt_ref):
    x = x_ref[...]

    @pl.when(pl.program_id(0) == 0)
    def _():
        xt_ref[...] = x.T

    pre = nn(x, wu_ref[...])
    sq = pre * pre
    t = jnp.tanh(GELU_C * (pre + GELU_A * (pre * sq)))
    half_up = 0.5 + 0.5 * t
    hid_ref[...] = (pre * half_up).astype(BF).T
    slope = (0.5 * GELU_C) * (1.0 - t * t) * (1.0 + (3.0 * GELU_A) * sq)
    gp_ref[...] = (half_up + pre * slope).astype(BF)


def patch_slopes(after, tokens, w_up):
    rows = tokens.shape[0]
    whole = lambda i: (0, 0)
    return pl.pallas_call(
        patch_slopes_kernel,
        grid=(STEPS1,),
        in_specs=[
            pl.BlockSpec(memory_space=pl.ANY),
            pl.BlockSpec((rows, D1), whole),
            pl.BlockSpec((D1, FB1), lambda i: (0, i)),
        ],
        out_specs=[
            pl.BlockSpec((FB1, rows), lambda i: (i, 0)),
            pl.BlockSpec((rows, FB1), lambda i: (0, i)),
            pl.BlockSpec((D1, rows), whole),
        ],
        out_shape=[
            pltpu.HBM((F1, rows), BF),
            pltpu.HBM((rows, F1), BF),
            pltpu.HBM((D1, rows), BF),
        ],
        compiler_params=params(61),
        cost_estimate=pl.CostEstimate(
            flops=3_000_000_000, bytes_accessed=12_000_000, transcendentals=0
        ),
        name="patch_slopes",
    )(after, tokens, w_up)


def gather_weights_kernel(*refs):
    ins, (wp_ref, ap_ref) = refs[:6], refs[6:]
    for i in range(4):
        wp_ref[i] = ins[i][...]
    for i in range(2):
        ap_ref[i] = ins[4 + i][...]


def gather_weights(weights):
    vm = pl.BlockSpec(memory_space=pltpu.VMEM)
    return pl.pallas_call(
        gather_weights_kernel,
        in_specs=[vm] * 6,
        out_specs=[vm] * 2,
        out_shape=[
            jax.ShapeDtypeStruct((4, D2, D2), BF),
            jax.ShapeDtypeStruct((2, D2, D2), F32),
        ],
        compiler_params=params(24),
        cost_estimate=pl.CostEstimate(
            flops=1_000_000_000, bytes_accessed=4_000_000, transcendentals=0
        ),
        name="gather_weights",
    )(*weights)


def tissue_row(idx_ref, tis_ref, r):
    return tis_ref[pl.ds(idx_ref[1] + r, 1), :].astype(F32)


def column_of(row, width):
    return jnp.broadcast_to(row, (PATCH, row.shape[1])).T[:, :width]


def head_mask(h, shape, dim):
    return (lax.broadcasted_iota(jnp.int32, shape, dim) // HEAD_DIM == h).astype(F32)


def region_forward_kernel(
    idx_ref, slide_ref, f_ref, tis_ref, wp_ref, ap_ref, aw_ref,
    p_ref, x_ref, asum_ref, reg_ref, tanh_ref, gate_ref, w_ref,
    part_ref,
):
    r = pl.program_id(0)
    trow = tissue_row(idx_ref, tis_ref, r)
    tcol = column_of(trow, D2)
    x = (f_ref[...].reshape(PATCH, D2).astype(F32) * tcol).astype(BF)
    q = nn(x, wp_ref[0]).astype(BF)
    k = nn(x, wp_ref[1])
    v = nn(x, wp_ref[2]).astype(BF)
    x_ref[0] = x
    spread = jnp.zeros((PATCH, D2), F32)
    for h in range(HEADS):
        mask = head_mask(h, (1, D2), 1)
        st = nt((k * mask).astype(BF), q) * SCALE
        top = jnp.max(st, axis=0, keepdims=True)
        ex = jnp.exp(st - top)
        total = jnp.sum(ex, axis=0, keepdims=True)
        pb = (ex * (1.0 / total)).astype(BF)
        p_ref[0, pl.ds(h * PATCH, PATCH), :] = pb
        spread = spread + nn(pb, (tcol * mask).astype(BF))
    asum = jnp.sum(spread * v.astype(F32), axis=0, keepdims=True)
    xsum = jnp.sum(x.astype(F32), axis=0, keepdims=True)
    count = jnp.maximum(jnp.sum(trow, axis=1, keepdims=True), 1.0)
    mixed = xsum + nn(jnp.broadcast_to(asum, (8, D2)), wp_ref[3].astype(F32), HIGHEST)[0:1]

    @pl.when(r == 0)
    def _():
        lane = lax.broadcasted_iota(jnp.int32, (8, PATCH), 1)
        reg_ref[...] = jnp.where(lane < D2, 0.0, 1.0)
        asum_ref[...] = jnp.zeros_like(asum_ref)

    asum_ref[pl.ds(r, 1), :] = asum
    reg_ref[pl.ds(r, 1), pl.ds(0, D2)] = mixed / count

    @pl.when(r == OWN - 1)
    def _():
        region = reg_ref[:, pl.ds(0, D2)]
        tanh_part = jnp.tanh(nn(region, ap_ref[0], HIGHEST))
        gate_part = jax.nn.sigmoid(nn(region, ap_ref[1], HIGHEST))
        tanh_ref[...] = tanh_part
        gate_ref[...] = gate_part
        score = jnp.sum(tanh_part * gate_part * aw_ref[...], axis=1, keepdims=True)
        weight = jnp.exp(score)
        w_ref[...] = jnp.broadcast_to(weight, w_ref.shape)
        wide = reg_ref[...] * weight
        slot = lax.broadcasted_iota(jnp.int32, (SLIDES, 1), 0)
        sums = jnp.zeros((SLIDES, PATCH), F32)
        for i in range(OWN):
            own = (slot == slide_ref[idx_ref[0] + i]).astype(F32)
            sums = sums + own * wide[i : i + 1]
        both = jnp.concatenate([sums[:, :128], sums[:, 128:]], axis=0)
        part_ref[...] = jnp.broadcast_to(both[None], part_ref.shape)


def packed_specs():
    return [
        pl.BlockSpec((4, D2, D2), lambda r, *_: (0, 0, 0)),
        pl.BlockSpec((2, D2, D2), lambda r, *_: (0, 0, 0)),
    ]


def region_forward(idx, slide, got, tissue, wp, ap, att_w):
    row8 = lambda width: pl.BlockSpec((8, width), lambda r, *_: (0, 0))
    per_region = lambda rows, width: pl.BlockSpec((1, rows, width), lambda r, *_: (r, 0, 0))
    return pl.pallas_call(
        region_forward_kernel,
        grid_spec=pltpu.PrefetchScalarGridSpec(
            num_scalar_prefetch=2,
            grid=(OWN,),
            in_specs=[
                pl.BlockSpec((GRP, 1, PATCH // GRP, D2), lambda r, *_: (0, r, 0, 0)),
                pl.BlockSpec((8, PATCH), lambda r, idx, _: (idx[2], 0)),
                *packed_specs(),
                pl.BlockSpec((1, D2), lambda r, *_: (0, 0)),
            ],
            out_specs=[
                per_region(HEADS * PATCH, PATCH),
                per_region(PATCH, D2),
                row8(D2),
                row8(PATCH),
                row8(D2),
                row8(D2),
                row8(128),
                pl.BlockSpec((GRP, 8, 128), lambda r, *_: (0, 0, 0)),
            ],
        ),
        out_shape=[
            jax.ShapeDtypeStruct((OWN, HEADS * PATCH, PATCH), BF),
            jax.ShapeDtypeStruct((OWN, PATCH, D2), BF),
            jax.ShapeDtypeStruct((8, D2), F32),
            jax.ShapeDtypeStruct((8, PATCH), F32),
            jax.ShapeDtypeStruct((8, D2), F32),
            jax.ShapeDtypeStruct((8, D2), F32),
            jax.ShapeDtypeStruct((8, 128), F32),
            jax.ShapeDtypeStruct((GRP, 8, 128), F32),
        ],
        compiler_params=params(40),
        name="region_forward",
    )(idx, slide, got, tissue, wp, ap, att_w)


def directions(
    idx_ref, slide_ref, tis_ref, wp_ref, ap_ref, aw_ref, wc_ref, gl_ref,
    asum_ref, reg_ref, tanh_ref, gate_ref, w_ref, rows_ref, cols_ref, scal_ref,
):
    d_summary = nn(gl_ref[...], wc_ref[...], HIGHEST)
    slot = lax.broadcasted_iota(jnp.int32, (SLIDES, 1), 0)
    row = lax.broadcasted_iota(jnp.int32, (8, 1), 0)
    d_own = jnp.zeros((8, D2), F32)
    count = jnp.ones((8, 1), F32)
    for i in range(OWN):
        mine = slot == slide_ref[idx_ref[0] + i]
        d_own = jnp.where(
            row == i, jnp.sum(jnp.where(mine, d_summary, 0.0), axis=0, keepdims=True), d_own
        )
        t_i = tissue_row(idx_ref, tis_ref, i)
        count = jnp.where(row == i, jnp.maximum(jnp.sum(t_i, axis=1, keepdims=True), 1.0), count)
    region = reg_ref[:, pl.ds(0, D2)]
    tanh_part = tanh_ref[...]
    gate_part = gate_ref[...]
    pre_v = aw_ref[...] * gate_part * (1.0 - tanh_part * tanh_part)
    pre_u = aw_ref[...] * tanh_part * gate_part * (1.0 - gate_part)
    second = nt(pre_v, ap_ref[0], HIGHEST) + nt(pre_u, ap_ref[1], HIGHEST)
    own = jnp.sum(d_own * region, axis=1, keepdims=True)
    dm = (d_own / count, second / count)
    kept = (
        pre_v, pre_u, dm[0], dm[1],
        jnp.broadcast_to(w_ref[:, 0:1], (8, D2)), jnp.broadcast_to(own, (8, D2)),
        nt(dm[0].astype(BF), wp_ref[3]), nt(dm[1].astype(BF), wp_ref[3]),
    )
    for i, value in enumerate(kept):
        rows_ref[pl.ds(8 * i, 8), :] = value
    turned = jnp.concatenate(
        [region, asum_ref[...], tanh_part * gate_part, jnp.zeros((104, D2), F32)], axis=0
    )
    cols_ref[...] = turned.T
    lane = lax.broadcasted_iota(jnp.int32, (1, PATCH), 1) // 64
    scalars = jnp.zeros((1, PATCH), F32)
    for i in range(OWN):
        scalars = jnp.where(lane == 2 * i, w_ref[i : i + 1, 0:1], scalars)
        scalars = jnp.where(lane == 2 * i + 1, own[i : i + 1], scalars)
    scal_ref[...] = jnp.broadcast_to(scalars, (8, PATCH))


def pull_back(r, idx_ref, tis_ref, wp_ref, p_ref, x_ref, rows_ref, df_ref, grad_ref, kt_s, dqt_s):
    trow = tissue_row(idx_ref, tis_ref, r)
    tcol = column_of(trow, D2)
    x = x_ref[0]
    q = nn(x, wp_ref[0]).astype(BF).astype(F32)
    v = nn(x, wp_ref[2]).astype(BF)
    kt_s[...] = nn(x, wp_ref[1]).T.astype(BF)
    spread = jnp.zeros((PATCH, D2), F32)
    dm = [rows_ref[pl.ds(8 * (2 + j) + r, 1), :] for j in range(2)]
    da = [rows_ref[pl.ds(8 * (6 + j) + r, 1), :].astype(BF).astype(F32) for j in range(2)]
    da_col = jnp.concatenate([jnp.broadcast_to(d, (128, D2)) for d in da], axis=0).T
    dk = [jnp.zeros((PATCH, D2), F32) for _ in range(2)]
    for h in range(HEADS):
        e = nn(v, (da_col * head_mask(h, (D2, 1), 0)).astype(BF))
        pb = p_ref[0, pl.ds(h * PATCH, PATCH), :]
        pt = pb.astype(F32)
        mask = head_mask(h, (1, D2), 1)
        spread = spread + nn(pb, (tcol * mask).astype(BF))
        q_head = (q * mask).astype(BF)
        k_head = kt_s[pl.ds(h * HEAD_DIM, HEAD_DIM), :]
        for j in range(2):
            e_j = e[:, 128 * j : 128 * j + 128]
            pe = pt * jnp.concatenate([e_j, e_j], axis=1)
            ds = (pe - pt * jnp.sum(pe, axis=0, keepdims=True)).astype(BF)
            dk[j] = dk[j] + nn(ds, q_head)
            dqt_s[j, pl.ds(h * HEAD_DIM, HEAD_DIM), :] = nn(k_head, ds)
    xt = x.astype(F32).T.astype(BF)
    for j in range(2):
        dq = (dqt_s[j] * (trow * SCALE)).T.astype(BF)
        dk_j = (dk[j] * SCALE).astype(BF)
        dv = (spread * da[j]).astype(BF)
        grad_ref[0, 0, j] = nn(xt, dq)
        grad_ref[0, 1, j] = nn(xt, dk_j)
        grad_ref[0, 2, j] = nn(xt, dv)
        d_flat = dm[j] + nt(dq, wp_ref[0]) + nt(dk_j, wp_ref[1]) + nt(dv, wp_ref[2])
        d_flat = (tcol * d_flat).astype(BF).reshape(GRP, PATCH // GRP, D2)
        df_ref[:, j, :, pl.ds(0, D2)] = d_flat
        df_ref[:, j, :, pl.ds(D2, 64)] = jnp.zeros((GRP, PATCH // GRP, 64), BF)


BLOCKS = 2 * OWN + 1


def region_backward_kernel(
    idx_ref, slide_ref, tis_ref, wp_ref, ap_ref, aw_ref, wc_ref, gl_ref,
    p_ref, x_ref, asum_ref, reg_ref, tanh_ref, gate_ref, w_ref,
    df_ref, grad_ref, rows_ref, cols_ref, scal_ref,
    kt_s, dqt_s,
):
    r = pl.program_id(0)

    @pl.when(r == 0)
    def _():
        directions(
            idx_ref, slide_ref, tis_ref, wp_ref, ap_ref, aw_ref, wc_ref, gl_ref,
            asum_ref, reg_ref, tanh_ref, gate_ref, w_ref, rows_ref, cols_ref, scal_ref,
        )

    pull_back(
        r, idx_ref, tis_ref, wp_ref, p_ref, x_ref, rows_ref, df_ref, grad_ref, kt_s, dqt_s
    )


def region_backward(idx, slide, tissue, wp, ap, att_w, w_class, g_logits, kept):
    whole = lambda rows, width: pl.BlockSpec((rows, width), lambda r, *_: (0, 0))
    region = lambda rows, width: pl.BlockSpec((1, rows, width), lambda r, *_: (r, 0, 0))
    return pl.pallas_call(
        region_backward_kernel,
        grid_spec=pltpu.PrefetchScalarGridSpec(
            num_scalar_prefetch=2,
            grid=(OWN,),
            in_specs=[
                pl.BlockSpec((8, PATCH), lambda r, idx, _: (idx[2], 0)),
                *packed_specs(),
                whole(1, D2), whole(3, D2), whole(SLIDES, 3),
                region(HEADS * PATCH, PATCH),
                region(PATCH, D2),
                whole(8, D2), whole(8, PATCH), whole(8, D2), whole(8, D2), whole(8, 128),
            ],
            out_specs=[
                pl.BlockSpec((GRP, 2, PATCH // GRP, PATCH), lambda r, *_: (0, r, 0, 0)),
                pl.BlockSpec((1, 3, 2, D2, D2), lambda r, *_: (r, 0, 0, 0, 0)),
                whole(64, D2),
                whole(D2, 128),
                whole(8, PATCH),
            ],
            scratch_shapes=[pltpu.VMEM((D2, PATCH), BF), pltpu.VMEM((2, D2, PATCH), F32)],
        ),
        out_shape=[
            pltpu.HBM((GRP, BLOCKS, PATCH // GRP, PATCH), BF),
            pltpu.HBM((OWN, 3, 2, D2, D2), F32),
            pltpu.HBM((64, D2), F32),
            pltpu.HBM((D2, 128), F32),
            jax.ShapeDtypeStruct((8, PATCH), F32),
        ],
        compiler_params=params(40),
        cost_estimate=pl.CostEstimate(
            flops=4_000_000_000, bytes_accessed=20_000_000, transcendentals=0
        ),
        name="region_backward",
    )(idx, slide, tissue, wp, ap, att_w, w_class, g_logits, *kept)


def split_three(x):
    parts = []
    for _ in range(3):
        top = x.astype(BF).astype(F32)
        parts.append(top)
        x = x - top
    return parts


def join_sums_kernel(z_ref, scal_ref, df_ref, out_ref, ext, wide, sem):
    z = jnp.sum(z_ref[...], axis=0)
    z = jnp.concatenate([z[0:SLIDES], z[SLIDES:]], axis=1)
    ext[...] = jnp.zeros_like(ext)
    for i, (part, tops) in enumerate(zip(split_three(z), split_three(scal_ref[0:1]))):
        ext[pl.ds(4 * i, 4), :] = part
        ext[pl.ds(12 + i, 1), :] = tops
    wide[...] = jnp.broadcast_to(ext[...].astype(BF)[None], wide.shape)
    copy = pltpu.make_async_copy(wide, out_ref.at[:, BLOCKS - 1], sem)
    copy.start()
    copy.wait()


def join_sums(z, scalars, df):
    return pl.pallas_call(
        join_sums_kernel,
        in_specs=[pl.BlockSpec(memory_space=pltpu.VMEM)] * 2
        + [pl.BlockSpec(memory_space=pl.ANY)],
        out_specs=pl.BlockSpec(memory_space=pl.ANY),
        out_shape=pltpu.HBM(df.shape, df.dtype),
        scratch_shapes=[
            pltpu.VMEM((16, PATCH), F32),
            pltpu.VMEM((GRP, 16, PATCH), BF),
            pltpu.SemaphoreType.DMA,
        ],
        input_output_aliases={2: 0},
        compiler_params=params(24),
        name="join_sums",
    )(z, scalars, df)


STEPS4 = 4
FB4 = F1 // STEPS4


def put_rest(pack, slot, grad, fill=None):
    at = REST_AT + 192 * slot
    if not isinstance(slot, int):
        at = pl.multiple_of(at, 64)
    for half in range(2):
        rows = grad[96 * half : 96 * half + 96]
        pack[half, pl.ds(at, 96), :] = rows[:, :128].astype(BF)
        tail = jnp.zeros((96, 64), F32) if fill is None else fill
        high = jnp.concatenate([rows[:, 128:], tail], axis=1)
        pack[half, pl.ds(at + 96, 96), :] = high.astype(BF)


def finish_slides(
    idx_ref, slide_ref, back_ref, rows_ref, cols_ref, wc_ref, gl_ref, logits_ref, gc_ref,
    df_s, pq_s, pack,
):
    ext = back_ref[:, BLOCKS - 1].astype(F32)
    sums = jnp.sum(ext, axis=0)
    sums = sums[0:4] + sums[4:8] + sums[8:12]
    total = sums[:, D2 : D2 + 1]
    summary = sums[:, :D2] / total
    wc = wc_ref[...]
    gl = gl_ref[...]
    logits_ref[...] = nt(summary, wc, HIGHEST)
    gc_ref[...] = tn(gl, summary, HIGHEST)
    along = jnp.sum(nn(gl, wc, HIGHEST) * summary, axis=1, keepdims=True)

    def of_slide(column, s):
        out = column[SLIDES - 1 : SLIDES]
        for i in range(SLIDES - 1):
            out = jnp.where(s == i, column[i : i + 1], out)
        return out

    def factors(w, a, s):
        share = w / of_slide(total, s)
        return share, share * (a - of_slide(along, s))

    for src in range(GRP):
        scalars = ext[src, 12:13] + ext[src, 13:14] + ext[src, 14:15]
        for i in range(OWN):
            w = scalars[:, 128 * i : 128 * i + 1]
            a = scalars[:, 128 * i + 64 : 128 * i + 65]
            p, q = factors(w, a, slide_ref[idx_ref[5] + OWN * src + i])
            f = [back_ref[src, 2 * i + j].astype(F32)[:, :D2] for j in range(2)]
            df_s[pl.ds(32 * src + 16 * i, 16), :] = (p * f[0] + q * f[1]).astype(BF)

    kept = [rows_ref[pl.ds(8 * i, 8), :] for i in range(6)]
    pre_v, pre_u, dm0, dm1, w_own, a_own = kept
    row = lax.broadcasted_iota(jnp.int32, (8, 1), 0)
    p_own = jnp.zeros((8, 1), F32)
    q_own = jnp.zeros((8, 1), F32)
    for i in range(OWN):
        p, q = factors(w_own[i : i + 1, 0:1], a_own[i : i + 1, 0:1], slide_ref[idx_ref[0] + i])
        p_own = jnp.where(row == i, p, p_own)
        q_own = jnp.where(row == i, q, q_own)
    pq_s[0] = jnp.broadcast_to(p_own, (8, 128))
    pq_s[1] = jnp.broadcast_to(q_own, (8, 128))

    def outer(at, rows):
        out = cols_ref[:, at : at + 1] * rows[0:1]
        return out + cols_ref[:, at + 1 : at + 2] * rows[1:2]

    put_rest(pack, 3, outer(8, p_own * dm0 + q_own * dm1))
    put_rest(pack, 4, outer(0, q_own * pre_v))
    g_aw = outer(16, jnp.broadcast_to(q_own, (8, 64)))
    lane = lax.broadcasted_iota(jnp.int32, (96, 64), 1)
    put_rest(pack, 5, outer(0, q_own * pre_u), jnp.where(lane == 0, g_aw[:96], g_aw[96:]))


def patch_backward_kernel(
    idx_ref, slide_ref, back_ref, xt_ref, mid_ref, hid_ref, gp_ref, we_ref, wd_ref,
    grad_ref, rows_ref, cols_ref, wc_ref, gl_ref,
    mine_ref, other_ref, logits_ref, gc_ref,
    pack, dmid_s, df_s, pq_s, sems,
):
    step = pl.program_id(0)
    core = idx_ref[3]

    def up_copies(i):
        rows = pl.ds(pl.multiple_of(576 * i, 64), 576)
        return (
            pltpu.make_async_copy(pack.at[core, rows], mine_ref.at[rows], sems.at[2 * i]),
            pltpu.make_async_copy(pack.at[1 - core, rows], other_ref.at[rows], sems.at[2 * i + 1]),
        )

    def down_copy(i, dst):
        rows = pl.ds(pl.multiple_of(DOWN_AT + 1152 * lax.rem(i, 2), 128), 1152)
        return pltpu.make_async_copy(pack.at[i // 2, rows], dst.at[rows], sems.at[8 + i])

    def rest_copies():
        rows = pl.ds(REST_AT, HALF_ROWS - REST_AT)
        return (
            pltpu.make_async_copy(pack.at[core, rows], mine_ref.at[rows], sems.at[12]),
            pltpu.make_async_copy(pack.at[1 - core, rows], other_ref.at[rows], sems.at[13]),
        )

    @pl.when(step == 0)
    def _():
        finish_slides(
            idx_ref, slide_ref, back_ref, rows_ref, cols_ref, wc_ref, gl_ref, logits_ref, gc_ref,
            df_s, pq_s, pack,
        )
        df = df_s[...]
        dmid_s[...] = nn(df, we_ref[...]).astype(BF)
        g_embed = tn(df, mid_ref[...]).astype(BF)
        for half in range(2):
            for l in range(3):
                block = g_embed[96 * half : 96 * half + 96, 128 * l : 128 * l + 128]
                pack[half, pl.ds(EMBED_AT + 96 * l, 96), :] = block
            pack[half, pl.ds(PAD_AT, 96), :] = jnp.zeros((96, 128), BF)

    @pl.when(step > 0)
    def _():
        grad = jnp.zeros((D2, D2), F32)
        for i in range(OWN):
            for j in range(2):
                grad = grad + pq_s[j, i : i + 1, 0:1] * grad_ref[i, 0, j]
        put_rest(pack, step - 1, grad)

    dmid = dmid_s[...]
    d_pre = (nt(dmid, wd_ref[...]) * gp_ref[...].astype(F32)).astype(BF)
    g_up = nn(xt_ref[...], d_pre).astype(BF)
    for half in range(2):
        for l in range(3):
            block = g_up[192 * half : 192 * half + 192, 128 * l : 128 * l + 128]
            pack[half, pl.ds(pl.multiple_of(576 * step + 192 * l, 64), 192), :] = block
    g_down = nn(hid_ref[...], dmid).astype(BF)
    at = DOWN_AT + 1152 * lax.rem(step, 2)
    for l in range(3):
        rows = pl.ds(pl.multiple_of(at + 384 * l, 128), 384)
        pack[step // 2, rows, :] = g_down[:, 128 * l : 128 * l + 128]

    for copy in up_copies(step):
        copy.start()

    @pl.when(step // 2 == core)
    def _():
        down_copy(step, mine_ref).start()

    @pl.when(step // 2 != core)
    def _():
        down_copy(step, other_ref).start()

    @pl.when(step == pl.num_programs(0) - 1)
    def _():
        for copy in rest_copies():
            copy.start()
        for copy in rest_copies():
            copy.wait()
        for i in range(STEPS4):
            for copy in up_copies(i):
                copy.wait()
            down_copy(i, mine_ref).wait()


def patch_backward(
    idx, slide, back, turned, mid, hid, gp, w_embed, w_down, grads, rows, cols, w_class, g_logits
):
    tokens = turned.shape[1]
    whole = lambda i, *_: (0, 0)
    grad = pl.BlockSpec(
        (OWN, 1, 2, D2, D2), lambda i, *_: (0, jnp.maximum(i - 1, 0), 0, 0, 0)
    )
    return pl.pallas_call(
        patch_backward_kernel,
        grid_spec=pltpu.PrefetchScalarGridSpec(
            num_scalar_prefetch=2,
            grid=(STEPS4,),
            in_specs=[
                pl.BlockSpec(back.shape, lambda i, *_: (0, 0, 0, 0)),
                pl.BlockSpec((D1, tokens), whole),
                pl.BlockSpec((tokens, D1), whole),
                pl.BlockSpec((FB4, tokens), lambda i, *_: (i, 0)),
                pl.BlockSpec((tokens, FB4), lambda i, *_: (0, i)),
                pl.BlockSpec((D2, D1), whole),
                pl.BlockSpec((FB4, D1), lambda i, *_: (i, 0)),
                grad,
                pl.BlockSpec((64, D2), whole),
                pl.BlockSpec((D2, 128), whole),
                pl.BlockSpec((3, D2), whole),
                pl.BlockSpec((SLIDES, 3), whole),
            ],
            out_specs=[
                pl.BlockSpec(memory_space=pl.ANY),
                pl.BlockSpec(memory_space=pl.ANY),
                pl.BlockSpec((SLIDES, 3), whole),
                pl.BlockSpec((3, D2), whole),
            ],
            scratch_shapes=[
                pltpu.VMEM((2, HALF_ROWS, 128), BF),
                pltpu.VMEM((tokens, D1), BF),
                pltpu.VMEM((tokens, D2), BF),
                pltpu.VMEM((2, 8, 128), F32),
                pltpu.SemaphoreType.DMA((14,)),
            ],
        ),
        out_shape=[
            jax.ShapeDtypeStruct((HALF_ROWS, 128), BF),
            jax.ShapeDtypeStruct((HALF_ROWS, 128), BF),
            jax.ShapeDtypeStruct((SLIDES, 3), F32),
            jax.ShapeDtypeStruct((3, D2), F32),
        ],
        compiler_params=params(61),
        name="patch_backward",
    )(
        idx, slide, back, turned, mid, hid, gp, w_embed, w_down, grads, rows, cols, w_class,
        g_logits,
    )


def unpack_kernel(idx_ref, src_ref, *refs):
    up_ref, down_ref, embed_ref, q_ref, k_ref, v_ref, o_ref, av_ref, au_ref, aw_ref = refs[-10:]
    for l in range(12):
        up_ref[:, pl.ds(128 * l, 128)] = src_ref[pl.ds(192 * l, 192), :].astype(F32)
    for i in range(2):
        for l in range(3):
            rows = src_ref[pl.ds(DOWN_AT + 1152 * i + 384 * l, 384), :]
            down_ref[pl.ds(384 * i, 384), pl.ds(128 * l, 128)] = rows.astype(F32)
    for slot, ref in enumerate((q_ref, k_ref, v_ref, o_ref, av_ref, au_ref)):
        at = REST_AT + 192 * slot
        ref[:, pl.ds(0, 128)] = src_ref[pl.ds(at, 96), :].astype(F32)
        ref[:, pl.ds(128, 64)] = src_ref[pl.ds(at + 96, 96), :][:, :64].astype(F32)
    for l in range(3):
        embed_ref[:, pl.ds(128 * l, 128)] = src_ref[pl.ds(EMBED_AT + 96 * l, 96), :].astype(F32)
    tail = src_ref[pl.ds(EMBED_AT - 96, 96), :].astype(F32).T
    aw_ref[:, pl.ds(0, 96)] = tail[64:65, :]
    aw_ref[:, pl.ds(96, 96)] = tail[65:66, :]


def unpack(idx, src, which, earlier=()):
    square = jax.ShapeDtypeStruct((D2, D2), F32)
    half = lambda rows, width: pl.BlockSpec((rows, width), lambda i, idx: (idx[which], 0))
    hbm = pl.BlockSpec(memory_space=pltpu.HBM)
    return pl.pallas_call(
        unpack_kernel,
        grid_spec=pltpu.PrefetchScalarGridSpec(
            num_scalar_prefetch=1,
            grid=(1,),
            in_specs=[pl.BlockSpec((HALF_ROWS, 128), lambda i, idx: (0, 0))] + [hbm] * len(earlier),
            out_specs=[
                half(D1 // 2, F1),
                half(F1 // 2, D1),
                half(D2 // 2, D1),
            ]
            + [half(D2 // 2, D2)] * 6
            + [pl.BlockSpec((1, D2), lambda i, idx: (0, 0))],
        ),
        out_shape=[
            jax.ShapeDtypeStruct((D1, F1), F32),
            jax.ShapeDtypeStruct((F1, D1), F32),
            jax.ShapeDtypeStruct((D2, D1), F32),
            square, square, square, square, square, square,
            jax.ShapeDtypeStruct((1, D2), F32),
        ],
        input_output_aliases={2 + i: i for i in range(len(earlier))},
        compiler_params=params(),
        name="unpack",
    )(idx, src, *earlier)


GRP_AXES = ("zl", "x", "c")
DEV_AXES = ("zh", "y")
ZLXY = ("y", "zl", "x")


def exchange(x, axes):
    return lax.all_to_all(x, axes, split_axis=0, concat_axis=0, tiled=True)


def swap_cores(x):
    return lax.ppermute(x, "c", [(0, 1), (1, 0)])


def spread(x, n):
    return jnp.broadcast_to(x[None], (n,) + x.shape)


def add_pair(x, y):
    return (x.astype(F32) + y.astype(F32)).astype(x.dtype)


def add_over_zh(x):
    got = [lax.ppermute(x, "zh", [(i, i ^ k) for i in range(4)]) for k in (1, 2, 3)]
    a, b, c, d = [y.astype(F32) for y in (x, *got)]
    return ((a + b) + (c + d)).astype(x.dtype)


def add_up(x):
    return jnp.sum(x.astype(F32), axis=0).astype(x.dtype)


def body(
    patches, tissue, region_slide, w_up, w_down, w_embed, w_query, w_key, w_value, w_out,
    att_v, att_u, att_w, w_class, g_logits,
):
    grp = lax.axis_index(GRP_AXES)
    dev = lax.axis_index(DEV_AXES)
    core = lax.axis_index("c")
    first = (dev * GRP + grp) * OWN
    idx = jnp.stack([first, first % 8, first // 8, core, 1 - core, dev * GRP * OWN]).astype(jnp.int32)
    tokens = patches.reshape(-1, D1)
    att_row = att_w.reshape(1, D2)
    class_rows = w_class.T
    feat, mid = patch_forward(tokens, w_up, w_down, w_embed.T)
    wp, ap = gather_weights((w_query, w_key, w_value, w_out, att_v, att_u))
    got = exchange(feat.reshape(GRP, -1, D2), GRP_AXES)
    got = got.reshape(GRP, OWN, PATCH // GRP, D2)
    *kept, part = region_forward(idx, region_slide, got, tissue, wp, ap, att_row)
    z = exchange(part, DEV_AXES)
    df, grads, rows, cols, scalars = region_backward(
        idx, region_slide, tissue, wp, ap, att_row, class_rows, g_logits, kept
    )
    df = join_sums(z, scalars, df)
    hid, gp, turned = patch_slopes(rows, tokens, w_up)
    back = exchange(df.reshape(GRP, -1, PATCH), GRP_AXES).reshape(df.shape)
    mine, other, logits, g_class = patch_backward(
        idx, region_slide, back, turned, mid, hid, gp, w_embed.T, w_down, grads, rows,
        cols, class_rows, g_logits,
    )
    half = add_pair(mine, swap_cores(other))
    chunk = add_up(exchange(half.reshape(PEERS, -1, 128), ZLXY))
    chunk = add_over_zh(chunk)
    half = exchange(spread(chunk, PEERS), ZLXY).reshape(HALF_ROWS, 128)
    other = swap_cores(half)
    grads = unpack(idx, other, 4, unpack(idx, half, 3))
    up, down, embed, query, key, value, out, gv, gu, gw = grads
    return (
        logits, up, down, embed.T, query, key, value, out, gv, gu, gw.reshape(D2), g_class.T,
    )


def solution(mesh):
    fine = Mesh(mesh.devices.reshape(2, 4, 2, 4, 4), GRP_AXES + DEV_AXES)
    placed = (P(DEV_AXES, GRP_AXES, None),) + (P(),) * 14
    return jax.shard_map(
        body,
        mesh=fine,
        in_specs=placed,
        out_specs=(P(),) * 12,
        check_vma=False,
    )
```

```python
import math

import jax
import jax.numpy as jnp
from jax import lax
from jax.experimental import pallas as pl
from jax.experimental.pallas import tpu as pltpu
from jax.sharding import Mesh, PartitionSpec as P

D1 = 384
F1 = 1536
HEADS = 6
HEAD_DIM = 32
D2 = 192
PATCH = 256
SLIDES = 4
GRP = 16
OWN = 2
SCALE = 1.0 / math.sqrt(HEAD_DIM)
GELU_C = math.sqrt(2.0 / math.pi)
GELU_A = 0.044715

BF = jnp.bfloat16
F32 = jnp.float32
HIGHEST = lax.Precision.HIGHEST
MIB = 1024 * 1024

HALF_ROWS = 6144
DOWN_AT = 2304
REST_AT = 4608
REST_ROWS = 1152
EMBED_AT = REST_AT + REST_ROWS
PAD_AT = EMBED_AT + 288
PEERS = 32


def nn(a, b, precision=None):
    return jnp.dot(a, b, precision=precision, preferred_element_type=F32)


def nt(a, b, precision=None):
    return lax.dot_general(
        a, b, (((1,), (1,)), ((), ())), precision=precision, preferred_element_type=F32
    )


def tn(a, b, precision=None):
    return lax.dot_general(
        a, b, (((0,), (0,)), ((), ())), precision=precision, preferred_element_type=F32
    )


def params(mib=32):
    return pltpu.CompilerParams(vmem_limit_bytes=mib * MIB)


STEPS1 = 4
FB1 = F1 // STEPS1


def begin(copies):
    for copy in copies:
        copy.start()
    return copies


def patch_forward_kernel(x_ref, wu_ref, wd_ref, we_ref, feat_ref, mid_ref):
    x = x_ref[...]
    pre = nn(x, wu_ref[...])
    t = jnp.tanh(GELU_C * (pre + GELU_A * (pre * (pre * pre))))
    hid = (pre * (0.5 + 0.5 * t)).astype(BF)
    mid = (x.astype(F32) + nn(hid, wd_ref[...])).astype(BF)
    mid_ref[...] = mid
    feat_ref[...] = nt(mid, we_ref[...]).astype(BF)


def patch_forward(tokens, w_up, w_down, w_embed):
    rows = tokens.shape[0]
    vmem = pl.BlockSpec(memory_space=pltpu.VMEM)
    return pl.pallas_call(
        patch_forward_kernel,
        in_specs=[vmem] * 4,
        out_specs=[vmem] * 2,
        out_shape=[
            jax.ShapeDtypeStruct((rows, D2), BF),
            jax.ShapeDtypeStruct((rows, D1), BF),
        ],
        compiler_params=params(61),
        name="patch_forward",
    )(tokens, w_up, w_down, w_embed)


def patch_slopes_kernel(after_ref, x_ref, wu_ref, hid_ref, gp_ref, xt_ref):
    x = x_ref[...]

    @pl.when(pl.program_id(0) == 0)
    def _():
        xt_ref[...] = x.T

    pre = nn(x, wu_ref[...])
    sq = pre * pre
    t = jnp.tanh(GELU_C * (pre + GELU_A * (pre * sq)))
    half_up = 0.5 + 0.5 * t
    hid_ref[...] = (pre * half_up).astype(BF).T
    slope = (0.5 * GELU_C) * (1.0 - t * t) * (1.0 + (3.0 * GELU_A) * sq)
    gp_ref[...] = (half_up + pre * slope).astype(BF)


def patch_slopes(after, tokens, w_up):
    rows = tokens.shape[0]
    whole = lambda i: (0, 0)
    return pl.pallas_call(
        patch_slopes_kernel,
        grid=(STEPS1,),
        in_specs=[
            pl.BlockSpec(memory_space=pl.ANY),
            pl.BlockSpec((rows, D1), whole),
            pl.BlockSpec((D1, FB1), lambda i: (0, i)),
        ],
        out_specs=[
            pl.BlockSpec((FB1, rows), lambda i: (i, 0)),
            pl.BlockSpec((rows, FB1), lambda i: (0, i)),
            pl.BlockSpec((D1, rows), whole),
        ],
        out_shape=[
            pltpu.HBM((F1, rows), BF),
            pltpu.HBM((rows, F1), BF),
            pltpu.HBM((D1, rows), BF),
        ],
        compiler_params=params(61),
        cost_estimate=pl.CostEstimate(
            flops=3_000_000_000, bytes_accessed=12_000_000, transcendentals=0
        ),
        name="patch_slopes",
    )(after, tokens, w_up)


def gather_weights_kernel(*refs):
    ins, (wp_ref, ap_ref) = refs[:6], refs[6:]
    for i in range(4):
        wp_ref[i] = ins[i][...]
    for i in range(2):
        ap_ref[i] = ins[4 + i][...]


def gather_weights(weights):
    vm = pl.BlockSpec(memory_space=pltpu.VMEM)
    return pl.pallas_call(
        gather_weights_kernel,
        in_specs=[vm] * 6,
        out_specs=[vm] * 2,
        out_shape=[
            jax.ShapeDtypeStruct((4, D2, D2), BF),
            jax.ShapeDtypeStruct((2, D2, D2), F32),
        ],
        compiler_params=params(24),
        cost_estimate=pl.CostEstimate(
            flops=1_000_000_000, bytes_accessed=4_000_000, transcendentals=0
        ),
        name="gather_weights",
    )(*weights)


def tissue_row(idx_ref, tis_ref, r):
    return tis_ref[pl.ds(idx_ref[1] + r, 1), :].astype(F32)


def column_of(row, width):
    return jnp.broadcast_to(row, (PATCH, row.shape[1])).T[:, :width]


def head_mask(h, shape, dim):
    return (lax.broadcasted_iota(jnp.int32, shape, dim) // HEAD_DIM == h).astype(F32)


def region_forward_kernel(
    idx_ref, slide_ref, f_ref, tis_ref, wp_ref, ap_ref, aw_ref,
    p_ref, x_ref, asum_ref, reg_ref, tanh_ref, gate_ref, w_ref,
    part_ref,
):
    lane = lax.broadcasted_iota(jnp.int32, (8, PATCH), 1)
    reg_ref[...] = jnp.where(lane < D2, 0.0, 1.0)
    asum_ref[...] = jnp.zeros_like(asum_ref)
    for r in range(OWN):
        trow = tissue_row(idx_ref, tis_ref, r)
        tcol = column_of(trow, D2)
        x = (f_ref[:, r].reshape(PATCH, D2).astype(F32) * tcol).astype(BF)
        q = nn(x, wp_ref[0]).astype(BF)
        k = nn(x, wp_ref[1])
        v = nn(x, wp_ref[2]).astype(BF)
        x_ref[r] = x
        spread = jnp.zeros((PATCH, D2), F32)
        for h in range(HEADS):
            mask = head_mask(h, (1, D2), 1)
            st = nt((k * mask).astype(BF), q) * SCALE
            top = jnp.max(st, axis=0, keepdims=True)
            ex = jnp.exp(st - top)
            total = jnp.sum(ex, axis=0, keepdims=True)
            pb = (ex * (1.0 / total)).astype(BF)
            p_ref[r, pl.ds(h * PATCH, PATCH), :] = pb
            spread = spread + nn(pb, (tcol * mask).astype(BF))
        asum = jnp.sum(spread * v.astype(F32), axis=0, keepdims=True)
        xsum = jnp.sum(x.astype(F32), axis=0, keepdims=True)
        count = jnp.maximum(jnp.sum(trow, axis=1, keepdims=True), 1.0)
        mixed = xsum + nn(jnp.broadcast_to(asum, (8, D2)), wp_ref[3].astype(F32), HIGHEST)[0:1]
        asum_ref[pl.ds(r, 1), :] = asum
        reg_ref[pl.ds(r, 1), pl.ds(0, D2)] = mixed / count

    region = reg_ref[:, pl.ds(0, D2)]
    tanh_part = jnp.tanh(nn(region, ap_ref[0], HIGHEST))
    gate_part = jax.nn.sigmoid(nn(region, ap_ref[1], HIGHEST))
    tanh_ref[...] = tanh_part
    gate_ref[...] = gate_part
    score = jnp.sum(tanh_part * gate_part * aw_ref[...], axis=1, keepdims=True)
    weight = jnp.exp(score)
    w_ref[...] = jnp.broadcast_to(weight, w_ref.shape)
    wide = reg_ref[...] * weight
    slot = lax.broadcasted_iota(jnp.int32, (SLIDES, 1), 0)
    sums = jnp.zeros((SLIDES, PATCH), F32)
    for i in range(OWN):
        own = (slot == slide_ref[idx_ref[0] + i]).astype(F32)
        sums = sums + own * wide[i : i + 1]
    both = jnp.concatenate([sums[:, :128], sums[:, 128:]], axis=0)
    part_ref[...] = jnp.broadcast_to(both[None], part_ref.shape)


def packed_specs():
    return [
        pl.BlockSpec((4, D2, D2), lambda r, *_: (0, 0, 0)),
        pl.BlockSpec((2, D2, D2), lambda r, *_: (0, 0, 0)),
    ]


def region_forward(idx, slide, got, tissue, wp, ap, att_w):
    row8 = lambda width: pl.BlockSpec((8, width), lambda r, *_: (0, 0))
    per_region = lambda rows, width: pl.BlockSpec((OWN, rows, width), lambda r, *_: (0, 0, 0))
    return pl.pallas_call(
        region_forward_kernel,
        grid_spec=pltpu.PrefetchScalarGridSpec(
            num_scalar_prefetch=2,
            grid=(1,),
            in_specs=[
                pl.BlockSpec((GRP, OWN, PATCH // GRP, D2), lambda r, *_: (0, 0, 0, 0)),
                pl.BlockSpec((8, PATCH), lambda r, idx, _: (idx[2], 0)),
                *packed_specs(),
                pl.BlockSpec((1, D2), lambda r, *_: (0, 0)),
            ],
            out_specs=[
                per_region(HEADS * PATCH, PATCH),
                per_region(PATCH, D2),
                row8(D2),
                row8(PATCH),
                row8(D2),
                row8(D2),
                row8(128),
                pl.BlockSpec((GRP, 8, 128), lambda r, *_: (0, 0, 0)),
            ],
        ),
        out_shape=[
            jax.ShapeDtypeStruct((OWN, HEADS * PATCH, PATCH), BF),
            jax.ShapeDtypeStruct((OWN, PATCH, D2), BF),
            jax.ShapeDtypeStruct((8, D2), F32),
            jax.ShapeDtypeStruct((8, PATCH), F32),
            jax.ShapeDtypeStruct((8, D2), F32),
            jax.ShapeDtypeStruct((8, D2), F32),
            jax.ShapeDtypeStruct((8, 128), F32),
            jax.ShapeDtypeStruct((GRP, 8, 128), F32),
        ],
        compiler_params=params(40),
        name="region_forward",
    )(idx, slide, got, tissue, wp, ap, att_w)


def directions(
    idx_ref, slide_ref, tis_ref, wp_ref, ap_ref, aw_ref, wc_ref, gl_ref,
    asum_ref, reg_ref, tanh_ref, gate_ref, w_ref, rows_ref, cols_ref, scal_ref,
):
    d_summary = nn(gl_ref[...], wc_ref[...], HIGHEST)
    slot = lax.broadcasted_iota(jnp.int32, (SLIDES, 1), 0)
    row = lax.broadcasted_iota(jnp.int32, (8, 1), 0)
    d_own = jnp.zeros((8, D2), F32)
    count = jnp.ones((8, 1), F32)
    for i in range(OWN):
        mine = slot == slide_ref[idx_ref[0] + i]
        d_own = jnp.where(
            row == i, jnp.sum(jnp.where(mine, d_summary, 0.0), axis=0, keepdims=True), d_own
        )
        t_i = tissue_row(idx_ref, tis_ref, i)
        count = jnp.where(row == i, jnp.maximum(jnp.sum(t_i, axis=1, keepdims=True), 1.0), count)
    region = reg_ref[:, pl.ds(0, D2)]
    tanh_part = tanh_ref[...]
    gate_part = gate_ref[...]
    pre_v = aw_ref[...] * gate_part * (1.0 - tanh_part * tanh_part)
    pre_u = aw_ref[...] * tanh_part * gate_part * (1.0 - gate_part)
    second = nt(pre_v, ap_ref[0], HIGHEST) + nt(pre_u, ap_ref[1], HIGHEST)
    own = jnp.sum(d_own * region, axis=1, keepdims=True)
    dm = (d_own / count, second / count)
    kept = (
        pre_v, pre_u, dm[0], dm[1],
        jnp.broadcast_to(w_ref[:, 0:1], (8, D2)), jnp.broadcast_to(own, (8, D2)),
        nt(dm[0].astype(BF), wp_ref[3]), nt(dm[1].astype(BF), wp_ref[3]),
    )
    for i, value in enumerate(kept):
        rows_ref[pl.ds(8 * i, 8), :] = value
    turned = jnp.concatenate(
        [region, asum_ref[...], tanh_part * gate_part, jnp.zeros((104, D2), F32)], axis=0
    )
    cols_ref[...] = turned.T
    lane = lax.broadcasted_iota(jnp.int32, (1, PATCH), 1) // 64
    scalars = jnp.zeros((1, PATCH), F32)
    for i in range(OWN):
        scalars = jnp.where(lane == 2 * i, w_ref[i : i + 1, 0:1], scalars)
        scalars = jnp.where(lane == 2 * i + 1, own[i : i + 1], scalars)
    scal_ref[...] = jnp.broadcast_to(scalars, (8, PATCH))


def pull_back(r, idx_ref, tis_ref, wp_ref, p_ref, x_ref, rows_ref, df_ref, grad_ref, kt_s, dqt_s):
    trow = tissue_row(idx_ref, tis_ref, r)
    tcol = column_of(trow, D2)
    x = x_ref[r]
    q = nn(x, wp_ref[0]).astype(BF).astype(F32)
    v = nn(x, wp_ref[2]).astype(BF)
    kt_s[r] = nn(x, wp_ref[1]).T.astype(BF)
    spread = jnp.zeros((PATCH, D2), F32)
    dm = [rows_ref[pl.ds(8 * (2 + j) + r, 1), :] for j in range(2)]
    da = [rows_ref[pl.ds(8 * (6 + j) + r, 1), :].astype(BF).astype(F32) for j in range(2)]
    da_col = jnp.concatenate([jnp.broadcast_to(d, (128, D2)) for d in da], axis=0).T
    dk = [jnp.zeros((PATCH, D2), F32) for _ in range(2)]
    for h in range(HEADS):
        e = nn(v, (da_col * head_mask(h, (D2, 1), 0)).astype(BF))
        pb = p_ref[r, pl.ds(h * PATCH, PATCH), :]
        pt = pb.astype(F32)
        mask = head_mask(h, (1, D2), 1)
        spread = spread + nn(pb, (tcol * mask).astype(BF))
        q_head = (q * mask).astype(BF)
        k_head = kt_s[r, pl.ds(h * HEAD_DIM, HEAD_DIM), :]
        for j in range(2):
            e_j = e[:, 128 * j : 128 * j + 128]
            pe = pt * jnp.concatenate([e_j, e_j], axis=1)
            ds = (pe - pt * jnp.sum(pe, axis=0, keepdims=True)).astype(BF)
            dk[j] = dk[j] + nn(ds, q_head)
            dqt_s[r, j, pl.ds(h * HEAD_DIM, HEAD_DIM), :] = nn(k_head, ds)
    xt = x.astype(F32).T.astype(BF)
    for j in range(2):
        dq = (dqt_s[r, j] * (trow * SCALE)).T.astype(BF)
        dk_j = (dk[j] * SCALE).astype(BF)
        dv = (spread * da[j]).astype(BF)
        grad_ref[r, 0, j] = nn(xt, dq)
        grad_ref[r, 1, j] = nn(xt, dk_j)
        grad_ref[r, 2, j] = nn(xt, dv)
        d_flat = dm[j] + nt(dq, wp_ref[0]) + nt(dk_j, wp_ref[1]) + nt(dv, wp_ref[2])
        d_flat = (tcol * d_flat).astype(BF).reshape(GRP, PATCH // GRP, D2)
        df_ref[:, 2 * r + j, :, pl.ds(0, D2)] = d_flat
        df_ref[:, 2 * r + j, :, pl.ds(D2, 64)] = jnp.zeros((GRP, PATCH // GRP, 64), BF)


BLOCKS = 2 * OWN + 1


def region_backward_kernel(
    idx_ref, slide_ref, tis_ref, wp_ref, ap_ref, aw_ref, wc_ref, gl_ref,
    p_ref, x_ref, asum_ref, reg_ref, tanh_ref, gate_ref, w_ref,
    df_ref, grad_ref, rows_ref, cols_ref, scal_ref,
    kt_s, dqt_s,
):
    directions(
        idx_ref, slide_ref, tis_ref, wp_ref, ap_ref, aw_ref, wc_ref, gl_ref,
        asum_ref, reg_ref, tanh_ref, gate_ref, w_ref, rows_ref, cols_ref, scal_ref,
    )
    for r in range(OWN):
        pull_back(
            r, idx_ref, tis_ref, wp_ref, p_ref, x_ref, rows_ref, df_ref, grad_ref, kt_s, dqt_s
        )


def region_backward(idx, slide, tissue, wp, ap, att_w, w_class, g_logits, kept):
    whole = lambda rows, width: pl.BlockSpec((rows, width), lambda r, *_: (0, 0))
    region = lambda rows, width: pl.BlockSpec((OWN, rows, width), lambda r, *_: (0, 0, 0))
    return pl.pallas_call(
        region_backward_kernel,
        grid_spec=pltpu.PrefetchScalarGridSpec(
            num_scalar_prefetch=2,
            grid=(1,),
            in_specs=[
                pl.BlockSpec((8, PATCH), lambda r, idx, _: (idx[2], 0)),
                *packed_specs(),
                whole(1, D2), whole(3, D2), whole(SLIDES, 3),
                region(HEADS * PATCH, PATCH),
                region(PATCH, D2),
                whole(8, D2), whole(8, PATCH), whole(8, D2), whole(8, D2), whole(8, 128),
            ],
            out_specs=[
                pl.BlockSpec((GRP, 2 * OWN, PATCH // GRP, PATCH), lambda r, *_: (0, 0, 0, 0)),
                pl.BlockSpec((OWN, 3, 2, D2, D2), lambda r, *_: (0, 0, 0, 0, 0)),
                whole(64, D2),
                whole(D2, 128),
                whole(8, PATCH),
            ],
            scratch_shapes=[
                pltpu.VMEM((OWN, D2, PATCH), BF),
                pltpu.VMEM((OWN, 2, D2, PATCH), F32),
            ],
        ),
        out_shape=[
            pltpu.HBM((GRP, BLOCKS, PATCH // GRP, PATCH), BF),
            pltpu.HBM((OWN, 3, 2, D2, D2), F32),
            pltpu.HBM((64, D2), F32),
            pltpu.HBM((D2, 128), F32),
            jax.ShapeDtypeStruct((8, PATCH), F32),
        ],
        compiler_params=params(40),
        cost_estimate=pl.CostEstimate(
            flops=4_000_000_000, bytes_accessed=20_000_000, transcendentals=0
        ),
        name="region_backward",
    )(idx, slide, tissue, wp, ap, att_w, w_class, g_logits, *kept)


def split_three(x):
    parts = []
    for _ in range(3):
        top = x.astype(BF).astype(F32)
        parts.append(top)
        x = x - top
    return parts


def join_sums_kernel(z_ref, scal_ref, df_ref, out_ref, ext, wide, sem):
    z = jnp.sum(z_ref[...], axis=0)
    z = jnp.concatenate([z[0:SLIDES], z[SLIDES:]], axis=1)
    ext[...] = jnp.zeros_like(ext)
    for i, (part, tops) in enumerate(zip(split_three(z), split_three(scal_ref[0:1]))):
        ext[pl.ds(4 * i, 4), :] = part
        ext[pl.ds(12 + i, 1), :] = tops
    wide[...] = jnp.broadcast_to(ext[...].astype(BF)[None], wide.shape)
    copy = pltpu.make_async_copy(wide, out_ref.at[:, BLOCKS - 1], sem)
    copy.start()
    copy.wait()


def join_sums(z, scalars, df):
    return pl.pallas_call(
        join_sums_kernel,
        in_specs=[pl.BlockSpec(memory_space=pltpu.VMEM)] * 2
        + [pl.BlockSpec(memory_space=pl.ANY)],
        out_specs=pl.BlockSpec(memory_space=pl.ANY),
        out_shape=pltpu.HBM(df.shape, df.dtype),
        scratch_shapes=[
            pltpu.VMEM((16, PATCH), F32),
            pltpu.VMEM((GRP, 16, PATCH), BF),
            pltpu.SemaphoreType.DMA,
        ],
        input_output_aliases={2: 0},
        compiler_params=params(24),
        name="join_sums",
    )(z, scalars, df)


def put_rest(pack, slot, grad, fill=None):
    at = REST_AT + 192 * slot
    if not isinstance(slot, int):
        at = pl.multiple_of(at, 64)
    for half in range(2):
        rows = grad[96 * half : 96 * half + 96]
        pack[half, pl.ds(at, 96), :] = rows[:, :128].astype(BF)
        tail = jnp.zeros((96, 64), F32) if fill is None else fill
        high = jnp.concatenate([rows[:, 128:], tail], axis=1)
        pack[half, pl.ds(at + 96, 96), :] = high.astype(BF)


def finish_slides(
    idx_ref, slide_ref, back_ref, rows_ref, cols_ref, wc_ref, gl_ref, logits_ref, gc_ref,
    df_s, pq_s, pack,
):
    ext = back_ref[:, BLOCKS - 1].astype(F32)
    sums = jnp.sum(ext, axis=0)
    sums = sums[0:4] + sums[4:8] + sums[8:12]
    total = sums[:, D2 : D2 + 1]
    summary = sums[:, :D2] / total
    wc = wc_ref[...]
    gl = gl_ref[...]
    logits_ref[...] = nt(summary, wc, HIGHEST)
    gc_ref[...] = tn(gl, summary, HIGHEST)
    along = jnp.sum(nn(gl, wc, HIGHEST) * summary, axis=1, keepdims=True)

    def of_slide(column, s):
        out = column[SLIDES - 1 : SLIDES]
        for i in range(SLIDES - 1):
            out = jnp.where(s == i, column[i : i + 1], out)
        return out

    def factors(w, a, s):
        share = w / of_slide(total, s)
        return share, share * (a - of_slide(along, s))

    for src in range(GRP):
        scalars = ext[src, 12:13] + ext[src, 13:14] + ext[src, 14:15]
        for i in range(OWN):
            w = scalars[:, 128 * i : 128 * i + 1]
            a = scalars[:, 128 * i + 64 : 128 * i + 65]
            p, q = factors(w, a, slide_ref[idx_ref[5] + OWN * src + i])
            f = [back_ref[src, 2 * i + j].astype(F32)[:, :D2] for j in range(2)]
            df_s[pl.ds(32 * src + 16 * i, 16), :] = (p * f[0] + q * f[1]).astype(BF)

    kept = [rows_ref[pl.ds(8 * i, 8), :] for i in range(6)]
    pre_v, pre_u, dm0, dm1, w_own, a_own = kept
    row = lax.broadcasted_iota(jnp.int32, (8, 1), 0)
    p_own = jnp.zeros((8, 1), F32)
    q_own = jnp.zeros((8, 1), F32)
    for i in range(OWN):
        p, q = factors(w_own[i : i + 1, 0:1], a_own[i : i + 1, 0:1], slide_ref[idx_ref[0] + i])
        p_own = jnp.where(row == i, p, p_own)
        q_own = jnp.where(row == i, q, q_own)
    pq_s[0] = jnp.broadcast_to(p_own, (8, 128))
    pq_s[1] = jnp.broadcast_to(q_own, (8, 128))

    def outer(at, rows):
        out = cols_ref[:, at : at + 1] * rows[0:1]
        return out + cols_ref[:, at + 1 : at + 2] * rows[1:2]

    put_rest(pack, 3, outer(8, p_own * dm0 + q_own * dm1))
    put_rest(pack, 4, outer(0, q_own * pre_v))
    g_aw = outer(16, jnp.broadcast_to(q_own, (8, 64)))
    lane = lax.broadcasted_iota(jnp.int32, (96, 64), 1)
    put_rest(pack, 5, outer(0, q_own * pre_u), jnp.where(lane == 0, g_aw[:96], g_aw[96:]))


def patch_backward_kernel(
    idx_ref, slide_ref, back_in, xt_in, mid_in, hid_in, gp_in, we_in, wd_in, grad_in,
    rows_ref, cols_ref, wc_ref, gl_ref,
    mine_ref, other_ref, logits_ref, gc_ref,
    back_ref, xt_ref, mid_ref, hid_ref, gp_ref, we_ref, wd_ref, grad_ref,
    pack, df_s, pq_s, in_sems, sems,
):
    core = idx_ref[3]
    pairs = (
        (back_in, back_ref), (we_in, we_ref), (wd_in, wd_ref), (gp_in, gp_ref), (xt_in, xt_ref),
        (hid_in, hid_ref), (mid_in, mid_ref), (grad_in, grad_ref),
    )
    fetch = begin(
        [pltpu.make_async_copy(a, b, in_sems.at[i]) for i, (a, b) in enumerate(pairs)]
    )
    sent = []

    def send(low, size):
        rows = pl.ds(low, size)
        at = len(sent)
        sent.extend(
            begin(
                [
                    pltpu.make_async_copy(
                        pack.at[core, rows], mine_ref.at[rows], sems.at[at]
                    ),
                    pltpu.make_async_copy(
                        pack.at[1 - core, rows], other_ref.at[rows], sems.at[at + 1]
                    ),
                ]
            )
        )

    fetch[0].wait()
    finish_slides(
        idx_ref, slide_ref, back_ref, rows_ref, cols_ref, wc_ref, gl_ref, logits_ref, gc_ref,
        df_s, pq_s, pack,
    )
    df = df_s[...]
    fetch[1].wait()
    dmid = nn(df, we_ref[...]).astype(BF)
    for i in range(2, 5):
        fetch[i].wait()
    d_pre = (nt(dmid, wd_ref[...]) * gp_ref[...].astype(F32)).astype(BF)
    g_up = nn(xt_ref[...], d_pre).astype(BF)
    for l in range(F1 // 128):
        for half in range(2):
            block = g_up[192 * half : 192 * half + 192, 128 * l : 128 * l + 128]
            pack[half, pl.ds(192 * l, 192), :] = block
    send(0, DOWN_AT)
    fetch[5].wait()
    g_down = nn(hid_ref[...], dmid).astype(BF)
    for half in range(2):
        for l in range(3):
            block = g_down[768 * half : 768 * half + 768, 128 * l : 128 * l + 128]
            pack[half, pl.ds(DOWN_AT + 768 * l, 768), :] = block
    send(DOWN_AT, REST_AT - DOWN_AT)
    fetch[6].wait()
    g_embed = tn(df, mid_ref[...]).astype(BF)
    for half in range(2):
        for l in range(3):
            block = g_embed[96 * half : 96 * half + 96, 128 * l : 128 * l + 128]
            pack[half, pl.ds(EMBED_AT + 96 * l, 96), :] = block
        pack[half, pl.ds(PAD_AT, 96), :] = jnp.zeros((96, 128), BF)
    fetch[7].wait()
    for slot in range(3):
        grad = jnp.zeros((D2, D2), F32)
        for i in range(OWN):
            for j in range(2):
                grad = grad + pq_s[j, i : i + 1, 0:1] * grad_ref[i, slot, j]
        put_rest(pack, slot, grad)
    send(REST_AT, HALF_ROWS - REST_AT)
    for copy in sent:
        copy.wait()


def patch_backward(
    idx, slide, back, turned, mid, hid, gp, w_embed, w_down, grads, rows, cols, w_class, g_logits
):
    hbm = pl.BlockSpec(memory_space=pl.ANY)
    vmem = pl.BlockSpec(memory_space=pltpu.VMEM)
    smem = pl.BlockSpec(memory_space=pltpu.SMEM)
    big = (back, turned, mid, hid, gp, w_embed, w_down, grads)
    return pl.pallas_call(
        patch_backward_kernel,
        in_specs=[smem] * 2 + [hbm] * 8 + [vmem] * 4,
        out_specs=[hbm] * 2 + [vmem] * 2,
        out_shape=[
            jax.ShapeDtypeStruct((HALF_ROWS, 128), BF),
            jax.ShapeDtypeStruct((HALF_ROWS, 128), BF),
            jax.ShapeDtypeStruct((SLIDES, 3), F32),
            jax.ShapeDtypeStruct((3, D2), F32),
        ],
        scratch_shapes=[pltpu.VMEM(a.shape, a.dtype) for a in big]
        + [
            pltpu.VMEM((2, HALF_ROWS, 128), BF),
            pltpu.VMEM((turned.shape[1], D2), BF),
            pltpu.VMEM((2, 8, 128), F32),
            pltpu.SemaphoreType.DMA((8,)),
            pltpu.SemaphoreType.DMA((6,)),
        ],
        compiler_params=params(61),
        name="patch_backward",
    )(idx, slide, *big, rows, cols, w_class, g_logits)


def unpack_kernel(idx_ref, src_ref, *refs):
    up_ref, down_ref, embed_ref, q_ref, k_ref, v_ref, o_ref, av_ref, au_ref, aw_ref = refs[-10:]
    for l in range(12):
        up_ref[:, pl.ds(128 * l, 128)] = src_ref[pl.ds(192 * l, 192), :].astype(F32)
    for l in range(3):
        rows = src_ref[pl.ds(DOWN_AT + 768 * l, 768), :]
        down_ref[:, pl.ds(128 * l, 128)] = rows.astype(F32)
    for slot, ref in enumerate((q_ref, k_ref, v_ref, o_ref, av_ref, au_ref)):
        at = REST_AT + 192 * slot
        ref[:, pl.ds(0, 128)] = src_ref[pl.ds(at, 96), :].astype(F32)
        ref[:, pl.ds(128, 64)] = src_ref[pl.ds(at + 96, 96), :][:, :64].astype(F32)
    for l in range(3):
        embed_ref[:, pl.ds(128 * l, 128)] = src_ref[pl.ds(EMBED_AT + 96 * l, 96), :].astype(F32)
    tail = src_ref[pl.ds(EMBED_AT - 96, 96), :].astype(F32).T
    aw_ref[:, pl.ds(0, 96)] = tail[64:65, :]
    aw_ref[:, pl.ds(96, 96)] = tail[65:66, :]


def unpack(idx, src, which, earlier=()):
    square = jax.ShapeDtypeStruct((D2, D2), F32)
    half = lambda rows, width: pl.BlockSpec((rows, width), lambda i, idx: (idx[which], 0))
    hbm = pl.BlockSpec(memory_space=pltpu.HBM)
    return pl.pallas_call(
        unpack_kernel,
        grid_spec=pltpu.PrefetchScalarGridSpec(
            num_scalar_prefetch=1,
            grid=(1,),
            in_specs=[pl.BlockSpec((HALF_ROWS, 128), lambda i, idx: (0, 0))] + [hbm] * len(earlier),
            out_specs=[
                half(D1 // 2, F1),
                half(F1 // 2, D1),
                half(D2 // 2, D1),
            ]
            + [half(D2 // 2, D2)] * 6
            + [pl.BlockSpec((1, D2), lambda i, idx: (0, 0))],
        ),
        out_shape=[
            jax.ShapeDtypeStruct((D1, F1), F32),
            jax.ShapeDtypeStruct((F1, D1), F32),
            jax.ShapeDtypeStruct((D2, D1), F32),
            square, square, square, square, square, square,
            jax.ShapeDtypeStruct((1, D2), F32),
        ],
        input_output_aliases={2 + i: i for i in range(len(earlier))},
        compiler_params=params(),
        name="unpack",
    )(idx, src, *earlier)


GRP_AXES = ("zl", "x", "c")
DEV_AXES = ("zh", "y")
ZLXY = ("y", "zl", "x")


def exchange(x, axes):
    return lax.all_to_all(x, axes, split_axis=0, concat_axis=0, tiled=True)


def swap_cores(x):
    return lax.ppermute(x, "c", [(0, 1), (1, 0)])


def spread(x, n):
    return jnp.broadcast_to(x[None], (n,) + x.shape)


def add_pair(x, y):
    return (x.astype(F32) + y.astype(F32)).astype(x.dtype)


def add_over_zh(x):
    got = [lax.ppermute(x, "zh", [(i, i ^ k) for i in range(4)]) for k in (1, 2, 3)]
    a, b, c, d = [y.astype(F32) for y in (x, *got)]
    return ((a + b) + (c + d)).astype(x.dtype)


def add_up(x):
    return jnp.sum(x.astype(F32), axis=0).astype(x.dtype)


def body(
    patches, tissue, region_slide, w_up, w_down, w_embed, w_query, w_key, w_value, w_out,
    att_v, att_u, att_w, w_class, g_logits,
):
    grp = lax.axis_index(GRP_AXES)
    dev = lax.axis_index(DEV_AXES)
    core = lax.axis_index("c")
    first = (dev * GRP + grp) * OWN
    idx = jnp.stack([first, first % 8, first // 8, core, 1 - core, dev * GRP * OWN]).astype(jnp.int32)
    tokens = patches.reshape(-1, D1)
    att_row = att_w.reshape(1, D2)
    class_rows = w_class.T
    feat, mid = patch_forward(tokens, w_up, w_down, w_embed.T)
    wp, ap = gather_weights((w_query, w_key, w_value, w_out, att_v, att_u))
    got = exchange(feat.reshape(GRP, -1, D2), GRP_AXES)
    got = got.reshape(GRP, OWN, PATCH // GRP, D2)
    *kept, part = region_forward(idx, region_slide, got, tissue, wp, ap, att_row)
    z = exchange(part, DEV_AXES)
    df, grads, rows, cols, scalars = region_backward(
        idx, region_slide, tissue, wp, ap, att_row, class_rows, g_logits, kept
    )
    df = join_sums(z, scalars, df)
    hid, gp, turned = patch_slopes(rows, tokens, w_up)
    back = exchange(df.reshape(GRP, -1, PATCH), GRP_AXES).reshape(df.shape)
    mine, other, logits, g_class = patch_backward(
        idx, region_slide, back, turned, mid, hid, gp, w_embed.T, w_down, grads, rows,
        cols, class_rows, g_logits,
    )
    half = add_pair(mine, swap_cores(other))
    chunk = add_up(exchange(half.reshape(PEERS, -1, 128), ZLXY))
    chunk = add_over_zh(chunk)
    half = exchange(spread(chunk, PEERS), ZLXY).reshape(HALF_ROWS, 128)
    other = swap_cores(half)
    grads = unpack(idx, other, 4, unpack(idx, half, 3))
    up, down, embed, query, key, value, out, gv, gu, gw = grads
    return (
        logits, up, down, embed.T, query, key, value, out, gv, gu, gw.reshape(D2), g_class.T,
    )


def solution(mesh):
    fine = Mesh(mesh.devices.reshape(2, 4, 2, 4, 4), GRP_AXES + DEV_AXES)
    placed = (P(DEV_AXES, GRP_AXES, None),) + (P(),) * 14
    return jax.shard_map(
        body,
        mesh=fine,
        in_specs=placed,
        out_specs=(P(),) * 12,
        check_vma=False,
    )
```

```python
import math

import jax
import jax.numpy as jnp
from jax import lax
from jax.experimental import pallas as pl
from jax.experimental.pallas import tpu as pltpu
from jax.sharding import Mesh, PartitionSpec as P

D1 = 384
F1 = 1536
HEADS = 6
HEAD_DIM = 32
D2 = 192
PATCH = 256
SLIDES = 4
GRP = 16
OWN = 2
SCALE = 1.0 / math.sqrt(HEAD_DIM)
GELU_C = math.sqrt(2.0 / math.pi)
GELU_A = 0.044715

BF = jnp.bfloat16
F32 = jnp.float32
HIGHEST = lax.Precision.HIGHEST
MIB = 1024 * 1024

HALF_ROWS = 6144
DOWN_AT = 2304
REST_AT = 4608
REST_ROWS = 1152
EMBED_AT = REST_AT + REST_ROWS
PAD_AT = EMBED_AT + 288
PEERS = 32


def nn(a, b, precision=None):
    return jnp.dot(a, b, precision=precision, preferred_element_type=F32)


def nt(a, b, precision=None):
    return lax.dot_general(
        a, b, (((1,), (1,)), ((), ())), precision=precision, preferred_element_type=F32
    )


def tn(a, b, precision=None):
    return lax.dot_general(
        a, b, (((0,), (0,)), ((), ())), precision=precision, preferred_element_type=F32
    )


def params(mib=32):
    return pltpu.CompilerParams(vmem_limit_bytes=mib * MIB)


STEPS1 = 4
FB1 = F1 // STEPS1


def begin(copies):
    for copy in copies:
        copy.start()
    return copies


def patch_forward_kernel(x_ref, wu_ref, wd_ref, we_ref, feat_ref, mid_ref):
    x = x_ref[...]
    pre = nn(x, wu_ref[...])
    t = jnp.tanh(GELU_C * (pre + GELU_A * (pre * (pre * pre))))
    hid = (pre * (0.5 + 0.5 * t)).astype(BF)
    mid = (x.astype(F32) + nn(hid, wd_ref[...])).astype(BF)
    mid_ref[...] = mid
    feat_ref[...] = nt(mid, we_ref[...]).astype(BF)


def patch_forward(tokens, w_up, w_down, w_embed):
    rows = tokens.shape[0]
    vmem = pl.BlockSpec(memory_space=pltpu.VMEM)
    return pl.pallas_call(
        patch_forward_kernel,
        in_specs=[vmem] * 4,
        out_specs=[vmem] * 2,
        out_shape=[
            jax.ShapeDtypeStruct((rows, D2), BF),
            jax.ShapeDtypeStruct((rows, D1), BF),
        ],
        compiler_params=params(61),
        name="patch_forward",
    )(tokens, w_up, w_down, w_embed)


def patch_slopes_kernel(after_ref, x_ref, wu_ref, hid_ref, gp_ref, xt_ref):
    x = x_ref[...]

    @pl.when(pl.program_id(0) == 0)
    def _():
        xt_ref[...] = x.T

    pre = nn(x, wu_ref[...])
    sq = pre * pre
    t = jnp.tanh(GELU_C * (pre + GELU_A * (pre * sq)))
    half_up = 0.5 + 0.5 * t
    hid_ref[...] = (pre * half_up).astype(BF).T
    slope = (0.5 * GELU_C) * (1.0 - t * t) * (1.0 + (3.0 * GELU_A) * sq)
    gp_ref[...] = (half_up + pre * slope).astype(BF)


def patch_slopes(after, tokens, w_up):
    rows = tokens.shape[0]
    whole = lambda i: (0, 0)
    return pl.pallas_call(
        patch_slopes_kernel,
        grid=(STEPS1,),
        in_specs=[
            pl.BlockSpec(memory_space=pl.ANY),
            pl.BlockSpec((rows, D1), whole),
            pl.BlockSpec((D1, FB1), lambda i: (0, i)),
        ],
        out_specs=[
            pl.BlockSpec((FB1, rows), lambda i: (i, 0)),
            pl.BlockSpec((rows, FB1), lambda i: (0, i)),
            pl.BlockSpec((D1, rows), whole),
        ],
        out_shape=[
            pltpu.HBM((F1, rows), BF),
            pltpu.HBM((rows, F1), BF),
            pltpu.HBM((D1, rows), BF),
        ],
        compiler_params=params(61),
        cost_estimate=pl.CostEstimate(
            flops=3_000_000_000, bytes_accessed=12_000_000, transcendentals=0
        ),
        name="patch_slopes",
    )(after, tokens, w_up)


def gather_weights_kernel(*refs):
    ins, (wp_ref, ap_ref) = refs[:6], refs[6:]
    for i in range(4):
        wp_ref[i] = ins[i][...]
    for i in range(2):
        ap_ref[i] = ins[4 + i][...]


def gather_weights(weights):
    vm = pl.BlockSpec(memory_space=pltpu.VMEM)
    return pl.pallas_call(
        gather_weights_kernel,
        in_specs=[vm] * 6,
        out_specs=[vm] * 2,
        out_shape=[
            jax.ShapeDtypeStruct((4, D2, D2), BF),
            jax.ShapeDtypeStruct((2, D2, D2), F32),
        ],
        compiler_params=params(24),
        cost_estimate=pl.CostEstimate(
            flops=1_000_000_000, bytes_accessed=4_000_000, transcendentals=0
        ),
        name="gather_weights",
    )(*weights)


def tissue_row(idx_ref, tis_ref, r):
    return tis_ref[pl.ds(idx_ref[1] + r, 1), :].astype(F32)


def turned_row(row, width):
    return jnp.broadcast_to(row, (PATCH, row.shape[1])).T[:, :width]


def column_of(row, width):
    first = lax.broadcasted_iota(jnp.int32, (16, row.shape[1]), 0) == 0
    return tn(jnp.where(first, row, 0.0).astype(BF), jnp.ones((16, width), BF))


def head_mask(h, shape, dim):
    return (lax.broadcasted_iota(jnp.int32, shape, dim) // HEAD_DIM == h).astype(F32)


def region_forward_kernel(
    idx_ref, slide_ref, f_ref, tis_ref, wp_ref, ap_ref, aw_ref,
    p_ref, x_ref, asum_ref, reg_ref, tanh_ref, gate_ref, w_ref,
    part_ref,
):
    lane = lax.broadcasted_iota(jnp.int32, (8, PATCH), 1)
    reg_ref[...] = jnp.where(lane < D2, 0.0, 1.0)
    asum_ref[...] = jnp.zeros_like(asum_ref)
    for r in range(OWN):
        trow = tissue_row(idx_ref, tis_ref, r)
        tcol = turned_row(trow, D2)
        x = (f_ref[:, r].reshape(PATCH, D2).astype(F32) * tcol).astype(BF)
        q = nn(x, wp_ref[0]).astype(BF)
        k = nn(x, wp_ref[1])
        v = nn(x, wp_ref[2]).astype(BF)
        x_ref[r] = x
        spread = jnp.zeros((PATCH, D2), F32)
        for h in range(HEADS):
            mask = head_mask(h, (1, D2), 1)
            st = nt((k * mask).astype(BF), q) * SCALE
            top = jnp.max(st, axis=0, keepdims=True)
            ex = jnp.exp(st - top)
            total = jnp.sum(ex, axis=0, keepdims=True)
            pb = (ex * (1.0 / total)).astype(BF)
            p_ref[r, pl.ds(h * PATCH, PATCH), :] = pb
            spread = spread + nn(pb, (tcol * mask).astype(BF))
        asum = jnp.sum(spread * v.astype(F32), axis=0, keepdims=True)
        xsum = jnp.sum(x.astype(F32), axis=0, keepdims=True)
        count = jnp.maximum(jnp.sum(trow, axis=1, keepdims=True), 1.0)
        mixed = xsum + nn(jnp.broadcast_to(asum, (8, D2)), wp_ref[3].astype(F32), HIGHEST)[0:1]
        asum_ref[pl.ds(r, 1), :] = asum
        reg_ref[pl.ds(r, 1), pl.ds(0, D2)] = mixed / count

    region = reg_ref[:, pl.ds(0, D2)]
    tanh_part = jnp.tanh(nn(region, ap_ref[0], HIGHEST))
    gate_part = jax.nn.sigmoid(nn(region, ap_ref[1], HIGHEST))
    tanh_ref[...] = tanh_part
    gate_ref[...] = gate_part
    score = jnp.sum(tanh_part * gate_part * aw_ref[...], axis=1, keepdims=True)
    weight = jnp.exp(score)
    w_ref[...] = jnp.broadcast_to(weight, w_ref.shape)
    wide = reg_ref[...] * weight
    slot = lax.broadcasted_iota(jnp.int32, (SLIDES, 1), 0)
    sums = jnp.zeros((SLIDES, PATCH), F32)
    for i in range(OWN):
        own = (slot == slide_ref[idx_ref[0] + i]).astype(F32)
        sums = sums + own * wide[i : i + 1]
    both = jnp.concatenate([sums[:, :128], sums[:, 128:]], axis=0)
    part_ref[...] = jnp.broadcast_to(both[None], part_ref.shape)


def packed_specs():
    return [
        pl.BlockSpec((4, D2, D2), lambda r, *_: (0, 0, 0)),
        pl.BlockSpec((2, D2, D2), lambda r, *_: (0, 0, 0)),
    ]


def region_forward(idx, slide, got, tissue, wp, ap, att_w):
    row8 = lambda width: pl.BlockSpec((8, width), lambda r, *_: (0, 0))
    per_region = lambda rows, width: pl.BlockSpec((OWN, rows, width), lambda r, *_: (0, 0, 0))
    return pl.pallas_call(
        region_forward_kernel,
        grid_spec=pltpu.PrefetchScalarGridSpec(
            num_scalar_prefetch=2,
            grid=(1,),
            in_specs=[
                pl.BlockSpec((GRP, OWN, PATCH // GRP, D2), lambda r, *_: (0, 0, 0, 0)),
                pl.BlockSpec((8, PATCH), lambda r, idx, _: (idx[2], 0)),
                *packed_specs(),
                pl.BlockSpec((1, D2), lambda r, *_: (0, 0)),
            ],
            out_specs=[
                per_region(HEADS * PATCH, PATCH),
                per_region(PATCH, D2),
                row8(D2),
                row8(PATCH),
                row8(D2),
                row8(D2),
                row8(128),
                pl.BlockSpec((GRP, 8, 128), lambda r, *_: (0, 0, 0)),
            ],
        ),
        out_shape=[
            jax.ShapeDtypeStruct((OWN, HEADS * PATCH, PATCH), BF),
            jax.ShapeDtypeStruct((OWN, PATCH, D2), BF),
            jax.ShapeDtypeStruct((8, D2), F32),
            jax.ShapeDtypeStruct((8, PATCH), F32),
            jax.ShapeDtypeStruct((8, D2), F32),
            jax.ShapeDtypeStruct((8, D2), F32),
            jax.ShapeDtypeStruct((8, 128), F32),
            jax.ShapeDtypeStruct((GRP, 8, 128), F32),
        ],
        compiler_params=params(40),
        name="region_forward",
    )(idx, slide, got, tissue, wp, ap, att_w)


def directions(
    idx_ref, slide_ref, tis_ref, wp_ref, ap_ref, aw_ref, wc_ref, gl_ref,
    asum_ref, reg_ref, tanh_ref, gate_ref, w_ref, rows_ref, cols_ref, scal_ref,
):
    d_summary = nn(gl_ref[...], wc_ref[...], HIGHEST)
    slot = lax.broadcasted_iota(jnp.int32, (SLIDES, 1), 0)
    row = lax.broadcasted_iota(jnp.int32, (8, 1), 0)
    d_own = jnp.zeros((8, D2), F32)
    count = jnp.ones((8, 1), F32)
    for i in range(OWN):
        mine = slot == slide_ref[idx_ref[0] + i]
        d_own = jnp.where(
            row == i, jnp.sum(jnp.where(mine, d_summary, 0.0), axis=0, keepdims=True), d_own
        )
        t_i = tissue_row(idx_ref, tis_ref, i)
        count = jnp.where(row == i, jnp.maximum(jnp.sum(t_i, axis=1, keepdims=True), 1.0), count)
    region = reg_ref[:, pl.ds(0, D2)]
    tanh_part = tanh_ref[...]
    gate_part = gate_ref[...]
    pre_v = aw_ref[...] * gate_part * (1.0 - tanh_part * tanh_part)
    pre_u = aw_ref[...] * tanh_part * gate_part * (1.0 - gate_part)
    second = nt(pre_v, ap_ref[0], HIGHEST) + nt(pre_u, ap_ref[1], HIGHEST)
    own = jnp.sum(d_own * region, axis=1, keepdims=True)
    dm = (d_own / count, second / count)
    kept = (
        pre_v, pre_u, dm[0], dm[1],
        jnp.broadcast_to(w_ref[:, 0:1], (8, D2)), jnp.broadcast_to(own, (8, D2)),
        nt(dm[0].astype(BF), wp_ref[3]), nt(dm[1].astype(BF), wp_ref[3]),
    )
    for i, value in enumerate(kept):
        rows_ref[pl.ds(8 * i, 8), :] = value
    turned = jnp.concatenate(
        [region, asum_ref[...], tanh_part * gate_part, jnp.zeros((104, D2), F32)], axis=0
    )
    cols_ref[...] = turned.T
    lane = lax.broadcasted_iota(jnp.int32, (1, PATCH), 1) // 64
    scalars = jnp.zeros((1, PATCH), F32)
    for i in range(OWN):
        scalars = jnp.where(lane == 2 * i, w_ref[i : i + 1, 0:1], scalars)
        scalars = jnp.where(lane == 2 * i + 1, own[i : i + 1], scalars)
    scal_ref[...] = jnp.broadcast_to(scalars, (8, PATCH))


def pull_back(idx_ref, tis_ref, wp_ref, p_ref, x_ref, rows_ref, df_ref, grad_ref, kt_s, dqt_s):
    regions = range(OWN)
    pairs = [(r, j) for r in regions for j in range(2)]
    trow = [tissue_row(idx_ref, tis_ref, r) for r in regions]
    tcol = [column_of(row, D2) for row in trow]
    x = [x_ref[r] for r in regions]
    q = [nn(x[r], wp_ref[0]).astype(BF).astype(F32) for r in regions]
    v = [nn(x[r], wp_ref[2]).astype(BF) for r in regions]
    for r in regions:
        kt_s[r] = lax.dot_general(
            wp_ref[1], x[r], (((0,), (1,)), ((), ())), preferred_element_type=F32
        ).astype(BF)
    dm = {(r, j): rows_ref[pl.ds(8 * (2 + j) + r, 1), :] for r, j in pairs}
    da = {
        (r, j): rows_ref[pl.ds(8 * (6 + j) + r, 1), :].astype(BF).astype(F32) for r, j in pairs
    }
    row = lax.broadcasted_iota(jnp.int32, (16, D2), 0)
    head = lax.broadcasted_iota(jnp.int32, (16, D2), 1) // HEAD_DIM
    e = []
    for r in regions:
        by_head = jnp.where(row // 2 == head, jnp.where(row % 2 == 0, da[r, 0], da[r, 1]), 0.0)
        e.append(nt(by_head.astype(BF), v[r]).T)
    spread = [jnp.zeros((PATCH, D2), F32) for _ in regions]
    dk = {pair: jnp.zeros((PATCH, D2), F32) for pair in pairs}
    for h in range(HEADS):
        mask = head_mask(h, (1, D2), 1)
        rows = pl.ds(h * HEAD_DIM, HEAD_DIM)
        for r in regions:
            pb = p_ref[r, pl.ds(h * PATCH, PATCH), :]
            pt = pb.astype(F32)
            spread[r] = spread[r] + nn(pb, (tcol[r] * mask).astype(BF))
            q_head = (q[r] * mask).astype(BF)
            k_head = kt_s[r, rows, :]
            for j in range(2):
                pe = pt * e[r][:, 2 * h + j : 2 * h + j + 1]
                ds = (pe - pt * jnp.sum(pe, axis=0, keepdims=True)).astype(BF)
                dk[r, j] = dk[r, j] + nn(ds, q_head)
                dqt_s[r, j, rows, :] = nn(k_head, ds)
    xt = [x[r].T for r in regions]
    flat = {}
    for r, j in pairs:
        dq = (dqt_s[r, j] * (trow[r] * SCALE)).astype(BF).T
        dk_j = (dk[r, j] * SCALE).astype(BF)
        dv = (spread[r] * da[r, j]).astype(BF)
        grad_ref[r, 0, j] = nn(xt[r], dq)
        grad_ref[r, 1, j] = nn(xt[r], dk_j)
        grad_ref[r, 2, j] = nn(xt[r], dv)
        d_flat = dm[r, j] + nt(dq, wp_ref[0]) + nt(dk_j, wp_ref[1]) + nt(dv, wp_ref[2])
        flat[r, j] = tcol[r] * d_flat
    for r in regions:
        both = jnp.concatenate([flat[r, 0], flat[r, 1]], axis=1).astype(BF)
        df_ref[:, r] = both.reshape(GRP, PATCH // GRP, 2 * D2)


WIDE = 2 * D2 + 128


def region_backward_kernel(
    idx_ref, slide_ref, tis_ref, wp_ref, ap_ref, aw_ref, wc_ref, gl_ref,
    p_ref, x_ref, asum_ref, reg_ref, tanh_ref, gate_ref, w_ref,
    df_ref, grad_ref, rows_ref, cols_ref, scal_ref,
    kt_s, dqt_s,
):
    directions(
        idx_ref, slide_ref, tis_ref, wp_ref, ap_ref, aw_ref, wc_ref, gl_ref,
        asum_ref, reg_ref, tanh_ref, gate_ref, w_ref, rows_ref, cols_ref, scal_ref,
    )
    pull_back(idx_ref, tis_ref, wp_ref, p_ref, x_ref, rows_ref, df_ref, grad_ref, kt_s, dqt_s)


def region_backward(idx, slide, tissue, wp, ap, att_w, w_class, g_logits, kept):
    whole = lambda rows, width: pl.BlockSpec((rows, width), lambda r, *_: (0, 0))
    region = lambda rows, width: pl.BlockSpec((OWN, rows, width), lambda r, *_: (0, 0, 0))
    return pl.pallas_call(
        region_backward_kernel,
        grid_spec=pltpu.PrefetchScalarGridSpec(
            num_scalar_prefetch=2,
            grid=(1,),
            in_specs=[
                pl.BlockSpec((8, PATCH), lambda r, idx, _: (idx[2], 0)),
                *packed_specs(),
                whole(1, D2), whole(3, D2), whole(SLIDES, 3),
                region(HEADS * PATCH, PATCH),
                region(PATCH, D2),
                whole(8, D2), whole(8, PATCH), whole(8, D2), whole(8, D2), whole(8, 128),
            ],
            out_specs=[
                pl.BlockSpec((GRP, OWN, PATCH // GRP, 2 * D2), lambda r, *_: (0, 0, 0, 0)),
                pl.BlockSpec((OWN, 3, 2, D2, D2), lambda r, *_: (0, 0, 0, 0, 0)),
                whole(64, D2),
                whole(D2, 128),
                whole(8, PATCH),
            ],
            scratch_shapes=[
                pltpu.VMEM((OWN, D2, PATCH), BF),
                pltpu.VMEM((OWN, 2, D2, PATCH), F32),
            ],
        ),
        out_shape=[
            pltpu.HBM((GRP, OWN, PATCH // GRP, WIDE), BF),
            pltpu.HBM((OWN, 3, 2, D2, D2), F32),
            pltpu.HBM((64, D2), F32),
            pltpu.HBM((D2, 128), F32),
            jax.ShapeDtypeStruct((8, PATCH), F32),
        ],
        compiler_params=params(40),
        cost_estimate=pl.CostEstimate(
            flops=4_000_000_000, bytes_accessed=20_000_000, transcendentals=0
        ),
        name="region_backward",
    )(idx, slide, tissue, wp, ap, att_w, w_class, g_logits, *kept)


def split_three(x):
    parts = []
    for _ in range(3):
        top = x.astype(BF).astype(F32)
        parts.append(top)
        x = x - top
    return parts


def join_sums_kernel(z_ref, scal_ref, df_ref, out_ref, ext, wide, sem):
    z = jnp.sum(z_ref[...], axis=0)
    z = jnp.concatenate([z[0:SLIDES], z[SLIDES:]], axis=1)
    ext[...] = jnp.zeros_like(ext)
    for i, (part, tops) in enumerate(zip(split_three(z), split_three(scal_ref[0:1]))):
        ext[pl.ds(4 * i, 4), :] = part
        ext[pl.ds(12 + i, 1), :] = tops
    for i in range(OWN):
        block = ext[:, pl.ds(128 * i, 128)].astype(BF)
        wide[:, i] = jnp.broadcast_to(block[None], (GRP, 16, 128))
    copy = pltpu.make_async_copy(wide, out_ref.at[:, :, :, pl.ds(2 * D2, 128)], sem)
    copy.start()
    copy.wait()


def join_sums(z, scalars, df):
    return pl.pallas_call(
        join_sums_kernel,
        in_specs=[pl.BlockSpec(memory_space=pltpu.VMEM)] * 2
        + [pl.BlockSpec(memory_space=pl.ANY)],
        out_specs=pl.BlockSpec(memory_space=pl.ANY),
        out_shape=pltpu.HBM(df.shape, df.dtype),
        scratch_shapes=[
            pltpu.VMEM((16, PATCH), F32),
            pltpu.VMEM((GRP, OWN, 16, 128), BF),
            pltpu.SemaphoreType.DMA,
        ],
        input_output_aliases={2: 0},
        compiler_params=params(24),
        name="join_sums",
    )(z, scalars, df)


def put_rest(pack, slot, grad, fill=None):
    at = REST_AT + 192 * slot
    if not isinstance(slot, int):
        at = pl.multiple_of(at, 64)
    for half in range(2):
        rows = grad[96 * half : 96 * half + 96]
        pack[half, pl.ds(at, 96), :] = rows[:, :128].astype(BF)
        tail = jnp.zeros((96, 64), F32) if fill is None else fill
        high = jnp.concatenate([rows[:, 128:], tail], axis=1)
        pack[half, pl.ds(at + 96, 96), :] = high.astype(BF)


def finish_slides(
    idx_ref, slide_ref, back_ref, rows_ref, cols_ref, wc_ref, gl_ref, logits_ref, gc_ref,
    df_s, pq_s, pack,
):
    ext = [back_ref[:, i, :, pl.ds(2 * D2, 128)].astype(F32) for i in range(OWN)]
    ext = jnp.concatenate(ext, axis=2)
    sums = jnp.sum(ext, axis=0)
    sums = sums[0:4] + sums[4:8] + sums[8:12]
    total = sums[:, D2 : D2 + 1]
    summary = sums[:, :D2] / total
    wc = wc_ref[...]
    gl = gl_ref[...]
    logits_ref[...] = nt(summary, wc, HIGHEST)
    gc_ref[...] = tn(gl, summary, HIGHEST)
    along = jnp.sum(nn(gl, wc, HIGHEST) * summary, axis=1, keepdims=True)

    def of_slide(column, s):
        out = column[SLIDES - 1 : SLIDES]
        for i in range(SLIDES - 1):
            out = jnp.where(s == i, column[i : i + 1], out)
        return out

    def factors(w, a, s):
        share = w / of_slide(total, s)
        return share, share * (a - of_slide(along, s))

    for src in range(GRP):
        scalars = ext[src, 12:13] + ext[src, 13:14] + ext[src, 14:15]
        for i in range(OWN):
            w = scalars[:, 128 * i : 128 * i + 1]
            a = scalars[:, 128 * i + 64 : 128 * i + 65]
            p, q = factors(w, a, slide_ref[idx_ref[5] + OWN * src + i])
            f = back_ref[src, i].astype(F32)
            rows = p * f[:, :D2] + q * f[:, D2 : 2 * D2]
            df_s[pl.ds(32 * src + 16 * i, 16), :] = rows.astype(BF)

    kept = [rows_ref[pl.ds(8 * i, 8), :] for i in range(6)]
    pre_v, pre_u, dm0, dm1, w_own, a_own = kept
    row = lax.broadcasted_iota(jnp.int32, (8, 1), 0)
    p_own = jnp.zeros((8, 1), F32)
    q_own = jnp.zeros((8, 1), F32)
    for i in range(OWN):
        p, q = factors(w_own[i : i + 1, 0:1], a_own[i : i + 1, 0:1], slide_ref[idx_ref[0] + i])
        p_own = jnp.where(row == i, p, p_own)
        q_own = jnp.where(row == i, q, q_own)
    pq_s[0] = jnp.broadcast_to(p_own, (8, 128))
    pq_s[1] = jnp.broadcast_to(q_own, (8, 128))

    def outer(at, rows):
        out = cols_ref[:, at : at + 1] * rows[0:1]
        return out + cols_ref[:, at + 1 : at + 2] * rows[1:2]

    put_rest(pack, 3, outer(8, p_own * dm0 + q_own * dm1))
    put_rest(pack, 4, outer(0, q_own * pre_v))
    g_aw = outer(16, jnp.broadcast_to(q_own, (8, 64)))
    lane = lax.broadcasted_iota(jnp.int32, (96, 64), 1)
    put_rest(pack, 5, outer(0, q_own * pre_u), jnp.where(lane == 0, g_aw[:96], g_aw[96:]))


def patch_backward_kernel(
    idx_ref, slide_ref, back_in, xt_in, mid_in, hid_in, gp_in, we_in, wd_in, grad_in,
    rows_ref, cols_ref, wc_ref, gl_ref,
    mine_ref, other_ref, logits_ref, gc_ref,
    back_ref, xt_ref, mid_ref, hid_ref, gp_ref, we_ref, wd_ref, grad_ref,
    pack, df_s, pq_s, in_sems, sems,
):
    core = idx_ref[3]
    pairs = (
        (back_in, back_ref), (we_in, we_ref), (wd_in, wd_ref), (gp_in, gp_ref), (xt_in, xt_ref),
        (hid_in, hid_ref), (mid_in, mid_ref), (grad_in, grad_ref),
    )
    fetch = [pltpu.make_async_copy(a, b, in_sems.at[i]) for i, (a, b) in enumerate(pairs)]
    begin(fetch)
    sent = []

    def send(low, size):
        rows = pl.ds(low, size)
        at = len(sent)
        sent.extend(
            begin(
                [
                    pltpu.make_async_copy(
                        pack.at[core, rows], mine_ref.at[rows], sems.at[at]
                    ),
                    pltpu.make_async_copy(
                        pack.at[1 - core, rows], other_ref.at[rows], sems.at[at + 1]
                    ),
                ]
            )
        )

    fetch[0].wait()
    finish_slides(
        idx_ref, slide_ref, back_ref, rows_ref, cols_ref, wc_ref, gl_ref, logits_ref, gc_ref,
        df_s, pq_s, pack,
    )
    df = df_s[...]
    fetch[1].wait()
    dmid = nn(df, we_ref[...]).astype(BF)
    for i in range(2, 5):
        fetch[i].wait()
    d_pre = (nt(dmid, wd_ref[...]) * gp_ref[...].astype(F32)).astype(BF)
    g_up = nn(xt_ref[...], d_pre).astype(BF)
    for l in range(F1 // 128):
        for half in range(2):
            block = g_up[192 * half : 192 * half + 192, 128 * l : 128 * l + 128]
            pack[half, pl.ds(192 * l, 192), :] = block
    send(0, DOWN_AT)
    fetch[5].wait()
    g_down = nn(hid_ref[...], dmid).astype(BF)
    for half in range(2):
        for l in range(3):
            block = g_down[768 * half : 768 * half + 768, 128 * l : 128 * l + 128]
            pack[half, pl.ds(DOWN_AT + 768 * l, 768), :] = block
    send(DOWN_AT, REST_AT - DOWN_AT)
    fetch[6].wait()
    g_embed = tn(df, mid_ref[...]).astype(BF)
    for half in range(2):
        for l in range(3):
            block = g_embed[96 * half : 96 * half + 96, 128 * l : 128 * l + 128]
            pack[half, pl.ds(EMBED_AT + 96 * l, 96), :] = block
        pack[half, pl.ds(PAD_AT, 96), :] = jnp.zeros((96, 128), BF)
    fetch[7].wait()
    for slot in range(3):
        grad = jnp.zeros((D2, D2), F32)
        for i in range(OWN):
            for j in range(2):
                grad = grad + pq_s[j, i : i + 1, 0:1] * grad_ref[i, slot, j]
        put_rest(pack, slot, grad)
    send(REST_AT, HALF_ROWS - REST_AT)
    for copy in sent:
        copy.wait()


def patch_backward(
    idx, slide, back, turned, mid, hid, gp, w_embed, w_down, grads, rows, cols, w_class, g_logits
):
    hbm = pl.BlockSpec(memory_space=pl.ANY)
    vmem = pl.BlockSpec(memory_space=pltpu.VMEM)
    smem = pl.BlockSpec(memory_space=pltpu.SMEM)
    big = (back, turned, mid, hid, gp, w_embed, w_down, grads)
    return pl.pallas_call(
        patch_backward_kernel,
        in_specs=[smem] * 2 + [hbm] * 8 + [vmem] * 4,
        out_specs=[hbm] * 2 + [vmem] * 2,
        out_shape=[
            jax.ShapeDtypeStruct((HALF_ROWS, 128), BF),
            jax.ShapeDtypeStruct((HALF_ROWS, 128), BF),
            jax.ShapeDtypeStruct((SLIDES, 3), F32),
            jax.ShapeDtypeStruct((3, D2), F32),
        ],
        scratch_shapes=[pltpu.VMEM(a.shape, a.dtype) for a in big]
        + [
            pltpu.VMEM((2, HALF_ROWS, 128), BF),
            pltpu.VMEM((turned.shape[1], D2), BF),
            pltpu.VMEM((2, 8, 128), F32),
            pltpu.SemaphoreType.DMA((8,)),
            pltpu.SemaphoreType.DMA((6,)),
        ],
        compiler_params=params(61),
        name="patch_backward",
    )(idx, slide, *big, rows, cols, w_class, g_logits)


def unpack_kernel(idx_ref, src_ref, *refs):
    up_ref, down_ref, embed_ref, q_ref, k_ref, v_ref, o_ref, av_ref, au_ref, aw_ref = refs[-10:]
    for l in range(12):
        up_ref[:, pl.ds(128 * l, 128)] = src_ref[pl.ds(192 * l, 192), :].astype(F32)
    for l in range(3):
        rows = src_ref[pl.ds(DOWN_AT + 768 * l, 768), :]
        down_ref[:, pl.ds(128 * l, 128)] = rows.astype(F32)
    for slot, ref in enumerate((q_ref, k_ref, v_ref, o_ref, av_ref, au_ref)):
        at = REST_AT + 192 * slot
        ref[:, pl.ds(0, 128)] = src_ref[pl.ds(at, 96), :].astype(F32)
        ref[:, pl.ds(128, 64)] = src_ref[pl.ds(at + 96, 96), :][:, :64].astype(F32)
    for l in range(3):
        embed_ref[:, pl.ds(128 * l, 128)] = src_ref[pl.ds(EMBED_AT + 96 * l, 96), :].astype(F32)
    tail = src_ref[pl.ds(EMBED_AT - 96, 96), :].astype(F32).T
    aw_ref[:, pl.ds(0, 96)] = tail[64:65, :]
    aw_ref[:, pl.ds(96, 96)] = tail[65:66, :]


def unpack(idx, src, which, earlier=()):
    square = jax.ShapeDtypeStruct((D2, D2), F32)
    half = lambda rows, width: pl.BlockSpec((rows, width), lambda i, idx: (idx[which], 0))
    hbm = pl.BlockSpec(memory_space=pltpu.HBM)
    return pl.pallas_call(
        unpack_kernel,
        grid_spec=pltpu.PrefetchScalarGridSpec(
            num_scalar_prefetch=1,
            grid=(1,),
            in_specs=[pl.BlockSpec((HALF_ROWS, 128), lambda i, idx: (0, 0))] + [hbm] * len(earlier),
            out_specs=[
                half(D1 // 2, F1),
                half(F1 // 2, D1),
                half(D2 // 2, D1),
            ]
            + [half(D2 // 2, D2)] * 6
            + [pl.BlockSpec((1, D2), lambda i, idx: (0, 0))],
        ),
        out_shape=[
            jax.ShapeDtypeStruct((D1, F1), F32),
            jax.ShapeDtypeStruct((F1, D1), F32),
            jax.ShapeDtypeStruct((D2, D1), F32),
            square, square, square, square, square, square,
            jax.ShapeDtypeStruct((1, D2), F32),
        ],
        input_output_aliases={2 + i: i for i in range(len(earlier))},
        compiler_params=params(),
        name="unpack",
    )(idx, src, *earlier)


GRP_AXES = ("zl", "x", "c")
DEV_AXES = ("zh", "y")
ZLXY = ("y", "zl", "x")


def exchange(x, axes):
    return lax.all_to_all(x, axes, split_axis=0, concat_axis=0, tiled=True)


def swap_cores(x):
    return lax.ppermute(x, "c", [(0, 1), (1, 0)])


def spread(x, n):
    return jnp.broadcast_to(x[None], (n,) + x.shape)


def add_pair(x, y):
    return (x.astype(F32) + y.astype(F32)).astype(x.dtype)


def add_over_zh(x):
    got = [lax.ppermute(x, "zh", [(i, i ^ k) for i in range(4)]) for k in (1, 2, 3)]
    a, b, c, d = [y.astype(F32) for y in (x, *got)]
    return ((a + b) + (c + d)).astype(x.dtype)


def add_up(x):
    return jnp.sum(x.astype(F32), axis=0).astype(x.dtype)


def body(
    patches, tissue, region_slide, w_up, w_down, w_embed, w_query, w_key, w_value, w_out,
    att_v, att_u, att_w, w_class, g_logits,
):
    grp = lax.axis_index(GRP_AXES)
    dev = lax.axis_index(DEV_AXES)
    core = lax.axis_index("c")
    first = (dev * GRP + grp) * OWN
    idx = jnp.stack([first, first % 8, first // 8, core, 1 - core, dev * GRP * OWN]).astype(jnp.int32)
    tokens = patches.reshape(-1, D1)
    att_row = att_w.reshape(1, D2)
    class_rows = w_class.T
    feat, mid = patch_forward(tokens, w_up, w_down, w_embed.T)
    wp, ap = gather_weights((w_query, w_key, w_value, w_out, att_v, att_u))
    got = exchange(feat.reshape(GRP, -1, D2), GRP_AXES)
    got = got.reshape(GRP, OWN, PATCH // GRP, D2)
    *kept, part = region_forward(idx, region_slide, got, tissue, wp, ap, att_row)
    z = exchange(part, DEV_AXES)
    df, grads, rows, cols, scalars = region_backward(
        idx, region_slide, tissue, wp, ap, att_row, class_rows, g_logits, kept
    )
    df = join_sums(z, scalars, df)
    hid, gp, turned = patch_slopes(rows, tokens, w_up)
    back = exchange(df.reshape(GRP, -1, WIDE), GRP_AXES).reshape(df.shape)
    mine, other, logits, g_class = patch_backward(
        idx, region_slide, back, turned, mid, hid, gp, w_embed.T, w_down, grads, rows,
        cols, class_rows, g_logits,
    )
    half = add_pair(mine, swap_cores(other))
    chunk = add_up(exchange(half.reshape(PEERS, -1, 128), ZLXY))
    chunk = add_over_zh(chunk)
    half = exchange(spread(chunk, PEERS), ZLXY).reshape(HALF_ROWS, 128)
    other = swap_cores(half)
    grads = unpack(idx, other, 4, unpack(idx, half, 3))
    up, down, embed, query, key, value, out, gv, gu, gw = grads
    return (
        logits, up, down, embed.T, query, key, value, out, gv, gu, gw.reshape(D2), g_class.T,
    )


def solution(mesh):
    fine = Mesh(mesh.devices.reshape(2, 4, 2, 4, 4), GRP_AXES + DEV_AXES)
    placed = (P(DEV_AXES, GRP_AXES, None),) + (P(),) * 14
    return jax.shard_map(
        body,
        mesh=fine,
        in_specs=placed,
        out_specs=(P(),) * 12,
        check_vma=False,
    )
```

```python
import math

import jax
import jax.numpy as jnp
from jax import lax
from jax.experimental import pallas as pl
from jax.experimental.pallas import tpu as pltpu
from jax.sharding import Mesh, PartitionSpec as P

D1 = 384
F1 = 1536
HEADS = 6
HEAD_DIM = 32
D2 = 192
PATCH = 256
SLIDES = 4
GRP = 16
OWN = 2
SCALE = 1.0 / math.sqrt(HEAD_DIM)
GELU_C = math.sqrt(2.0 / math.pi)
GELU_A = 0.044715

BF = jnp.bfloat16
F32 = jnp.float32
HIGHEST = lax.Precision.HIGHEST
MIB = 1024 * 1024

HALF_ROWS = 6144
DOWN_AT = 2304
REST_AT = 4608
REST_ROWS = 1152
EMBED_AT = REST_AT + REST_ROWS
PAD_AT = EMBED_AT + 288
PEERS = 32


def nn(a, b, precision=None):
    return jnp.dot(a, b, precision=precision, preferred_element_type=F32)


def nt(a, b, precision=None):
    return lax.dot_general(
        a, b, (((1,), (1,)), ((), ())), precision=precision, preferred_element_type=F32
    )


def tn(a, b, precision=None):
    return lax.dot_general(
        a, b, (((0,), (0,)), ((), ())), precision=precision, preferred_element_type=F32
    )


def params(mib=32):
    return pltpu.CompilerParams(vmem_limit_bytes=mib * MIB)


STEPS1 = 4
FB1 = F1 // STEPS1


def begin(copies):
    for copy in copies:
        copy.start()
    return copies


def patch_forward_kernel(x_ref, wu_ref, wd_ref, we_ref, feat_ref, mid_ref):
    x = x_ref[...]
    pre = nn(x, wu_ref[...])
    t = jnp.tanh(GELU_C * (pre + GELU_A * (pre * (pre * pre))))
    hid = (pre * (0.5 + 0.5 * t)).astype(BF)
    mid = (x.astype(F32) + nn(hid, wd_ref[...])).astype(BF)
    mid_ref[...] = mid
    feat_ref[...] = nt(mid, we_ref[...]).astype(BF)


def patch_forward(tokens, w_up, w_down, w_embed):
    rows = tokens.shape[0]
    vmem = pl.BlockSpec(memory_space=pltpu.VMEM)
    return pl.pallas_call(
        patch_forward_kernel,
        in_specs=[vmem] * 4,
        out_specs=[vmem] * 2,
        out_shape=[
            jax.ShapeDtypeStruct((rows, D2), BF),
            jax.ShapeDtypeStruct((rows, D1), BF),
        ],
        compiler_params=params(61),
        name="patch_forward",
    )(tokens, w_up, w_down, w_embed)


def patch_slopes_kernel(after_ref, x_ref, wu_ref, hid_ref, gp_ref, xt_ref):
    x = x_ref[...]

    @pl.when(pl.program_id(0) == 0)
    def _():
        xt_ref[...] = x.T

    pre = nn(x, wu_ref[...])
    sq = pre * pre
    t = jnp.tanh(GELU_C * (pre + GELU_A * (pre * sq)))
    half_up = 0.5 + 0.5 * t
    hid_ref[...] = (pre * half_up).astype(BF).T
    slope = (0.5 * GELU_C) * (1.0 - t * t) * (1.0 + (3.0 * GELU_A) * sq)
    gp_ref[...] = (half_up + pre * slope).astype(BF)


def patch_slopes(after, tokens, w_up):
    rows = tokens.shape[0]
    whole = lambda i: (0, 0)
    return pl.pallas_call(
        patch_slopes_kernel,
        grid=(STEPS1,),
        in_specs=[
            pl.BlockSpec(memory_space=pl.ANY),
            pl.BlockSpec((rows, D1), whole),
            pl.BlockSpec((D1, FB1), lambda i: (0, i)),
        ],
        out_specs=[
            pl.BlockSpec((FB1, rows), lambda i: (i, 0)),
            pl.BlockSpec((rows, FB1), lambda i: (0, i)),
            pl.BlockSpec((D1, rows), whole),
        ],
        out_shape=[
            pltpu.HBM((F1, rows), BF),
            pltpu.HBM((rows, F1), BF),
            pltpu.HBM((D1, rows), BF),
        ],
        compiler_params=params(61),
        cost_estimate=pl.CostEstimate(
            flops=3_000_000_000, bytes_accessed=12_000_000, transcendentals=0
        ),
        name="patch_slopes",
    )(after, tokens, w_up)


def gather_weights_kernel(*refs):
    ins, (wp_ref, ap_ref) = refs[:6], refs[6:]
    for i in range(4):
        wp_ref[i] = ins[i][...]
    for i in range(2):
        ap_ref[i] = ins[4 + i][...]


def gather_weights(weights):
    vm = pl.BlockSpec(memory_space=pltpu.VMEM)
    return pl.pallas_call(
        gather_weights_kernel,
        in_specs=[vm] * 6,
        out_specs=[vm] * 2,
        out_shape=[
            jax.ShapeDtypeStruct((4, D2, D2), BF),
            jax.ShapeDtypeStruct((2, D2, D2), F32),
        ],
        compiler_params=params(24),
        cost_estimate=pl.CostEstimate(
            flops=1_000_000_000, bytes_accessed=4_000_000, transcendentals=0
        ),
        name="gather_weights",
    )(*weights)


def tissue_row(idx_ref, tis_ref, r):
    return tis_ref[pl.ds(idx_ref[1] + r, 1), :].astype(F32)


def turned_row(row, width):
    return jnp.broadcast_to(row, (PATCH, row.shape[1])).T[:, :width]


def column_of(row, width):
    first = lax.broadcasted_iota(jnp.int32, (16, row.shape[1]), 0) == 0
    return tn(jnp.where(first, row, 0.0).astype(BF), jnp.ones((16, width), BF))


def head_mask(h, shape, dim):
    return (lax.broadcasted_iota(jnp.int32, shape, dim) // HEAD_DIM == h).astype(F32)


def region_forward_kernel(
    idx_ref, slide_ref, f_ref, tis_ref, wp_ref, ap_ref, aw_ref,
    p_ref, x_ref, asum_ref, reg_ref, tanh_ref, gate_ref, w_ref,
    part_ref,
):
    lane = lax.broadcasted_iota(jnp.int32, (8, PATCH), 1)
    reg_ref[...] = jnp.where(lane < D2, 0.0, 1.0)
    asum_ref[...] = jnp.zeros_like(asum_ref)
    for r in range(OWN):
        trow = tissue_row(idx_ref, tis_ref, r)
        tcol = turned_row(trow, D2)
        x = (f_ref[:, r].reshape(PATCH, D2).astype(F32) * tcol).astype(BF)
        q = nn(x, wp_ref[0]).astype(BF)
        k = nn(x, wp_ref[1])
        v = nn(x, wp_ref[2]).astype(BF)
        x_ref[r] = x
        spread = jnp.zeros((PATCH, D2), F32)
        for h in range(HEADS):
            mask = head_mask(h, (1, D2), 1)
            st = nt((k * mask).astype(BF), q) * SCALE
            top = jnp.max(st, axis=0, keepdims=True)
            ex = jnp.exp(st - top)
            total = jnp.sum(ex, axis=0, keepdims=True)
            pb = (ex * (1.0 / total)).astype(BF)
            p_ref[r, pl.ds(h * PATCH, PATCH), :] = pb
            spread = spread + nn(pb, (tcol * mask).astype(BF))
        asum = jnp.sum(spread * v.astype(F32), axis=0, keepdims=True)
        xsum = jnp.sum(x.astype(F32), axis=0, keepdims=True)
        count = jnp.maximum(jnp.sum(trow, axis=1, keepdims=True), 1.0)
        mixed = xsum + nn(jnp.broadcast_to(asum, (8, D2)), wp_ref[3].astype(F32), HIGHEST)[0:1]
        asum_ref[pl.ds(r, 1), :] = asum
        reg_ref[pl.ds(r, 1), pl.ds(0, D2)] = mixed / count

    region = reg_ref[:, pl.ds(0, D2)]
    tanh_part = jnp.tanh(nn(region, ap_ref[0], HIGHEST))
    gate_part = jax.nn.sigmoid(nn(region, ap_ref[1], HIGHEST))
    tanh_ref[...] = tanh_part
    gate_ref[...] = gate_part
    score = jnp.sum(tanh_part * gate_part * aw_ref[...], axis=1, keepdims=True)
    weight = jnp.exp(score)
    w_ref[...] = jnp.broadcast_to(weight, w_ref.shape)
    wide = reg_ref[...] * weight
    slot = lax.broadcasted_iota(jnp.int32, (SLIDES, 1), 0)
    sums = jnp.zeros((SLIDES, PATCH), F32)
    for i in range(OWN):
        own = (slot == slide_ref[idx_ref[0] + i]).astype(F32)
        sums = sums + own * wide[i : i + 1]
    both = jnp.concatenate([sums[:, :128], sums[:, 128:]], axis=0)
    part_ref[...] = jnp.broadcast_to(both[None], part_ref.shape)


def packed_specs():
    return [
        pl.BlockSpec((4, D2, D2), lambda r, *_: (0, 0, 0)),
        pl.BlockSpec((2, D2, D2), lambda r, *_: (0, 0, 0)),
    ]


def region_forward(idx, slide, got, tissue, wp, ap, att_w):
    row8 = lambda width: pl.BlockSpec((8, width), lambda r, *_: (0, 0))
    per_region = lambda rows, width: pl.BlockSpec((OWN, rows, width), lambda r, *_: (0, 0, 0))
    return pl.pallas_call(
        region_forward_kernel,
        grid_spec=pltpu.PrefetchScalarGridSpec(
            num_scalar_prefetch=2,
            grid=(1,),
            in_specs=[
                pl.BlockSpec((GRP, OWN, PATCH // GRP, D2), lambda r, *_: (0, 0, 0, 0)),
                pl.BlockSpec((8, PATCH), lambda r, idx, _: (idx[2], 0)),
                *packed_specs(),
                pl.BlockSpec((1, D2), lambda r, *_: (0, 0)),
            ],
            out_specs=[
                per_region(HEADS * PATCH, PATCH),
                per_region(PATCH, D2),
                row8(D2),
                row8(PATCH),
                row8(D2),
                row8(D2),
                row8(128),
                pl.BlockSpec((GRP, 8, 128), lambda r, *_: (0, 0, 0)),
            ],
        ),
        out_shape=[
            jax.ShapeDtypeStruct((OWN, HEADS * PATCH, PATCH), BF),
            jax.ShapeDtypeStruct((OWN, PATCH, D2), BF),
            jax.ShapeDtypeStruct((8, D2), F32),
            jax.ShapeDtypeStruct((8, PATCH), F32),
            jax.ShapeDtypeStruct((8, D2), F32),
            jax.ShapeDtypeStruct((8, D2), F32),
            jax.ShapeDtypeStruct((8, 128), F32),
            jax.ShapeDtypeStruct((GRP, 8, 128), F32),
        ],
        compiler_params=params(40),
        name="region_forward",
    )(idx, slide, got, tissue, wp, ap, att_w)


def directions(
    idx_ref, slide_ref, tis_ref, wp_ref, ap_ref, aw_ref, wc_ref, gl_ref,
    asum_ref, reg_ref, tanh_ref, gate_ref, w_ref, rows_ref, cols_ref, scal_ref,
):
    d_summary = nn(gl_ref[...], wc_ref[...], HIGHEST)
    slot = lax.broadcasted_iota(jnp.int32, (SLIDES, 1), 0)
    row = lax.broadcasted_iota(jnp.int32, (8, 1), 0)
    d_own = jnp.zeros((8, D2), F32)
    count = jnp.ones((8, 1), F32)
    for i in range(OWN):
        mine = slot == slide_ref[idx_ref[0] + i]
        d_own = jnp.where(
            row == i, jnp.sum(jnp.where(mine, d_summary, 0.0), axis=0, keepdims=True), d_own
        )
        t_i = tissue_row(idx_ref, tis_ref, i)
        count = jnp.where(row == i, jnp.maximum(jnp.sum(t_i, axis=1, keepdims=True), 1.0), count)
    region = reg_ref[:, pl.ds(0, D2)]
    tanh_part = tanh_ref[...]
    gate_part = gate_ref[...]
    pre_v = aw_ref[...] * gate_part * (1.0 - tanh_part * tanh_part)
    pre_u = aw_ref[...] * tanh_part * gate_part * (1.0 - gate_part)
    second = nt(pre_v, ap_ref[0], HIGHEST) + nt(pre_u, ap_ref[1], HIGHEST)
    own = jnp.sum(d_own * region, axis=1, keepdims=True)
    dm = (d_own / count, second / count)
    kept = (
        pre_v, pre_u, dm[0], dm[1],
        jnp.broadcast_to(w_ref[:, 0:1], (8, D2)), jnp.broadcast_to(own, (8, D2)),
        nt(dm[0].astype(BF), wp_ref[3]), nt(dm[1].astype(BF), wp_ref[3]),
    )
    for i, value in enumerate(kept):
        rows_ref[pl.ds(8 * i, 8), :] = value
    turned = jnp.concatenate(
        [region, asum_ref[...], tanh_part * gate_part, jnp.zeros((104, D2), F32)], axis=0
    )
    cols_ref[...] = turned.T
    lane = lax.broadcasted_iota(jnp.int32, (1, PATCH), 1) // 64
    scalars = jnp.zeros((1, PATCH), F32)
    for i in range(OWN):
        scalars = jnp.where(lane == 2 * i, w_ref[i : i + 1, 0:1], scalars)
        scalars = jnp.where(lane == 2 * i + 1, own[i : i + 1], scalars)
    scal_ref[...] = jnp.broadcast_to(scalars, (8, PATCH))


def pull_back(idx_ref, tis_ref, wp_ref, p_ref, x_ref, rows_ref, df_ref, grad_ref, kt_s, dqt_s):
    regions = range(OWN)
    pairs = [(r, j) for r in regions for j in range(2)]
    trow = [tissue_row(idx_ref, tis_ref, r) for r in regions]
    tcol = [column_of(row, D2) for row in trow]
    x = [x_ref[r] for r in regions]
    q = [nn(x[r], wp_ref[0]).astype(BF).astype(F32) for r in regions]
    v = [nn(x[r], wp_ref[2]).astype(BF) for r in regions]
    for r in regions:
        kt_s[r] = lax.dot_general(
            wp_ref[1], x[r], (((0,), (1,)), ((), ())), preferred_element_type=F32
        ).astype(BF)
    dm = {(r, j): rows_ref[pl.ds(8 * (2 + j) + r, 1), :] for r, j in pairs}
    da = {
        (r, j): rows_ref[pl.ds(8 * (6 + j) + r, 1), :].astype(BF).astype(F32) for r, j in pairs
    }
    row = lax.broadcasted_iota(jnp.int32, (16, D2), 0)
    head = lax.broadcasted_iota(jnp.int32, (16, D2), 1) // HEAD_DIM
    e = []
    for r in regions:
        by_head = jnp.where(row // 2 == head, jnp.where(row % 2 == 0, da[r, 0], da[r, 1]), 0.0)
        e.append(nt(by_head.astype(BF), v[r]).T)
    spread = [jnp.zeros((PATCH, D2), F32) for _ in regions]
    dk = {pair: jnp.zeros((PATCH, D2), F32) for pair in pairs}
    for h in range(HEADS):
        mask = head_mask(h, (1, D2), 1)
        rows = pl.ds(h * HEAD_DIM, HEAD_DIM)
        for r in regions:
            pb = p_ref[r, pl.ds(h * PATCH, PATCH), :]
            pt = pb.astype(F32)
            spread[r] = spread[r] + nn(pb, (tcol[r] * mask).astype(BF))
            q_head = (q[r] * mask).astype(BF)
            k_head = kt_s[r, rows, :]
            for j in range(2):
                pe = pt * e[r][:, 2 * h + j : 2 * h + j + 1]
                ds = (pe - pt * jnp.sum(pe, axis=0, keepdims=True)).astype(BF)
                dk[r, j] = dk[r, j] + nn(ds, q_head)
                dqt_s[r, j, rows, :] = nn(k_head, ds)
    xt = [x[r].T for r in regions]
    flat = {}
    for r, j in pairs:
        dq = (dqt_s[r, j] * (trow[r] * SCALE)).astype(BF).T
        dk_j = (dk[r, j] * SCALE).astype(BF)
        dv = (spread[r] * da[r, j]).astype(BF)
        grad_ref[r, 0, j] = nn(xt[r], dq)
        grad_ref[r, 1, j] = nn(xt[r], dk_j)
        grad_ref[r, 2, j] = nn(xt[r], dv)
        d_flat = dm[r, j] + nt(dq, wp_ref[0]) + nt(dk_j, wp_ref[1]) + nt(dv, wp_ref[2])
        flat[r, j] = tcol[r] * d_flat
    for r in regions:
        both = jnp.concatenate([flat[r, 0], flat[r, 1]], axis=1).astype(BF)
        df_ref[:, r] = both.reshape(GRP, PATCH // GRP, 2 * D2)


WIDE = 2 * D2 + 128


def region_backward_kernel(
    idx_ref, slide_ref, tis_ref, wp_ref, ap_ref, aw_ref, wc_ref, gl_ref,
    p_ref, x_ref, asum_ref, reg_ref, tanh_ref, gate_ref, w_ref,
    df_ref, grad_ref, rows_ref, cols_ref, scal_ref,
    kt_s, dqt_s,
):
    directions(
        idx_ref, slide_ref, tis_ref, wp_ref, ap_ref, aw_ref, wc_ref, gl_ref,
        asum_ref, reg_ref, tanh_ref, gate_ref, w_ref, rows_ref, cols_ref, scal_ref,
    )
    pull_back(idx_ref, tis_ref, wp_ref, p_ref, x_ref, rows_ref, df_ref, grad_ref, kt_s, dqt_s)


def region_backward(idx, slide, tissue, wp, ap, att_w, w_class, g_logits, kept):
    whole = lambda rows, width: pl.BlockSpec((rows, width), lambda r, *_: (0, 0))
    region = lambda rows, width: pl.BlockSpec((OWN, rows, width), lambda r, *_: (0, 0, 0))
    return pl.pallas_call(
        region_backward_kernel,
        grid_spec=pltpu.PrefetchScalarGridSpec(
            num_scalar_prefetch=2,
            grid=(1,),
            in_specs=[
                pl.BlockSpec((8, PATCH), lambda r, idx, _: (idx[2], 0)),
                *packed_specs(),
                whole(1, D2), whole(3, D2), whole(SLIDES, 3),
                region(HEADS * PATCH, PATCH),
                region(PATCH, D2),
                whole(8, D2), whole(8, PATCH), whole(8, D2), whole(8, D2), whole(8, 128),
            ],
            out_specs=[
                pl.BlockSpec((GRP, OWN, PATCH // GRP, 2 * D2), lambda r, *_: (0, 0, 0, 0)),
                pl.BlockSpec((OWN, 3, 2, D2, D2), lambda r, *_: (0, 0, 0, 0, 0)),
                whole(64, D2),
                whole(D2, 128),
                whole(8, PATCH),
            ],
            scratch_shapes=[
                pltpu.VMEM((OWN, D2, PATCH), BF),
                pltpu.VMEM((OWN, 2, D2, PATCH), F32),
            ],
        ),
        out_shape=[
            pltpu.HBM((GRP, OWN, PATCH // GRP, WIDE), BF),
            pltpu.HBM((OWN, 3, 2, D2, D2), F32),
            pltpu.HBM((64, D2), F32),
            pltpu.HBM((D2, 128), F32),
            jax.ShapeDtypeStruct((8, PATCH), F32),
        ],
        compiler_params=params(40),
        cost_estimate=pl.CostEstimate(
            flops=4_000_000_000, bytes_accessed=20_000_000, transcendentals=0
        ),
        name="region_backward",
    )(idx, slide, tissue, wp, ap, att_w, w_class, g_logits, *kept)


def split_three(x):
    parts = []
    for _ in range(3):
        top = x.astype(BF).astype(F32)
        parts.append(top)
        x = x - top
    return parts


def join_sums_kernel(z_ref, scal_ref, df_ref, out_ref, ext, wide, sem):
    z = jnp.sum(z_ref[...], axis=0)
    z = jnp.concatenate([z[0:SLIDES], z[SLIDES:]], axis=1)
    ext[...] = jnp.zeros_like(ext)
    for i, (part, tops) in enumerate(zip(split_three(z), split_three(scal_ref[0:1]))):
        ext[pl.ds(4 * i, 4), :] = part
        ext[pl.ds(12 + i, 1), :] = tops
    for i in range(OWN):
        block = ext[:, pl.ds(128 * i, 128)].astype(BF)
        wide[:, i] = jnp.broadcast_to(block[None], (GRP, 16, 128))
    copy = pltpu.make_async_copy(wide, out_ref.at[:, :, :, pl.ds(2 * D2, 128)], sem)
    copy.start()
    copy.wait()


def join_sums(z, scalars, df):
    return pl.pallas_call(
        join_sums_kernel,
        in_specs=[pl.BlockSpec(memory_space=pltpu.VMEM)] * 2
        + [pl.BlockSpec(memory_space=pl.ANY)],
        out_specs=pl.BlockSpec(memory_space=pl.ANY),
        out_shape=pltpu.HBM(df.shape, df.dtype),
        scratch_shapes=[
            pltpu.VMEM((16, PATCH), F32),
            pltpu.VMEM((GRP, OWN, 16, 128), BF),
            pltpu.SemaphoreType.DMA,
        ],
        input_output_aliases={2: 0},
        compiler_params=params(24),
        name="join_sums",
    )(z, scalars, df)


def put_rest(pack, slot, grad, fill=None):
    at = REST_AT + 192 * slot
    if not isinstance(slot, int):
        at = pl.multiple_of(at, 64)
    for half in range(2):
        rows = grad[96 * half : 96 * half + 96]
        pack[half, pl.ds(at, 96), :] = rows[:, :128].astype(BF)
        tail = jnp.zeros((96, 64), F32) if fill is None else fill
        high = jnp.concatenate([rows[:, 128:], tail], axis=1)
        pack[half, pl.ds(at + 96, 96), :] = high.astype(BF)


def finish_slides(
    idx_ref, slide_ref, back_ref, rows_ref, cols_ref, wc_ref, gl_ref, logits_ref, gc_ref,
    df_s, pq_s, pack,
):
    ext = [back_ref[:, i, :, pl.ds(2 * D2, 128)].astype(F32) for i in range(OWN)]
    ext = jnp.concatenate(ext, axis=2)
    sums = jnp.sum(ext, axis=0)
    sums = sums[0:4] + sums[4:8] + sums[8:12]
    total = sums[:, D2 : D2 + 1]
    summary = sums[:, :D2] / total
    wc = wc_ref[...]
    gl = gl_ref[...]
    logits_ref[...] = nt(summary, wc, HIGHEST)
    gc_ref[...] = tn(gl, summary, HIGHEST)
    along = jnp.sum(nn(gl, wc, HIGHEST) * summary, axis=1, keepdims=True)

    def of_slide(column, s):
        out = column[SLIDES - 1 : SLIDES]
        for i in range(SLIDES - 1):
            out = jnp.where(s == i, column[i : i + 1], out)
        return out

    def factors(w, a, s):
        share = w / of_slide(total, s)
        return share, share * (a - of_slide(along, s))

    for src in range(GRP):
        scalars = ext[src, 12:13] + ext[src, 13:14] + ext[src, 14:15]
        for i in range(OWN):
            w = scalars[:, 128 * i : 128 * i + 1]
            a = scalars[:, 128 * i + 64 : 128 * i + 65]
            p, q = factors(w, a, slide_ref[idx_ref[5] + OWN * src + i])
            f = back_ref[src, i].astype(F32)
            rows = p * f[:, :D2] + q * f[:, D2 : 2 * D2]
            df_s[pl.ds(32 * src + 16 * i, 16), :] = rows.astype(BF)

    kept = [rows_ref[pl.ds(8 * i, 8), :] for i in range(6)]
    pre_v, pre_u, dm0, dm1, w_own, a_own = kept
    row = lax.broadcasted_iota(jnp.int32, (8, 1), 0)
    p_own = jnp.zeros((8, 1), F32)
    q_own = jnp.zeros((8, 1), F32)
    for i in range(OWN):
        p, q = factors(w_own[i : i + 1, 0:1], a_own[i : i + 1, 0:1], slide_ref[idx_ref[0] + i])
        p_own = jnp.where(row == i, p, p_own)
        q_own = jnp.where(row == i, q, q_own)
    pq_s[0] = jnp.broadcast_to(p_own, (8, 128))
    pq_s[1] = jnp.broadcast_to(q_own, (8, 128))

    def outer(at, rows):
        out = cols_ref[:, at : at + 1] * rows[0:1]
        return out + cols_ref[:, at + 1 : at + 2] * rows[1:2]

    put_rest(pack, 3, outer(8, p_own * dm0 + q_own * dm1))
    put_rest(pack, 4, outer(0, q_own * pre_v))
    g_aw = outer(16, jnp.broadcast_to(q_own, (8, 64)))
    lane = lax.broadcasted_iota(jnp.int32, (96, 64), 1)
    put_rest(pack, 5, outer(0, q_own * pre_u), jnp.where(lane == 0, g_aw[:96], g_aw[96:]))


def patch_backward_kernel(
    idx_ref, slide_ref, back_in, xt_in, mid_in, hid_in, gp_in, we_in, wd_in, grad_in,
    rows_ref, cols_ref, wc_ref, gl_ref,
    mine_ref, other_ref, logits_ref, gc_ref,
    back_ref, xt_ref, mid_ref, hid_ref, gp_ref, we_ref, wd_ref, grad_ref,
    pack, df_s, pq_s, in_sems, sems,
):
    core = idx_ref[3]
    pairs = (
        (back_in, back_ref), (we_in, we_ref), (wd_in, wd_ref), (gp_in, gp_ref), (xt_in, xt_ref),
        (hid_in, hid_ref), (mid_in, mid_ref), (grad_in, grad_ref),
    )
    fetch = [pltpu.make_async_copy(a, b, in_sems.at[i]) for i, (a, b) in enumerate(pairs)]
    begin(fetch)
    sent = []

    def send(low, size):
        rows = pl.ds(low, size)
        at = len(sent)
        sent.extend(
            begin(
                [
                    pltpu.make_async_copy(
                        pack.at[core, rows], mine_ref.at[rows], sems.at[at]
                    ),
                    pltpu.make_async_copy(
                        pack.at[1 - core, rows], other_ref.at[rows], sems.at[at + 1]
                    ),
                ]
            )
        )

    fetch[0].wait()
    finish_slides(
        idx_ref, slide_ref, back_ref, rows_ref, cols_ref, wc_ref, gl_ref, logits_ref, gc_ref,
        df_s, pq_s, pack,
    )
    df = df_s[...]
    fetch[1].wait()
    dmid = nn(df, we_ref[...]).astype(BF)
    for i in range(2, 5):
        fetch[i].wait()
    d_pre = (nt(dmid, wd_ref[...]) * gp_ref[...].astype(F32)).astype(BF)
    g_up = nn(xt_ref[...], d_pre).astype(BF)
    for l in range(F1 // 128):
        for half in range(2):
            block = g_up[192 * half : 192 * half + 192, 128 * l : 128 * l + 128]
            pack[half, pl.ds(192 * l, 192), :] = block
    send(0, DOWN_AT)
    fetch[5].wait()
    g_down = nn(hid_ref[...], dmid).astype(BF)
    for half in range(2):
        for l in range(3):
            block = g_down[768 * half : 768 * half + 768, 128 * l : 128 * l + 128]
            pack[half, pl.ds(DOWN_AT + 768 * l, 768), :] = block
    send(DOWN_AT, REST_AT - DOWN_AT)
    fetch[6].wait()
    g_embed = tn(df, mid_ref[...]).astype(BF)
    for half in range(2):
        for l in range(3):
            block = g_embed[96 * half : 96 * half + 96, 128 * l : 128 * l + 128]
            pack[half, pl.ds(EMBED_AT + 96 * l, 96), :] = block
        pack[half, pl.ds(PAD_AT, 96), :] = jnp.zeros((96, 128), BF)
    fetch[7].wait()
    for slot in range(3):
        grad = jnp.zeros((D2, D2), F32)
        for i in range(OWN):
            for j in range(2):
                grad = grad + pq_s[j, i : i + 1, 0:1] * grad_ref[i, slot, j]
        put_rest(pack, slot, grad)
    send(REST_AT, HALF_ROWS - REST_AT)
    for copy in sent:
        copy.wait()


def patch_backward(
    idx, slide, back, turned, mid, hid, gp, w_embed, w_down, grads, rows, cols, w_class, g_logits
):
    hbm = pl.BlockSpec(memory_space=pl.ANY)
    vmem = pl.BlockSpec(memory_space=pltpu.VMEM)
    smem = pl.BlockSpec(memory_space=pltpu.SMEM)
    big = (back, turned, mid, hid, gp, w_embed, w_down, grads)
    return pl.pallas_call(
        patch_backward_kernel,
        in_specs=[smem] * 2 + [hbm] * 8 + [vmem] * 4,
        out_specs=[hbm] * 2 + [vmem] * 2,
        out_shape=[
            jax.ShapeDtypeStruct((HALF_ROWS, 128), BF),
            jax.ShapeDtypeStruct((HALF_ROWS, 128), BF),
            jax.ShapeDtypeStruct((SLIDES, 3), F32),
            jax.ShapeDtypeStruct((3, D2), F32),
        ],
        scratch_shapes=[pltpu.VMEM(a.shape, a.dtype) for a in big]
        + [
            pltpu.VMEM((2, HALF_ROWS, 128), BF),
            pltpu.VMEM((turned.shape[1], D2), BF),
            pltpu.VMEM((2, 8, 128), F32),
            pltpu.SemaphoreType.DMA((8,)),
            pltpu.SemaphoreType.DMA((6,)),
        ],
        compiler_params=params(61),
        name="patch_backward",
    )(idx, slide, *big, rows, cols, w_class, g_logits)


def bring_in_kernel(src_ref, out_ref, sem):
    copy = pltpu.make_async_copy(src_ref, out_ref, sem)
    copy.start()
    copy.wait()


def bring_in(x):
    return pl.pallas_call(
        bring_in_kernel,
        in_specs=[pl.BlockSpec(memory_space=pl.ANY)],
        out_specs=pl.BlockSpec(memory_space=pltpu.VMEM),
        out_shape=jax.ShapeDtypeStruct(x.shape, x.dtype),
        scratch_shapes=[pltpu.SemaphoreType.DMA],
        compiler_params=params(16),
        cost_estimate=pl.CostEstimate(flops=0, bytes_accessed=6_000_000, transcendentals=0),
        name="bring_in",
    )(x)


def unpack_kernel(idx_ref, src_ref, *refs):
    up_ref, down_ref, embed_ref, q_ref, k_ref, v_ref, o_ref, av_ref, au_ref, aw_ref = refs[-10:]
    for l in range(12):
        up_ref[:, pl.ds(128 * l, 128)] = src_ref[pl.ds(192 * l, 192), :].astype(F32)
    for l in range(3):
        rows = src_ref[pl.ds(DOWN_AT + 768 * l, 768), :]
        down_ref[:, pl.ds(128 * l, 128)] = rows.astype(F32)
    for slot, ref in enumerate((q_ref, k_ref, v_ref, o_ref, av_ref, au_ref)):
        at = REST_AT + 192 * slot
        ref[:, pl.ds(0, 128)] = src_ref[pl.ds(at, 96), :].astype(F32)
        ref[:, pl.ds(128, 64)] = src_ref[pl.ds(at + 96, 96), :][:, :64].astype(F32)
    for l in range(3):
        embed_ref[:, pl.ds(128 * l, 128)] = src_ref[pl.ds(EMBED_AT + 96 * l, 96), :].astype(F32)
    tail = src_ref[pl.ds(EMBED_AT - 96, 96), :].astype(F32).T
    aw_ref[:, pl.ds(0, 96)] = tail[64:65, :]
    aw_ref[:, pl.ds(96, 96)] = tail[65:66, :]


def unpack(idx, src, which, earlier=()):
    square = jax.ShapeDtypeStruct((D2, D2), F32)
    half = lambda rows, width: pl.BlockSpec((rows, width), lambda i, idx: (idx[which], 0))
    hbm = pl.BlockSpec(memory_space=pltpu.HBM)
    return pl.pallas_call(
        unpack_kernel,
        grid_spec=pltpu.PrefetchScalarGridSpec(
            num_scalar_prefetch=1,
            grid=(1,),
            in_specs=[pl.BlockSpec((HALF_ROWS, 128), lambda i, idx: (0, 0))] + [hbm] * len(earlier),
            out_specs=[
                half(D1 // 2, F1),
                half(F1 // 2, D1),
                half(D2 // 2, D1),
            ]
            + [half(D2 // 2, D2)] * 6
            + [pl.BlockSpec((1, D2), lambda i, idx: (0, 0))],
        ),
        out_shape=[
            jax.ShapeDtypeStruct((D1, F1), F32),
            jax.ShapeDtypeStruct((F1, D1), F32),
            jax.ShapeDtypeStruct((D2, D1), F32),
            square, square, square, square, square, square,
            jax.ShapeDtypeStruct((1, D2), F32),
        ],
        input_output_aliases={2 + i: i for i in range(len(earlier))},
        compiler_params=params(),
        name="unpack",
    )(idx, src, *earlier)


GRP_AXES = ("zl", "x", "c")
DEV_AXES = ("zh", "y")
ZLXY = ("y", "zl", "x")


def exchange(x, axes):
    return lax.all_to_all(x, axes, split_axis=0, concat_axis=0, tiled=True)


def swap_cores(x):
    return lax.ppermute(x, "c", [(0, 1), (1, 0)])


def spread(x, n):
    return jnp.broadcast_to(x[None], (n,) + x.shape)


def add_pair(x, y):
    return (x.astype(F32) + y.astype(F32)).astype(x.dtype)


def add_over_zh(x):
    got = [lax.ppermute(x, "zh", [(i, i ^ k) for i in range(4)]) for k in (1, 2, 3)]
    a, b, c, d = [y.astype(F32) for y in (x, *got)]
    return ((a + b) + (c + d)).astype(x.dtype)


def add_up(x):
    return jnp.sum(x.astype(F32), axis=0).astype(x.dtype)


def body(
    patches, tissue, region_slide, w_up, w_down, w_embed, w_query, w_key, w_value, w_out,
    att_v, att_u, att_w, w_class, g_logits,
):
    grp = lax.axis_index(GRP_AXES)
    dev = lax.axis_index(DEV_AXES)
    core = lax.axis_index("c")
    first = (dev * GRP + grp) * OWN
    idx = jnp.stack([first, first % 8, first // 8, core, 1 - core, dev * GRP * OWN]).astype(jnp.int32)
    tokens = patches.reshape(-1, D1)
    att_row = att_w.reshape(1, D2)
    class_rows = w_class.T
    feat, mid = patch_forward(tokens, w_up, w_down, w_embed.T)
    wp, ap = gather_weights((w_query, w_key, w_value, w_out, att_v, att_u))
    got = exchange(feat.reshape(GRP, -1, D2), GRP_AXES)
    got = got.reshape(GRP, OWN, PATCH // GRP, D2)
    *kept, part = region_forward(idx, region_slide, got, tissue, wp, ap, att_row)
    z = exchange(part, DEV_AXES)
    df, grads, rows, cols, scalars = region_backward(
        idx, region_slide, tissue, wp, ap, att_row, class_rows, g_logits, kept
    )
    df = join_sums(z, scalars, df)
    hid, gp, turned = patch_slopes(rows, tokens, w_up)
    back = exchange(df.reshape(GRP, -1, WIDE), GRP_AXES).reshape(df.shape)
    mine, other, logits, g_class = patch_backward(
        idx, region_slide, back, turned, mid, hid, gp, w_embed.T, w_down, grads, rows,
        cols, class_rows, g_logits,
    )
    half = add_pair(bring_in(mine), swap_cores(other))
    chunk = add_up(exchange(half.reshape(PEERS, -1, 128), ZLXY))
    chunk = add_over_zh(chunk)
    half = exchange(spread(chunk, PEERS), ZLXY).reshape(HALF_ROWS, 128)
    other = swap_cores(half)
    grads = unpack(idx, other, 4, unpack(idx, half, 3))
    up, down, embed, query, key, value, out, gv, gu, gw = grads
    return (
        logits, up, down, embed.T, query, key, value, out, gv, gu, gw.reshape(D2), g_class.T,
    )


def solution(mesh):
    fine = Mesh(mesh.devices.reshape(2, 4, 2, 4, 4), GRP_AXES + DEV_AXES)
    placed = (P(DEV_AXES, GRP_AXES, None),) + (P(),) * 14
    return jax.shard_map(
        body,
        mesh=fine,
        in_specs=placed,
        out_specs=(P(),) * 12,
        check_vma=False,
    )
```
